512 devices in a mesh: wide: 64 (over y, z_lo, core), narrow: 8 (over z_hi, x).
Axes of the slice: x: 4, y: 4, z: 16 (z_hi: 2, z_lo: 8; z = z_hi * 8 + z_lo), core: 2. Of those that a mesh axis runs over, the one named last changes fastest.
Arguments:
- velocity: float32 [3, 8, 1024, 1024], P(None, 'narrow', 'wide'), may hold values from -6 to 6
- buoyancy: float32 [8, 1024, 1024], P('narrow', 'wide'), may hold values from -6 to 6
- cell_mask: int32 [8, 1024, 1024], P('narrow', 'wide'), may hold values 0 or 1
- spacing: float32 [8], replicated, may hold values from 0.5 to 2
- cotangent: float32 [3, 8, 1024, 1024], P(None, 'narrow', 'wide'), may hold values from -6 to 6
- w_in: float32 [32, 4], replicated, may hold values from -3 to 3
- b_in: float32 [32], replicated, may hold values from -3 to 3
- w_mid: float32 [32, 32], replicated, may hold values from -1 to 1
- b_mid: float32 [32], replicated, may hold values from -3 to 3
- w_out: float32 [3, 32], replicated, may hold values from -1 to 1
Outputs:
- grad_velocity: float32 [3, 8, 1024, 1024], P(None, 'narrow', 'wide')
- grad_buoyancy: float32 [8, 1024, 1024], P('narrow', 'wide')
- grad_w_in: float32 [32, 4], replicated
- grad_b_in: float32 [32], replicated
- grad_w_mid: float32 [32, 32], replicated
- grad_b_mid: float32 [32], replicated
- grad_w_out: float32 [3, 32], replicated
The draws below stay inside these ranges and needn't reach their ends.
All inputs are finite; a program needn't handle non-finite values. No bound on the sum of `cell_mask` on one device may be relied on, other than what follows from the above.
Results may differ from the reference program's by a relative error of at most 0.0003.
Values sent between devices are 32-bit elements; how exact they have to be, the bound alone decides.
No kernel may reach another device: no remote copies, remote signals or barrier semaphores. Data moves between devices by JAX's collectives and lax.ppermute only.
A program may use at most 64 MiB of HBM per device.

```python
import math
import jax
import jax.numpy as jnp
from jax import lax

NX = 1024
NY = 1024
NZ = 8
WIDTH = 32


def touch_ends(drawn, own_key, least, top_value):
    shape = drawn.shape
    place = [jax.random.randint(jax.random.fold_in(own_key, axis), (), 0, shape[axis]) for axis in range(len(shape))]
    drawn = drawn.at[tuple(place)].set(least)
    longest = shape.index(max(shape))
    place[longest] = (place[longest] + 1) % shape[longest]
    return drawn.at[tuple(place)].set(top_value)


def steps_of(stream_key, extent, split, least, largest):
    factor_of = 1.0
    for position, blocks in split:
        heights = jax.random.uniform(jax.random.fold_in(jax.random.fold_in(stream_key, 6), position), (blocks,), jnp.float32, least / len(split), largest / len(split))
        factor_of = factor_of * jnp.repeat(jnp.exp(heights), extent[position] // blocks).reshape((-1,) + (1,) * (len(extent) - 1 - position))
    return factor_of


def scatter_about(rng, dims, width, reach, split=(), held_as=jnp.bfloat16):
    values = width * jax.random.normal(rng, dims, jnp.float32)
    if split:
        values = values * steps_of(rng, dims, split, -0.22, 0.18)
    return jnp.clip(values, -reach, reach).astype(held_as)


def setup_inputs(seed: int = 0) -> dict:
    key_of = jax.random.split(jax.random.key(seed), 11)
    velocity = scatter_about(key_of[0], (3, NZ, NY, NX), 1.0, 6.0, ((1, 8), (2, 64)), jnp.float32)
    buoyancy = scatter_about(key_of[1], (NZ, NY, NX), 1.0, 6.0, ((0, 8), (1, 64)), jnp.float32)
    cell_mask = touch_ends((jax.random.randint(key_of[2], (NZ, NY, NX), 0, 8) < 7).astype(jnp.int32), jax.random.fold_in(key_of[2], 1), 0, 1)
    spacing = jnp.clip(jnp.exp(jax.random.uniform(key_of[3], (NZ,), jnp.float32, math.log(0.5), math.log(2.0))), 0.5, 2.0)
    cotangent = scatter_about(key_of[4], (3, NZ, NY, NX), 1.0, 6.0, ((1, 8), (2, 64)), jnp.float32)
    w_in = scatter_about(key_of[5], (WIDTH, 4), 4 ** -0.5, 3.0, (), jnp.float32)
    b_in = scatter_about(key_of[6], (WIDTH,), 0.5, 3.0, (), jnp.float32)
    w_mid = scatter_about(key_of[7], (WIDTH, WIDTH), WIDTH ** -0.5, 1.0, (), jnp.float32)
    b_mid = scatter_about(key_of[8], (WIDTH,), 0.5, 3.0, (), jnp.float32)
    w_out = scatter_about(key_of[9], (3, WIDTH), WIDTH ** -0.5, 1.0, (), jnp.float32)
    return dict(velocity=velocity, buoyancy=buoyancy, cell_mask=cell_mask, spacing=spacing, cotangent=cotangent, w_in=w_in, b_in=b_in, w_mid=w_mid, b_mid=b_mid, w_out=w_out)


free_surface = 0.05
highest = lax.Precision.HIGHEST

def dft_table(length):
    indices = jnp.arange(length, dtype=jnp.int32)
    frequency = jnp.minimum(indices, length - indices)
    product = frequency[:, None] * indices[None, :] % length
    angle = 2.0 * math.pi / length * product.astype(jnp.float32)
    weights = jnp.where((frequency == 0) | (2 * frequency == length), 1.0, 2.0).astype(jnp.float32) / length
    rows_cos = (indices <= length // 2)[:, None]
    return jnp.where(rows_cos, jnp.cos(angle), jnp.sin(angle)) * jnp.sqrt(weights)[:, None]

def eigenvalue(indices, length):
    frequency = jnp.minimum(indices, length - indices).astype(jnp.float32)
    return -4.0 * jnp.sin(math.pi / length * frequency) ** 2

def vertical(spacing):
    count = spacing.shape[0]
    inv_dz = 1.0 / spacing
    nothing = jnp.zeros((1,), jnp.float32)
    inv_face = jnp.concatenate([2.0 / (spacing[:-1] + spacing[1:]), nothing])
    lower = jnp.concatenate([nothing, inv_dz[1:] * inv_face[:-1]])
    upper = inv_dz * inv_face
    top_flag = (jnp.arange(count, dtype=jnp.int32) == count - 1).astype(jnp.float32)
    base = -(lower + upper) - free_surface * inv_dz * top_flag
    sub_diag = jnp.concatenate([nothing, upper[:-1]])
    super_diag = jnp.concatenate([lower[1:], nothing])
    return (inv_dz, inv_face, sub_diag, base, super_diag, 1.0 - top_flag)

def tridiagonal(right, sub_diag, base, super_diag, offset):
    count = right.shape[0]
    ratios = []
    values = []
    for level in range(count):
        diagonal = base[level] + offset
        if level > 0:
            diagonal = diagonal - sub_diag[level] * ratios[-1]
            value = (right[level] - sub_diag[level] * values[-1]) / diagonal
        else:
            value = right[level] / diagonal
        ratios.append(super_diag[level] / diagonal)
        values.append(value)
    result = [values[-1]]
    for level in range(count - 2, -1, -1):
        result.append(values[level] - ratios[level] * result[-1])
    return jnp.stack(result[::-1])

def closure_pass(weights, features, projected, wet):
    w_in, b_in, w_mid, b_mid, w_out = weights
    channels, levels, rows, columns = features.shape
    feats = jnp.moveaxis(features, 1, 0).reshape(levels, channels, rows * columns)
    grads = jnp.moveaxis(projected, 1, 0).reshape(levels, 3, rows * columns)
    masks = wet.reshape(levels, rows * columns).astype(jnp.float32)

    def level_step(totals, inputs):
        feat_level, grad_level, mask_level = inputs
        first = jnp.tanh(jnp.einsum('hc,cn->hn', w_in, feat_level, precision=highest) + b_in[:, None])
        second = jnp.tanh(jnp.einsum('hg,gn->hn', w_mid, first, precision=highest) + b_mid[:, None])
        delta = grad_level * mask_level[None, :]
        err_second = jnp.einsum('oh,on->hn', w_out, delta, precision=highest) * (1.0 - second * second)
        err_first = jnp.einsum('hg,hn->gn', w_mid, err_second, precision=highest) * (1.0 - first * first)
        outgoing = jnp.einsum('hc,hn->cn', w_in, err_first, precision=highest)
        totals = (totals[0] + jnp.einsum('hn,cn->hc', err_first, feat_level, precision=highest), totals[1] + lax.optimization_barrier(jnp.sum(err_first, axis=1)), totals[2] + jnp.einsum('hn,gn->hg', err_second, first, precision=highest), totals[3] + lax.optimization_barrier(jnp.sum(err_second, axis=1)), totals[4] + jnp.einsum('on,hn->oh', delta, second, precision=highest))
        return (totals, outgoing)
    initial = tuple((jnp.zeros_like(weight_item) for weight_item in weights))
    totals, outgoing = lax.scan(level_step, initial, (feats, grads, masks))
    closure_grad = jnp.moveaxis(outgoing.reshape(levels, channels, rows, columns), 0, 1)
    return (closure_grad, totals)

def reference(velocity, buoyancy, cell_mask, spacing, cotangent, w_in, b_in, w_mid, b_mid, w_out):
    inv_dz, inv_face, sub_diag, base, super_diag, keep = vertical(spacing)
    flow_east, flow_north, flow_up = (cotangent[0], cotangent[1], cotangent[2])
    up_face = flow_up * inv_face[:, None, None]
    source = flow_east - jnp.roll(flow_east, -1, axis=2) + flow_north - jnp.roll(flow_north, -1, axis=1)
    source = source + jnp.concatenate([jnp.zeros_like(up_face[:1]), up_face[:-1]], axis=0) - up_face
    table_x = dft_table(NX)
    table_y = dft_table(NY)
    spectral = jnp.einsum('zyx,kx->zyk', source, table_x, precision=highest)
    spectral = jnp.einsum('zyk,qy->zqk', spectral, table_y, precision=highest)
    offset = eigenvalue(jnp.arange(NY, dtype=jnp.int32), NY)[:, None] + eigenvalue(jnp.arange(NX, dtype=jnp.int32), NX)[None, :]
    solution = tridiagonal(spectral, sub_diag, base, super_diag, offset)
    pressure = jnp.einsum('zqk,qy->zyk', solution, table_y, precision=highest)
    pressure = jnp.einsum('zyk,kx->zyx', pressure, table_x, precision=highest)
    east_back = jnp.roll(pressure, 1, axis=2) - pressure
    north_back = jnp.roll(pressure, 1, axis=1) - pressure
    scaled = pressure * inv_dz[:, None, None]
    up_back = (scaled - jnp.concatenate([scaled[1:], jnp.zeros_like(scaled[:1])], axis=0)) * keep[:, None, None]
    projected = jnp.stack([flow_east - east_back, flow_north - north_back, flow_up - up_back])
    features = jnp.concatenate([velocity, buoyancy[None]], axis=0)
    closure_grad, totals = closure_pass((w_in, b_in, w_mid, b_mid, w_out), features, projected, cell_mask)
    scale = 1.0 / math.sqrt(NX * NY * NZ)
    return (projected + closure_grad[:3], closure_grad[3], totals[0] * scale, totals[1] * scale, totals[2] * scale, totals[3] * scale, totals[4] * scale)
```

```python
import functools
import math

import jax
import jax.numpy as jnp
import ml_dtypes
import numpy as np
from jax import lax
from jax.experimental import pallas as pl
from jax.experimental.pallas import tpu as pltpu
from jax.sharding import Mesh
from jax.sharding import PartitionSpec as P

free_surface = 0.05
f32 = jnp.float32
bf16 = jnp.bfloat16
LANES = 128
LEVELS = 8
VMEM_LIMIT = 24 * 1024 * 1024

FINE = (("y", 4), ("zl", 8), ("c", 2), ("zh", 2), ("x", 4))
WIDE = ("y", "zl", "c")
NARROW = ("zh", "x")
PLANE = ("zh", "y", "zl", "c")
SLAB = ("y", "x", "c")
COLUMN = ("zl", "zh")


def dft_table(length):
    indices = np.arange(length)
    frequency = np.minimum(indices, length - indices)
    angle = 2.0 * np.pi / length * (frequency[:, None] * indices[None, :] % length)
    weights = np.where((frequency == 0) | (2 * frequency == length), 1.0, 2.0) / length
    rows_cos = (indices <= length // 2)[:, None]
    return np.where(rows_cos, np.cos(angle), np.sin(angle)) * np.sqrt(weights)[:, None]


def two_parts(table):
    high = table.astype(np.float32).astype(ml_dtypes.bfloat16)
    low = (table - high.astype(np.float64)).astype(np.float32).astype(ml_dtypes.bfloat16)
    return high, low


def eigenvalue(length):
    indices = np.arange(length)
    frequency = np.minimum(indices, length - indices)
    return -4.0 * np.sin(np.pi / length * frequency) ** 2


def split(value):
    high = value.astype(bf16)
    low = (value - high.astype(f32)).astype(bf16)
    return high, low


def split_f32(value):
    high = value.astype(bf16).astype(f32)
    return high, value - high


def dot(a, b):
    return jnp.dot(a, b, preferred_element_type=f32)


def dot_nt(a, b):
    return lax.dot_general(a, b, (((1,), (1,)), ((), ())), preferred_element_type=f32)


def roll(value, shift, axis):
    size = value.shape[axis]
    shift = shift % size
    return value if shift == 0 else pltpu.roll(value, shift, axis)


def lane_of(shape):
    return lax.broadcasted_iota(jnp.int32, shape, len(shape) - 1)


def start_copy(source, target, sems, index):
    copy = pltpu.make_async_copy(source, target, sems.at[index])
    copy.start()
    return copy


def call(kernel, out_shape, args, smem=(), hbm=(), hbm_out=(), scratch=(), flops=0, name=None):
    def space(index, held):
        return pl.BlockSpec(memory_space=held.get(index, pltpu.VMEM))

    held = {i: pltpu.SMEM for i in smem} | {i: pl.ANY for i in hbm}
    args = [
        pltpu.with_memory_space_constraint(a, pltpu.HBM) if i in hbm else a
        for i, a in enumerate(args)
    ]
    moved = sum(int(np.prod(a.shape)) * a.dtype.itemsize for a in args)
    return pl.pallas_call(
        kernel,
        out_shape=out_shape,
        in_specs=[space(i, held) for i in range(len(args))],
        out_specs=[space(i, {o: pl.ANY for o in hbm_out}) for i in range(len(out_shape))],
        scratch_shapes=list(scratch),
        compiler_params=pltpu.CompilerParams(vmem_limit_bytes=VMEM_LIMIT),
        cost_estimate=pl.CostEstimate(flops=flops, bytes_accessed=moved, transcendentals=0),
        name=name,
    )(*args)


def forward_x(cot_hbm, high_hbm, low_hbm, out_ref, mark_ref, high_ref, low_ref, cot_ref, sems):
    first = start_copy(cot_hbm, cot_ref, sems, 16)
    blocks = [slice(LANES * t, LANES * (t + 1)) for t in range(8)]
    copies = []
    for t, block in enumerate(blocks):
        copies.append(
            (
                start_copy(high_hbm.at[block, :], high_ref.at[block, :], sems, 2 * t),
                start_copy(low_hbm.at[block, :], low_ref.at[block, :], sems, 2 * t + 1),
            )
        )
    first.wait()
    east, north, up = cot_ref[0, 0], cot_ref[1, 0], cot_ref[2, 0]
    rows, width = east.shape
    east = east - roll(east, -1, 1)
    high, low = split_f32(jnp.concatenate([east, north, up], axis=0))
    none = jnp.zeros((rows, width), f32)
    both = jnp.concatenate([high, none, low, none], axis=0).T.astype(bf16)
    lane = lane_of((LANES, LANES))
    packed = [jnp.zeros((LANES, LANES), f32)] * 3
    for t, block in enumerate(blocks):
        for copy in copies[t]:
            copy.wait()
        got = dot(high_ref[block, :], both) + dot(low_ref[block, :], both)
        got = got + roll(got, 64, 1)
        for field in range(3):
            packed[field] = jnp.where(
                lane // 16 == t, roll(got, 16 * (t - field), 1), packed[field]
            )
    for field in range(3):
        out_ref[:, 0, LANES * field : LANES * (field + 1)] = packed[field]
    mark_ref[...] = jnp.zeros(mark_ref.shape, f32)


def forward_y(msg_ref, high_hbm, low_hbm, mark_ref, out_ref, line_ref, high_ref, low_ref, sems):
    blocks = [slice(256 * g, 256 * (g + 1)) for g in range(4)]
    copies = [
        (
            start_copy(high_hbm.at[block, :], high_ref.at[block, :], sems, 2 * g),
            start_copy(low_hbm.at[block, :], low_ref.at[block, :], sems, 2 * g + 1),
        )
        for g, block in enumerate(blocks)
    ]
    lane = lane_of((64, LANES))
    within = lane % 16
    highs = []
    lows = []
    for half in range(2):
        part = slice(64 * half, 64 * (half + 1))
        east = msg_ref[part, 0, 0:LANES]
        north = msg_ref[part, 0, LANES : 2 * LANES]
        up = msg_ref[part, 0, 2 * LANES : 3 * LANES]
        after = jnp.where(
            within < 15, roll(north, -1, 1), roll(roll(north, -1, 0), 15, 1)
        )
        for value in (east + north - after, up):
            high, low = split_f32(value)
            highs.append(high)
            lows.append(low)
    shifted = [roll(value, c, 1) for c, value in enumerate(highs + lows)]
    for j in range(16):
        line = jnp.zeros((64, LANES), f32)
        for c, value in enumerate(shifted):
            line = jnp.where(within == (c + j) % 16, value, line)
        line_ref[pl.ds(j, 64, stride=16), :] = roll(line, -j, 1)
    lines = line_ref[...].astype(bf16)
    lane = lane_of((256, LANES))
    packed = jnp.zeros((256, LANES), f32)
    for g, block in enumerate(blocks):
        for copy in copies[g]:
            copy.wait()
        got = dot(high_ref[block, :], lines) + dot(low_ref[block, :], lines)
        got = got + roll(got, -4, 1)
        packed = jnp.where(lane % 16 // 4 == g, roll(got, 4 * g, 1), packed)
    for peer in range(4):
        out_ref[peer] = packed


def vertical(spacing):
    one = jnp.ones((1, LANES), f32)
    none = jnp.zeros((1, LANES), f32)
    spacing = [one * spacing[k] for k in range(LEVELS)]
    inv_dz = [1.0 / value for value in spacing]
    face = [2.0 / (spacing[k] + spacing[k + 1]) for k in range(LEVELS - 1)] + [none]
    lower = [none] + [inv_dz[k] * face[k - 1] for k in range(1, LEVELS)]
    upper = [inv_dz[k] * face[k] for k in range(LEVELS)]
    base = [-(lower[k] + upper[k]) for k in range(LEVELS)]
    base[-1] = base[-1] - free_surface * inv_dz[-1]
    sub = [none] + upper[:-1]
    sup = lower[1:] + [none]
    keep = [one] * (LEVELS - 1) + [none]
    return inv_dz, face, sub, base, sup, keep


def solve_back(spacing_ref, got_ref, lam_hbm, high_hbm, low_hbm, out_ref,
               lam_ref, high_ref, low_ref, sems):
    lam_copy = start_copy(lam_hbm, lam_ref, sems, 16)
    copies = []
    for pair in range(8):
        block = slice(LANES * pair, LANES * (pair + 1))
        copies.append(
            (
                start_copy(high_hbm.at[block, :], high_ref.at[block, :], sems, 2 * pair),
                start_copy(low_hbm.at[block, :], low_ref.at[block, :], sems, 2 * pair + 1),
            )
        )
    lam_copy.wait()
    at = lax.axis_index("x")
    lam = lam_ref[...]
    rows = lam.shape[0]
    lane = lane_of((rows, LANES))
    inv_dz, face, sub, base, sup, keep = vertical([spacing_ref[k] for k in range(LEVELS)])
    ratios = []
    values = []
    below = None
    for k in range(LEVELS):
        packed = got_ref[k % 4]
        half = k // 4
        flux = roll(packed, -(2 * half + 1), 1) * face[k]
        right = roll(packed, -2 * half, 1) - flux
        if k > 0:
            right = right + below
        below = flux
        diagonal = lam + base[k]
        if k > 0:
            diagonal = diagonal - sub[k] * ratios[-1]
            right = right - sub[k] * values[-1]
        inverse = 1.0 / diagonal
        ratios.append(sup[k] * inverse)
        values.append(right * inverse)
    result = [None] * LEVELS
    result[-1] = values[-1]
    for k in range(LEVELS - 2, -1, -1):
        result[k] = values[k] - ratios[k] * result[k + 1]
    scaled = [result[k] * inv_dz[k] for k in range(LEVELS)] + [jnp.zeros_like(lam)]
    change = [(scaled[k] - scaled[k + 1]) * keep[k] for k in range(LEVELS)]

    def own(items, half):
        value = items[4 * half]
        for x in range(1, 4):
            value = jnp.where(at == x, items[4 * half + x], value)
        return value

    column = lane % 4
    both = own(result, 0)
    both = jnp.where(column == 1, roll(own(change, 0), 1, 1), both)
    both = jnp.where(column == 2, roll(own(result, 1), 2, 1), both)
    both = jnp.where(column == 3, roll(own(change, 1), 3, 1), both)
    high, low = split_f32(both)
    blocks = [
        jnp.where(lane % 16 < 4, roll(high, -4 * g, 1), roll(low, 4 - 4 * g, 1)).astype(bf16)
        for g in range(4)
    ]
    columns = jnp.concatenate(blocks, axis=0)
    within = lane_of((64, LANES)) % 16
    packed = [jnp.zeros((64, LANES), f32)] * 4
    for pair in range(8):
        block = slice(LANES * pair, LANES * (pair + 1))
        for copy in copies[pair]:
            copy.wait()
        got = dot(high_ref[block, :], columns) + dot(low_ref[block, :], columns)
        got = got + roll(got, -4, 1)
        for one in range(2):
            j = 2 * pair + one
            moved = roll(got[64 * one : 64 * (one + 1)], j, 1)
            for c in range(4):
                packed[c] = jnp.where(within == (j + c) % 16, moved, packed[c])
    for half in range(2):
        part = slice(64 * half, 64 * (half + 1))
        pressure = roll(packed[2 * half], -2 * half, 1)
        change_up = roll(packed[2 * half + 1], -(2 * half + 1), 1)
        before = jnp.where(
            within > 0, roll(pressure, 1, 1), roll(roll(pressure, 1, 0), -15, 1)
        )
        out_ref[part, 0, 0:LANES] = pressure
        out_ref[part, 0, LANES : 2 * LANES] = change_up
        out_ref[part, 0, 2 * LANES : 3 * LANES] = before - pressure


CHUNK = 256


def unit_rows(shape, axis):
    return lax.broadcasted_iota(jnp.int32, shape, axis) % 8


def same_row(value):
    shape = value.shape
    return jnp.where(unit_rows(shape, 0) == unit_rows(shape, 1), value, 0.0)


def gather(shape, step):
    to = lax.broadcasted_iota(jnp.int32, shape, 1)
    return (lax.broadcasted_iota(jnp.int32, shape, 0) // step == to).astype(f32)


def exact(a, b):
    return jnp.dot(a, b, precision=lax.Precision.HIGHEST, preferred_element_type=f32)


def spread(weight, columns):
    tall, wide = weight.shape
    step = (
        lax.broadcasted_iota(jnp.int32, (wide, columns), 1) // 8
        == lax.broadcasted_iota(jnp.int32, (wide, columns), 0)
    ).astype(f32)
    value = exact(weight, step)
    value = jnp.broadcast_to(value[:, None, :], (tall, 8, columns)).reshape(8 * tall, columns)
    return same_row(value)


def closure_forward(vel_hbm, buoy_hbm, win_ref, bin_ref, wmid_ref, bmid_ref, wout_ref,
                    ey_hbm, ex_hbm, mark_ref,
                    f1h_hbm, f1l_hbm, f2h_hbm, f2l_hbm, ft_hbm, wide_hbm, win_hbm, lam_hbm, done_ref,
                    f1h_ref, f1l_ref, f2h_ref, f2l_ref, ft_ref, wide_ref, in_ref, lam_ref,
                    vel_ref, buoy_ref, ex_ref, sems, out_sems):
    copies = [
        start_copy(vel_hbm, vel_ref, sems, 0),
        start_copy(buoy_hbm, buoy_ref, sems, 1),
        start_copy(ex_hbm, ex_ref, sems, 2),
        start_copy(ey_hbm, lam_ref, sems, 3),
    ]
    win_t = win_ref[...]
    wmid = wmid_ref[...]
    wout_h, wout_l = split_f32(spread(wout_ref[...].T, 32))
    wide_ref[:, 0:96] = jnp.concatenate([wout_h, wout_h, wout_l], axis=1).astype(bf16)
    wide_ref[:, 96:128] = jnp.zeros((256, 32), bf16)
    wide_ref[:, 128:384], wide_ref[:, 384:640] = split(spread(wmid.T, 256))
    in_ref[:, 0:256], in_ref[:, 256:512] = split(spread(win_t, 256))
    win_h, win_l = split_f32(spread(win_t.T, 32))
    win_cat = jnp.concatenate([win_h, win_h, win_l], axis=1).astype(bf16)
    wmh, wml = split(spread(wmid, 256))

    def tall(row):
        column = row.T
        return jnp.broadcast_to(column[:, None, :], (32, 8, 1)).reshape(256, 1)

    b_in, b_mid = tall(bin_ref[...]), tall(bmid_ref[...])
    for copy in copies:
        copy.wait()
    lam_ref[...] = lam_ref[...] + ex_ref[pl.ds(lax.axis_index(PLANE), 1), :]
    copies = [
        start_copy(wide_ref, wide_hbm, out_sems, 0),
        start_copy(in_ref, win_hbm, out_sems, 1),
        start_copy(lam_ref, lam_hbm, out_sems, 2),
    ]
    width = buoy_ref.shape[-1]
    for half in range(2):
        part = slice(8 * half, 8 * (half + 1))
        for start in range(0, width, CHUNK):
            col = slice(start, start + CHUNK)
            to = slice(half * width + start, half * width + start + CHUNK)
            feats = jnp.concatenate(
                [vel_ref[c, 0, part, col] for c in range(3)] + [buoy_ref[0, part, col]], axis=0
            )
            high, low = split_f32(feats)
            stack = jnp.concatenate([high, low, high], axis=0).astype(bf16)
            ft_ref[:, to] = jnp.concatenate(
                [high, low, jnp.ones((32, CHUNK), f32)], axis=0
            ).astype(bf16)
            first = jnp.tanh(dot(win_cat, stack) + b_in)
            fh, fl = split(first)
            f1h_ref[:, to] = fh
            f1l_ref[:, to] = fl
            second = dot(wmh, fh) + dot(wmh, fl) + dot(wml, fh)
            second = jnp.tanh(second + b_mid)
            sh, sl = split(second)
            f2h_ref[:, to] = sh
            f2l_ref[:, to] = sl
        whole = slice(half * width, (half + 1) * width)
        for i, (held, target) in enumerate(
            (
                (f1h_ref, f1h_hbm),
                (f1l_ref, f1l_hbm),
                (f2h_ref, f2h_hbm),
                (f2l_ref, f2l_hbm),
                (ft_ref, ft_hbm),
            )
        ):
            copies.append(
                start_copy(held.at[:, whole], target.at[:, whole], out_sems, 3 + 5 * half + i)
            )
    done_ref[...] = jnp.zeros(done_ref.shape, f32)
    for copy in copies:
        copy.wait()


def closure_back(msg_ref, high_hbm, low_hbm, cot_hbm, mask_hbm,
                 f1h_hbm, f1l_hbm, f2h_hbm, f2l_hbm, ft_hbm, wide_hbm,
                 total_ref, e1h_hbm, e1l_hbm, proj_hbm,
                 high_ref, low_ref, cot_ref, mask_ref,
                 f1h_ref, f1l_ref, f2h_ref, f2l_ref, ft_ref, wide_ref,
                 e1h_ref, e1l_ref, proj_ref, e2h_ref, e2l_ref, dl_ref, b2_ref, sems, out_sems):
    width = mask_ref.shape[-1]
    table_copies = [start_copy(high_hbm, high_ref, sems, 0), start_copy(low_hbm, low_ref, sems, 1)]
    copies = [
        start_copy(cot_hbm, cot_ref, sems, 2),
        start_copy(mask_hbm, mask_ref, sems, 3),
        start_copy(wide_hbm, wide_ref, sems, 4),
    ]
    hidden_copies = []
    for half in range(2):
        whole = slice(half * width, (half + 1) * width)
        hidden_copies.append(
            [
                start_copy(held.at[:, whole], target.at[:, whole], sems, 5 + 4 * half + i)
                for i, (held, target) in enumerate(
                    (
                        (f2h_hbm, f2h_ref),
                        (f2l_hbm, f2l_ref),
                        (f1h_hbm, f1h_ref),
                        (f1l_hbm, f1l_ref),
                    )
                )
            ]
        )
    ft_copy = start_copy(ft_hbm, ft_ref, sems, 13)
    lane = lane_of((LANES, LANES))
    columns = []
    for t in range(8):
        value = jnp.zeros((LANES, LANES), f32)
        for field in range(3):
            item = msg_ref[:, 0, LANES * field : LANES * (field + 1)]
            value = jnp.where(lane // 16 == field, roll(item, 16 * (field - t), 1), value)
        high, low = split_f32(value)
        columns.append((high + roll(low, 64, 1)).T.astype(bf16))
    columns = jnp.concatenate(columns, axis=1)
    for copy in table_copies:
        copy.wait()
    field = dot(columns, high_ref[...]) + dot(columns, low_ref[...])
    pressure = field[0:16] + field[64:80]
    east_back = roll(pressure, 1, 1) - pressure
    for copy in copies:
        copy.wait()
    projected = (
        cot_ref[0, 0] - east_back,
        cot_ref[1, 0] - (field[32:48] + field[96:112]),
        cot_ref[2, 0] - (field[16:32] + field[80:96]),
    )
    wet = mask_ref[0].astype(f32)
    for c in range(3):
        proj_ref[c, 0] = projected[c]
    out_copies = [start_copy(proj_ref, proj_hbm, out_sems, 0)]
    deltas = [value * wet for value in projected]
    blank = jnp.zeros((8, CHUNK), f32)
    bias2 = jnp.zeros((256, LANES), f32)
    for half in range(2):
        part = slice(8 * half, 8 * (half + 1))
        for copy in hidden_copies[half]:
            copy.wait()
        for start in range(0, width, CHUNK):
            col = slice(start, start + CHUNK)
            to = slice(half * width + start, half * width + start + CHUNK)
            delta = jnp.concatenate([value[part, col] for value in deltas] + [blank], axis=0)
            dh, dl = split_f32(delta)
            stack = jnp.concatenate([dh, dl, dh], axis=0).astype(bf16)
            dl_ref[:, to] = stack[0:64]
            second = f2h_ref[:, to].astype(f32) + f2l_ref[:, to].astype(f32)
            err2 = dot(wide_ref[:, 0:96], stack) * (1.0 - second * second)
            bias2 = bias2 + err2[:, 0:LANES] + err2[:, LANES : 2 * LANES]
            e2h, e2l = split(err2)
            e2h_ref[:, to] = e2h
            e2l_ref[:, to] = e2l
            first = f1h_ref[:, to].astype(f32) + f1l_ref[:, to].astype(f32)
            err1 = (
                dot(wide_ref[:, 128:384], e2h)
                + dot(wide_ref[:, 128:384], e2l)
                + dot(wide_ref[:, 384:640], e2h)
            )
            err1 = err1 * (1.0 - first * first)
            e1h, e1l = split(err1)
            e1h_ref[:, to] = e1h
            e1l_ref[:, to] = e1l
        whole = slice(half * width, (half + 1) * width)
        out_copies.append(
            start_copy(e1h_ref.at[:, whole], e1h_hbm.at[:, whole], out_sems, 1 + 2 * half)
        )
        out_copies.append(
            start_copy(e1l_ref.at[:, whole], e1l_hbm.at[:, whole], out_sems, 2 + 2 * half)
        )
    b2_ref[...] = bias2
    ft_copy.wait()
    mid = (
        dot_nt(e2h_ref[...], f1h_ref[...])
        + dot_nt(e2h_ref[...], f1l_ref[...])
        + dot_nt(e2l_ref[...], f1h_ref[...])
    )
    both1 = dot_nt(e1h_ref[...], ft_ref[...])
    rest1 = dot_nt(e1l_ref[...], ft_ref[...])
    win = both1[:, 0:32] + both1[:, 32:64] + rest1[:, 0:32]
    bin_ = both1[:, 64:96] + rest1[:, 64:96]
    both2 = dot_nt(f2h_ref[...], dl_ref[...])
    rest2 = dot_nt(f2l_ref[...], dl_ref[...])
    wout = both2[:, 0:32] + both2[:, 32:64] + rest2[:, 0:32]

    def fold_rows(value):
        return jnp.sum(value.reshape(32, 8, value.shape[1]), axis=1)

    mid = exact(fold_rows(same_row(mid)), gather((256, LANES), 8))
    small = jnp.concatenate(
        [
            fold_rows(same_row(win)),
            fold_rows(same_row(wout)),
            fold_rows(jnp.where(lane_of((256, 32)) == 0, bin_, 0.0)),
        ],
        axis=1,
    )
    small = roll(exact(small, gather((96, LANES), 8)), 32, 1)
    b2 = jnp.sum(fold_rows(b2_ref[...]), axis=1, keepdims=True)
    every = mid + small + jnp.where(lane_of((32, LANES)) == 39, b2, 0.0)
    units = jnp.concatenate([every[8 * i : 8 * (i + 1), 0:32] for i in range(4)], axis=1)
    turned = every.T
    rows = [units[i : i + 1] for i in range(8)]
    for start in (32, 36):
        rows.append(
            jnp.concatenate([turned[start + i : start + i + 1] for i in range(4)], axis=1)
        )
    rows.append(jnp.concatenate([turned[40:41], jnp.zeros((1, 96), f32)], axis=1))
    for peer in range(32):
        for i, row in enumerate(rows):
            total_ref[peer, :, LANES * i : LANES * (i + 1)] = row
    for copy in out_copies:
        copy.wait()


def outgoing(proj_hbm, e1h_hbm, e1l_hbm, win_hbm, mark_ref, gvel_ref, gbuoy_ref,
             proj_ref, e1h_ref, e1l_ref, win_ref, sems):
    copies = [
        start_copy(proj_hbm, proj_ref, sems, 0),
        start_copy(e1h_hbm, e1h_ref, sems, 1),
        start_copy(e1l_hbm, e1l_ref, sems, 2),
        start_copy(win_hbm, win_ref, sems, 3),
    ]
    for copy in copies:
        copy.wait()
    width = gbuoy_ref.shape[-1]
    for half in range(2):
        part = slice(8 * half, 8 * (half + 1))
        to = slice(half * width, (half + 1) * width)
        out = (
            dot(win_ref[:, 0:256], e1h_ref[:, to])
            + dot(win_ref[:, 0:256], e1l_ref[:, to])
            + dot(win_ref[:, 256:512], e1h_ref[:, to])
        )
        for c in range(3):
            gvel_ref[c, 0, part, :] = proj_ref[c, 0, part, :] + out[8 * c : 8 * (c + 1)]
        gbuoy_ref[0, part, :] = out[24:32]


def sum_slab(got_ref, out_ref, mark_ref):
    total = jnp.sum(got_ref[...], axis=0)
    for peer in range(16):
        out_ref[peer] = total
    mark_ref[...] = jnp.zeros(mark_ref.shape, f32)


def sum_column(scale, got_ref, win_ref, bin_ref, wmid_ref, bmid_ref, wout_ref):
    total = jnp.sum(got_ref[...], axis=0) * scale
    rows = [total[:, LANES * i : LANES * (i + 1)] for i in range(11)]
    units = jnp.concatenate(rows[:8], axis=0)
    wmid_ref[...] = jnp.concatenate([units[:, 32 * i : 32 * (i + 1)] for i in range(4)], axis=0)
    win_ref[...] = jnp.concatenate([rows[8][:, 32 * i : 32 * (i + 1)] for i in range(4)], axis=0)
    wout_ref[...] = jnp.concatenate([rows[9][:, 32 * i : 32 * (i + 1)] for i in range(3)], axis=0)
    bmid_ref[...] = rows[9][:, 96:128]
    bin_ref[...] = rows[10][:, 0:32]


def shards(velocity, buoyancy, cell_mask, spacing, cotangent, w_in, b_in, w_mid, b_mid, w_out):
    levels, rows, width = buoyancy.shape
    depth = spacing.shape[0]
    span_y = rows * 64
    order = (np.arange(1024) % 128) * 8 + np.arange(1024) // 128
    table = dft_table(width)[order]
    x_high, x_low = two_parts(table)
    row_order = (np.arange(1024) % 64) * 16 + np.arange(1024) // 64
    y_high, y_low = two_parts(table[:, row_order].T)
    eigen = eigenvalue(width)
    lanes = np.arange(LANES)
    ey = eigen[order].reshape(4, 256)[lanes % 16 // 4].T.astype(np.float32)
    ex = eigen[(8 * np.arange(128))[:, None] + lanes[None, :] // 16].astype(np.float32)
    x_high, x_low, y_high, y_low, ey, ex = map(
        jnp.asarray, (x_high, x_low, y_high, y_low, ey, ex)
    )
    cells = rows * width // 8
    dma = pltpu.SemaphoreType.DMA
    type_of = jax.ShapeDtypeStruct
    table = pltpu.VMEM((1024, 1024), bf16)
    wide = pltpu.VMEM((256, cells), bf16)
    wide_type = pltpu.HBM((256, cells), bf16)
    mark_type = type_of((8, LANES), f32)
    table_flops = 4 * 1024 * 1024 * 128
    msg_type = type_of((128, 1, 3 * LANES), f32)
    msg, mark = call(
        forward_x,
        (msg_type, mark_type),
        (cotangent, x_high, x_low),
        hbm=(0, 1, 2),
        scratch=(table, table, pltpu.VMEM(cotangent.shape, f32), dma((17,))),
        flops=table_flops,
        name="forward_x",
    )
    msg = lax.all_to_all(msg, PLANE, 0, 0)

    *hidden, wide_w, win_w, lam, mark = call(
        closure_forward,
        (
            (wide_type,) * 4
            + (
                pltpu.HBM((96, cells), bf16),
                pltpu.HBM((256, 640), bf16),
                pltpu.HBM((32, 512), bf16),
                pltpu.HBM((256, LANES), f32),
                mark_type,
            )
        ),
        (velocity, buoyancy, w_in.T, b_in[None], w_mid, b_mid[None], w_out, ey, ex, mark),
        hbm=(0, 1, 7, 8),
        hbm_out=range(8),
        scratch=(wide,) * 4
        + (
            pltpu.VMEM((96, cells), bf16),
            pltpu.VMEM((256, 640), bf16),
            pltpu.VMEM((32, 512), bf16),
            pltpu.VMEM((256, LANES), f32),
            pltpu.VMEM(velocity.shape, f32),
            pltpu.VMEM(buoyancy.shape, f32),
            pltpu.VMEM((LANES, LANES), f32),
            dma((4,)),
            dma((13,)),
        ),
        flops=2 * 256 * 256 * cells * 4,
        name="closure_forward",
    )
    (gathered,) = call(
        forward_y,
        (type_of((4, 256, LANES), f32),),
        (msg, x_high, x_low, mark),
        hbm=(1, 2),
        scratch=(pltpu.VMEM((1024, LANES), f32), table, table, dma((8,))),
        flops=table_flops,
        name="forward_y",
    )
    gathered = lax.all_to_all(gathered, "x", 0, 0)
    (msg,) = call(
        solve_back,
        (msg_type,),
        (spacing, gathered, lam, y_high, y_low),
        smem=(0,),
        hbm=(2, 3, 4),
        scratch=(pltpu.VMEM((256, LANES), f32), table, table, dma((17,))),
        flops=table_flops,
        name="solve_back",
    )
    msg = lax.all_to_all(msg, PLANE, 0, 0)
    totals, e1h, e1l, projected = call(
        closure_back,
        (
            type_of((32, 1, 11 * LANES), f32),
            wide_type,
            wide_type,
            pltpu.HBM(cotangent.shape, f32),
        ),
        (msg, x_high, x_low, cotangent, cell_mask, *hidden, wide_w),
        hbm=range(1, 11),
        hbm_out=(1, 2, 3),
        scratch=(
            table,
            table,
            pltpu.VMEM(cotangent.shape, f32),
            pltpu.VMEM(cell_mask.shape, jnp.int32),
            wide,
            wide,
            wide,
            wide,
            pltpu.VMEM((96, cells), bf16),
            pltpu.VMEM((256, 640), bf16),
            wide,
            wide,
            pltpu.VMEM(cotangent.shape, f32),
            wide,
            wide,
            pltpu.VMEM((64, cells), bf16),
            pltpu.VMEM((256, LANES), f32),
            dma((14,)),
            dma((5,)),
        ),
        flops=table_flops + 2 * 256 * 256 * cells * 10,
        name="closure_back",
    )
    totals = lax.all_to_all(totals, SLAB, 0, 0)
    totals, mark = call(
        sum_slab, (type_of((16, 1, 11 * LANES), f32), mark_type), (totals,), name="sum_slab"
    )
    totals = lax.all_to_all(totals, COLUMN, 0, 0)
    grad_velocity, grad_buoyancy = call(
        outgoing,
        (type_of(cotangent.shape, f32), type_of(buoyancy.shape, f32)),
        (projected, e1h, e1l, win_w, mark),
        hbm=(0, 1, 2, 3),
        scratch=(
            pltpu.VMEM(cotangent.shape, f32),
            wide,
            wide,
            pltpu.VMEM((32, 512), bf16),
            dma((4,)),
        ),
        flops=2 * 256 * 256 * cells,
        name="outgoing",
    )
    scale = 1.0 / math.sqrt(width * span_y * depth)
    grad_in, grad_b_in, grad_mid, grad_b_mid, grad_out = call(
        functools.partial(sum_column, scale),
        (
            type_of((4, 32), f32),
            type_of((1, 32), f32),
            type_of((32, 32), f32),
            type_of((1, 32), f32),
            type_of((3, 32), f32),
        ),
        (totals,),
        name="sum_column",
    )
    return (
        grad_velocity,
        grad_buoyancy,
        grad_in.T,
        grad_b_in[0],
        grad_mid,
        grad_b_mid[0],
        grad_out,
    )


def solution(mesh):
    fine = Mesh(
        mesh.devices.reshape([size for _, size in FINE]), tuple(name for name, _ in FINE)
    )
    field = P(None, NARROW, WIDE, None)
    cell = P(NARROW, WIDE, None)
    in_specs = (field, cell, cell, P(), field, P(), P(), P(), P(), P())
    out_specs = (field, cell, P(), P(), P(), P(), P())
    return jax.shard_map(shards, mesh=fine, in_specs=in_specs, out_specs=out_specs, check_vma=False)
```

```python
import functools
import math

import jax
import jax.numpy as jnp
import ml_dtypes
import numpy as np
from jax import lax
from jax.experimental import pallas as pl
from jax.experimental.pallas import tpu as pltpu
from jax.sharding import Mesh
from jax.sharding import PartitionSpec as P

free_surface = 0.05
f32 = jnp.float32
bf16 = jnp.bfloat16
LANES = 128
LEVELS = 8
VMEM_LIMIT = 24 * 1024 * 1024

FINE = (("y", 4), ("zl", 8), ("c", 2), ("zh", 2), ("x", 4))
WIDE = ("y", "zl", "c")
NARROW = ("zh", "x")
PLANE = ("zh", "y", "zl", "c")
SLAB = ("y", "x", "c")
COLUMN = ("zl", "zh")


def dft_table(count, length):
    indices = np.arange(count)
    angle = 2.0 * np.pi / count * (indices[:, None] * indices[None, :] % count)
    return np.concatenate([np.cos(angle), np.sin(angle)], axis=0) * np.sqrt(2.0 / length)


def twiddles(count, length):
    angle = 2.0 * np.pi / length * np.arange(count)[:, None] * np.arange(4)[None, :]
    held = np.zeros((count, LANES))
    held[:, 0:8:2] = np.cos(angle)
    held[:, 1:8:2] = np.sin(angle)
    return held.astype(np.float32)


def wavenumbers(length):
    half = np.arange(length // 2)
    return np.concatenate([half, np.where(half == 0, length // 2, half)])


def two_parts(table):
    high = table.astype(np.float32).astype(ml_dtypes.bfloat16)
    low = (table - high.astype(np.float64)).astype(np.float32).astype(ml_dtypes.bfloat16)
    return np.concatenate([high, low], axis=0)


def eigenvalue(length):
    return -4.0 * np.sin(np.pi / length * wavenumbers(length)) ** 2


def split(value):
    high = value.astype(bf16)
    low = (value - high.astype(f32)).astype(bf16)
    return high, low


def split_f32(value):
    high = value.astype(bf16).astype(f32)
    return high, value - high


def dot(a, b):
    return jnp.dot(a, b, preferred_element_type=f32)


def dot_table(table_ref, b):
    rows = table_ref.shape[0] // 2
    return dot(table_ref[0:rows], b) + dot(table_ref[rows : 2 * rows], b)


def dot_nt(a, b):
    return lax.dot_general(a, b, (((1,), (1,)), ((), ())), preferred_element_type=f32)


def roll(value, shift, axis):
    size = value.shape[axis]
    shift = shift % size
    return value if shift == 0 else pltpu.roll(value, shift, axis)


def lane_of(shape):
    return lax.broadcasted_iota(jnp.int32, shape, len(shape) - 1)


def start_copy(source, target, sems, index):
    copy = pltpu.make_async_copy(source, target, sems.at[index])
    copy.start()
    return copy


def call(kernel, out_shape, args, smem=(), hbm=(), hbm_out=(), scratch=(), flops=0, name=None):
    def space(index, held):
        return pl.BlockSpec(memory_space=held.get(index, pltpu.VMEM))

    held = {i: pltpu.SMEM for i in smem} | {i: pl.ANY for i in hbm}
    args = [
        pltpu.with_memory_space_constraint(a, pltpu.HBM) if i in hbm else a
        for i, a in enumerate(args)
    ]
    moved = sum(int(np.prod(a.shape)) * a.dtype.itemsize for a in args)
    return pl.pallas_call(
        kernel,
        out_shape=out_shape,
        in_specs=[space(i, held) for i in range(len(args))],
        out_specs=[space(i, {o: pl.ANY for o in hbm_out}) for i in range(len(out_shape))],
        scratch_shapes=list(scratch),
        compiler_params=pltpu.CompilerParams(vmem_limit_bytes=VMEM_LIMIT),
        cost_estimate=pl.CostEstimate(flops=flops, bytes_accessed=moved, transcendentals=0),
        name=name,
    )(*args)


def first_row(shape):
    return lax.broadcasted_iota(jnp.int32, shape, 0) == 0


def join(cos_r, sin_r):
    even_c, even_s = cos_r[0] + cos_r[2], sin_r[0] + sin_r[2]
    odd_c, odd_s = cos_r[1] + cos_r[3], sin_r[1] + sin_r[3]
    top = first_row(even_c.shape)
    ends = jnp.where(top, math.sqrt(0.5), 1.0)
    return (
        (even_c + odd_c) * ends,
        cos_r[0] - cos_r[2] - (sin_r[1] - sin_r[3]),
        jnp.where(top, even_c - odd_c, even_s + odd_s) * ends,
        sin_r[0] - sin_r[2] + (cos_r[1] - cos_r[3]),
    )


def part_back(blocks):
    top = first_row(blocks[0].shape)
    ends = jnp.where(top, math.sqrt(0.5), 1.0)
    low_c, high_c, low_s, high_s = blocks
    low_c, low_s = low_c * ends, low_s * ends
    last = jnp.where(top, low_s, 0.0)
    low_s = jnp.where(top, 0.0, low_s)
    even, odd = low_c + last, low_c - last
    return (
        (even + high_c, odd + high_s, even - high_c, odd - high_s),
        (low_s + high_s, low_s - high_c, low_s - high_s, low_s + high_c),
    )


def turn(cos_part, sin_part, cos_turn, sin_turn):
    return cos_part * cos_turn - sin_part * sin_turn, sin_part * cos_turn + cos_part * sin_turn


def turn_of(turn_ref, remainder):
    rows, shape = slice(0, 256), (256, LANES)
    return (
        jnp.broadcast_to(turn_ref[rows, 2 * remainder : 2 * remainder + 1], shape),
        jnp.broadcast_to(turn_ref[rows, 2 * remainder + 1 : 2 * remainder + 2], shape),
    )


def forward_x(cot_hbm, table_hbm, turn_hbm, out_ref, mark_ref,
              table_ref, turn_ref, cot_ref, line_ref, sems):
    first = start_copy(cot_hbm, cot_ref, sems, 0)
    copies = [
        start_copy(table_hbm, table_ref, sems, 1),
        start_copy(turn_hbm, turn_ref, sems, 2),
    ]
    first.wait()
    east, north, up = cot_ref[0, 0], cot_ref[1, 0], cot_ref[2, 0]
    rows, width = east.shape
    east = east - roll(east, -1, 1)
    high, low = split_f32(jnp.concatenate([east, north, up], axis=0))
    none = jnp.zeros((rows, width), f32)
    line_ref[...] = jnp.concatenate([high, none, low, none], axis=0).T
    lines = jnp.concatenate(
        [line_ref[pl.ds(r, 256, stride=4), :].astype(bf16) for r in range(4)], axis=1
    )
    for copy in copies:
        copy.wait()
    got = dot_table(table_ref, lines)
    cos_r, sin_r = [], []
    for r in range(4):
        cos_part = got[0:256, LANES * r : LANES * (r + 1)]
        sin_part = got[256:512, LANES * r : LANES * (r + 1)]
        if r > 0:
            cos_part, sin_part = turn(cos_part, sin_part, *turn_of(turn_ref, r))
        cos_r.append(cos_part)
        sin_r.append(sin_part)
    blocks = [block + roll(block, 64, 1) for block in join(cos_r, sin_r)]
    lane = lane_of((LANES, LANES))
    for field in range(3):
        packed = jnp.zeros((LANES, LANES), f32)
        for t in range(8):
            block = blocks[t // 2][LANES * (t % 2) : LANES * (t % 2 + 1)]
            packed = jnp.where(lane // 16 == t, roll(block, 16 * (t - field), 1), packed)
        out_ref[:, 0, LANES * field : LANES * (field + 1)] = packed
    mark_ref[...] = jnp.zeros(mark_ref.shape, f32)


def pair_turns(turn_ref, pair, within):
    one, two = turn_of(turn_ref, 2 * pair), turn_of(turn_ref, 2 * pair + 1)
    return tuple(jnp.where(within < 8, a, b) for a, b in zip(one, two))


def forward_y(msg_ref, table_hbm, turn_hbm, second_hbm, back_hbm, mark_ref,
              out_ref, turn_ref, second_ref, back_ref, table_ref, sems):
    copies = [
        start_copy(table_hbm, table_ref, sems, 0),
        start_copy(turn_hbm, turn_ref, sems, 1),
    ]
    later_copies = [
        start_copy(back_hbm, back_ref, sems, 2),
        start_copy(second_hbm, second_ref, sems, 3),
    ]
    within = lane_of((64, LANES)) % 16
    highs = []
    lows = []
    for half in range(2):
        part = slice(64 * half, 64 * (half + 1))
        east = msg_ref[part, 0, 0:LANES]
        north = msg_ref[part, 0, LANES : 2 * LANES]
        up = msg_ref[part, 0, 2 * LANES : 3 * LANES]
        after = jnp.where(
            within < 15, roll(north, -1, 1), roll(roll(north, -1, 0), 15, 1)
        )
        for value in (east + north - after, up):
            high, low = split_f32(value)
            highs.append(high)
            lows.append(low)
    shifted = [roll(value, c, 1) for c, value in enumerate(highs + lows)]

    def line_of(j, to):
        line = shifted[0]
        for c in range(1, 8):
            line = jnp.where(within == (c + j) % 16, shifted[c], line)
        return roll(line, to - j, 1)

    lines = []
    for pair in range(2):
        rows = []
        for step in range(4):
            j = 4 * step + 2 * pair
            rows.append(jnp.where(within < 8, line_of(j, 0), line_of(j + 1, 8)).astype(bf16))
        lines.append(jnp.concatenate(rows, axis=0))
    lines = jnp.concatenate(lines, axis=1)
    for copy in copies:
        copy.wait()
    got = dot_table(table_ref, lines)
    within = lane_of((256, LANES)) % 16
    turned = [
        turn(
            got[0:256, LANES * pair : LANES * (pair + 1)],
            got[256:512, LANES * pair : LANES * (pair + 1)],
            *pair_turns(turn_ref, pair, within),
        )
        for pair in range(2)
    ]
    cos_r = [turned[0][0], roll(turned[0][0], -8, 1), turned[1][0], roll(turned[1][0], -8, 1)]
    sin_r = [turned[0][1], roll(turned[0][1], -8, 1), turned[1][1], roll(turned[1][1], -8, 1)]
    packed = jnp.zeros((256, LANES), f32)
    for g, block in enumerate(join(cos_r, sin_r)):
        block = block + roll(block, -4, 1)
        packed = jnp.where(within // 4 == g, roll(block, 4 * g, 1), packed)
    for peer in range(4):
        out_ref[peer] = packed
    for copy in later_copies:
        copy.wait()


def vertical(spacing):
    one = jnp.ones((1, LANES), f32)
    none = jnp.zeros((1, LANES), f32)
    spacing = [one * spacing[k] for k in range(LEVELS)]
    inv_dz = [1.0 / value for value in spacing]
    face = [2.0 / (spacing[k] + spacing[k + 1]) for k in range(LEVELS - 1)] + [none]
    lower = [none] + [inv_dz[k] * face[k - 1] for k in range(1, LEVELS)]
    upper = [inv_dz[k] * face[k] for k in range(LEVELS)]
    base = [-(lower[k] + upper[k]) for k in range(LEVELS)]
    base[-1] = base[-1] - free_surface * inv_dz[-1]
    sub = [none] + upper[:-1]
    sup = lower[1:] + [none]
    keep = [one] * (LEVELS - 1) + [none]
    return inv_dz, face, sub, base, sup, keep


def solve_back(got_ref, turn_ref, table_hbm, cot_hbm, mask_hbm, first_hbm, wide_hbm,
               out_ref, cot_ref, mask_ref, first_ref, wide_ref, table_ref, sems):
    copies = [start_copy(table_hbm, table_ref, sems, 0)]
    later_copies = [
        start_copy(cot_hbm, cot_ref, sems, 1),
        start_copy(mask_hbm, mask_ref, sems, 2),
        start_copy(wide_hbm, wide_ref, sems, 3),
        start_copy(first_hbm, first_ref, sems, 4),
    ]
    at = lax.axis_index("x")
    rows = got_ref.shape[1]
    lam = turn_ref[256 : 256 + rows]
    lane = lane_of((rows, LANES))
    inv_dz, face, sub, base, sup, keep = (
        [turn_ref[512 + 8 * i + k : 513 + 8 * i + k] for k in range(LEVELS)]
        for i in range(6)
    )
    ratios = []
    values = []
    below = None
    for k in range(LEVELS):
        packed = got_ref[k % 4]
        half = k // 4
        flux = roll(packed, -(2 * half + 1), 1) * face[k]
        right = roll(packed, -2 * half, 1) - flux
        if k > 0:
            right = right + below
        below = flux
        diagonal = lam + base[k]
        if k > 0:
            diagonal = diagonal - sub[k] * ratios[-1]
            right = right - sub[k] * values[-1]
        inverse = 1.0 / diagonal
        ratios.append(sup[k] * inverse)
        values.append(right * inverse)
    result = [None] * LEVELS
    result[-1] = values[-1]
    for k in range(LEVELS - 2, -1, -1):
        result[k] = values[k] - ratios[k] * result[k + 1]
    scaled = [result[k] * inv_dz[k] for k in range(LEVELS)] + [jnp.zeros_like(lam)]
    change = [(scaled[k] - scaled[k + 1]) * keep[k] for k in range(LEVELS)]

    def own(items, half):
        value = items[4 * half]
        for x in range(1, 4):
            value = jnp.where(at == x, items[4 * half + x], value)
        return value

    column = lane % 4
    both = own(result, 0)
    both = jnp.where(column == 1, roll(own(change, 0), 1, 1), both)
    both = jnp.where(column == 2, roll(own(result, 1), 2, 1), both)
    both = jnp.where(column == 3, roll(own(change, 1), 3, 1), both)
    for copy in copies:
        copy.wait()
    within = lane % 16
    blocks = []
    for g in range(4):
        block = roll(both, -4 * g, 1)
        blocks.append(jnp.where(within < 8, block, roll(block, 8, 1)))
    cos_r, sin_r = part_back(blocks)
    parts = ([], [])
    for pair in range(2):
        cos_part = jnp.where(within < 8, cos_r[2 * pair], cos_r[2 * pair + 1])
        sin_part = jnp.where(within < 8, sin_r[2 * pair], sin_r[2 * pair + 1])
        cos_turn, sin_turn = pair_turns(turn_ref, pair, within)
        for i, value in enumerate(turn(cos_part, sin_part, cos_turn, -sin_turn)):
            high, low = split_f32(jnp.where(within % 8 < 4, value, 0.0))
            parts[i].append((high + roll(low, 4, 1)).astype(bf16))
    columns = jnp.concatenate([jnp.concatenate(part, axis=1) for part in parts], axis=0)
    got = dot_table(table_ref, columns)
    within = lane_of((64, LANES)) % 16
    packed = [jnp.zeros((64, LANES), f32)] * 4
    for pair in range(2):
        found = got[:, LANES * pair : LANES * (pair + 1)]
        found = found + roll(found, -4, 1)
        for step in range(4):
            for one in range(2):
                j = 4 * step + 2 * pair + one
                moved = roll(found[64 * step : 64 * (step + 1)], j - 8 * one, 1)
                for c in range(4):
                    packed[c] = jnp.where(within == (j + c) % 16, moved, packed[c])
    for half in range(2):
        part = slice(64 * half, 64 * (half + 1))
        pressure = roll(packed[2 * half], -2 * half, 1)
        change_up = roll(packed[2 * half + 1], -(2 * half + 1), 1)
        before = jnp.where(
            within > 0, roll(pressure, 1, 1), roll(roll(pressure, 1, 0), -15, 1)
        )
        out_ref[part, 0, 0:LANES] = pressure
        out_ref[part, 0, LANES : 2 * LANES] = change_up
        out_ref[part, 0, 2 * LANES : 3 * LANES] = before - pressure
    for copy in later_copies:
        copy.wait()


CHUNK = 1024


def unit_rows(shape, axis):
    return lax.broadcasted_iota(jnp.int32, shape, axis) % 8


def same_row(value):
    shape = value.shape
    return jnp.where(unit_rows(shape, 0) == unit_rows(shape, 1), value, 0.0)


def gather(shape, step):
    to = lax.broadcasted_iota(jnp.int32, shape, 1)
    return (lax.broadcasted_iota(jnp.int32, shape, 0) // step == to).astype(f32)


def exact(a, b):
    return jnp.dot(a, b, precision=lax.Precision.HIGHEST, preferred_element_type=f32)


def spread(weight, columns):
    tall, wide = weight.shape
    step = (
        lax.broadcasted_iota(jnp.int32, (wide, columns), 1) // 8
        == lax.broadcasted_iota(jnp.int32, (wide, columns), 0)
    ).astype(f32)
    value = exact(weight, step)
    value = jnp.broadcast_to(value[:, None, :], (tall, 8, columns)).reshape(8 * tall, columns)
    return same_row(value)


def closure_forward(vel_hbm, buoy_hbm, win_ref, bin_ref, wmid_ref, bmid_ref, wout_ref,
                    fixed_hbm, mark_ref, spacing_ref,
                    first_hbm, second_hbm, wide_hbm, turn_hbm, done_ref,
                    first_ref, second_ref, wide_ref, turn_ref, vel_ref, buoy_ref, sems, out_sems):
    copies = [
        start_copy(vel_hbm, vel_ref, sems, 0),
        start_copy(buoy_hbm, buoy_ref, sems, 1),
        start_copy(fixed_hbm, turn_ref, sems, 2),
    ]
    win_t = win_ref[...]
    wmid = wmid_ref[...]
    wout_h, wout_l = split_f32(spread(wout_ref[...].T, 32))
    wide_ref[0:256, 0:96] = jnp.concatenate([wout_h, wout_h, wout_l], axis=1).astype(bf16)
    wide_ref[0:256, 96:128] = jnp.zeros((256, 32), bf16)
    wide_ref[0:256, 128:384], wide_ref[0:256, 384:640] = split(spread(wmid.T, 256))
    wide_ref[256:288, 0:128] = jnp.zeros((32, 128), bf16)
    wide_ref[256:288, 128:384], wide_ref[256:288, 384:640] = split(spread(win_t, 256))
    win_h, win_l = split_f32(spread(win_t.T, 32))
    win_cat = jnp.concatenate([win_h, win_h, win_l], axis=1).astype(bf16)
    wmh, wml = split(spread(wmid, 256))

    def tall(row):
        column = row.T
        return jnp.broadcast_to(column[:, None, :], (32, 8, 1)).reshape(256, 1)

    b_in, b_mid = tall(bin_ref[...]), tall(bmid_ref[...])
    for copy in copies:
        copy.wait()
    own = turn_ref[pl.ds(512 + lax.axis_index(PLANE), 1), :]
    turn_ref[256:512] = turn_ref[256:512] + own
    for i, rows in enumerate(vertical([spacing_ref[k] for k in range(LEVELS)])):
        turn_ref[512 + 8 * i : 520 + 8 * i] = jnp.concatenate(rows, axis=0)
    copies = [
        start_copy(wide_ref, wide_hbm, out_sems, 0),
        start_copy(turn_ref, turn_hbm, out_sems, 1),
    ]
    width = buoy_ref.shape[-1]
    for half in range(2):
        part = slice(8 * half, 8 * (half + 1))
        for start in range(0, width, CHUNK):
            col = slice(start, start + CHUNK)
            to = slice(half * width + start, half * width + start + CHUNK)
            feats = jnp.concatenate(
                [vel_ref[c, 0, part, col] for c in range(3)] + [buoy_ref[0, part, col]], axis=0
            )
            high, low = split_f32(feats)
            stack = jnp.concatenate([high, low, high], axis=0).astype(bf16)
            first_ref[512:608, to] = jnp.concatenate(
                [high, low, jnp.ones((32, CHUNK), f32)], axis=0
            ).astype(bf16)
            first = jnp.tanh(dot(win_cat, stack) + b_in)
            fh, fl = split(first)
            first_ref[0:256, to] = fh
            first_ref[256:512, to] = fl
            second = dot(wmh, fh) + dot(wmh, fl) + dot(wml, fh)
            second = jnp.tanh(second + b_mid)
            sh, sl = split(second)
            second_ref[0:256, to] = sh
            second_ref[256:512, to] = sl
        whole = slice(half * width, (half + 1) * width)
        for i, (held, target) in enumerate(((first_ref, first_hbm), (second_ref, second_hbm))):
            copies.append(
                start_copy(held.at[:, whole], target.at[:, whole], out_sems, 2 + 2 * half + i)
            )
    done_ref[...] = jnp.zeros(done_ref.shape, f32)
    for copy in copies:
        copy.wait()


def closure_back(msg_ref, turn_ref, second_ref, table_ref, cot_ref, mask_ref, first_ref,
                 wide_ref, total_ref, gvel_hbm, gbuoy_hbm,
                 line_ref, e1h_ref, e1l_ref, e2h_ref, e2l_ref, dl_ref, b2_ref,
                 gvel_ref, gbuoy_ref, out_sems):
    width = mask_ref.shape[-1]
    lane = lane_of((LANES, LANES))
    halves = []
    for t in range(8):
        value = jnp.zeros((LANES, LANES), f32)
        for field in range(3):
            item = msg_ref[:, 0, LANES * field : LANES * (field + 1)]
            value = jnp.where(lane // 16 == field, roll(item, 16 * (field - t), 1), value)
        halves.append(value)
    cos_r, sin_r = part_back(
        [jnp.concatenate(halves[2 * i : 2 * i + 2], axis=0) for i in range(4)]
    )
    parts = ([], [])
    for r in range(4):
        pair = (cos_r[r], sin_r[r])
        if r > 0:
            cos_turn, sin_turn = turn_of(turn_ref, r)
            pair = turn(*pair, cos_turn, -sin_turn)
        for i, value in enumerate(pair):
            high, low = split_f32(value)
            parts[i].append((high + roll(low, 64, 1)).astype(bf16))
    columns = jnp.concatenate([jnp.concatenate(part, axis=1) for part in parts], axis=0)
    found = dot_table(table_ref, columns)
    for r in range(4):
        block = found[:, LANES * r : LANES * (r + 1)]
        line_ref[pl.ds(r, 256, stride=4), :] = block + roll(block, 64, 1)
    field = line_ref[...].T
    pressure = field[0:16]
    east_back = roll(pressure, 1, 1) - pressure
    projected = (
        cot_ref[0, 0] - east_back,
        cot_ref[1, 0] - field[32:48],
        cot_ref[2, 0] - field[16:32],
    )
    wet = mask_ref[0].astype(f32)
    out_copies = []
    deltas = [value * wet for value in projected]
    blank = jnp.zeros((8, CHUNK), f32)
    bias2 = jnp.zeros((256, LANES), f32)
    for half in range(2):
        part = slice(8 * half, 8 * (half + 1))
        for start in range(0, width, CHUNK):
            col = slice(start, start + CHUNK)
            to = slice(half * width + start, half * width + start + CHUNK)
            delta = jnp.concatenate([value[part, col] for value in deltas] + [blank], axis=0)
            dh, dl = split_f32(delta)
            stack = jnp.concatenate([dh, dl, dh], axis=0).astype(bf16)
            dl_ref[:, to] = stack[0:64]
            second = second_ref[0:256, to].astype(f32) + second_ref[256:512, to].astype(f32)
            err2 = dot(wide_ref[0:256, 0:96], stack) * (1.0 - second * second)
            bias2 = bias2 + sum(err2[:, LANES * i : LANES * (i + 1)] for i in range(CHUNK // LANES))
            e2h, e2l = split(err2)
            e2h_ref[:, to] = e2h
            e2l_ref[:, to] = e2l
            first = first_ref[0:256, to].astype(f32) + first_ref[256:512, to].astype(f32)
            err1 = (
                dot(wide_ref[0:256, 128:384], e2h)
                + dot(wide_ref[0:256, 128:384], e2l)
                + dot(wide_ref[0:256, 384:640], e2h)
            )
            err1 = err1 * (1.0 - first * first)
            e1h, e1l = split(err1)
            e1h_ref[:, to] = e1h
            e1l_ref[:, to] = e1l
            out = (
                dot(wide_ref[256:288, 128:384], e1h)
                + dot(wide_ref[256:288, 128:384], e1l)
                + dot(wide_ref[256:288, 384:640], e1h)
            )
            for c in range(3):
                gvel_ref[c, 0, part, col] = projected[c][part, col] + out[8 * c : 8 * (c + 1)]
            gbuoy_ref[0, part, col] = out[24:32]
        out_copies += [
            start_copy(gvel_ref.at[:, :, part, :], gvel_hbm.at[:, :, part, :], out_sems, 2 * half),
            start_copy(gbuoy_ref.at[:, part, :], gbuoy_hbm.at[:, part, :], out_sems, 2 * half + 1),
        ]
    b2_ref[...] = bias2
    mid = (
        dot_nt(e2h_ref[...], first_ref[0:256])
        + dot_nt(e2h_ref[...], first_ref[256:512])
        + dot_nt(e2l_ref[...], first_ref[0:256])
    )
    both1 = dot_nt(first_ref[512:608], e1h_ref[...])
    rest1 = dot_nt(first_ref[512:608], e1l_ref[...])
    win = both1[0:32] + both1[32:64] + rest1[0:32]
    bin_ = both1[64:65] + rest1[64:65]
    both2 = dot_nt(dl_ref[...], second_ref[0:256])
    rest2 = dot_nt(dl_ref[...], second_ref[256:512])
    wout = both2[0:32] + both2[32:64] + rest2[0:32]

    def fold_rows(value):
        return jnp.sum(value.reshape(value.shape[0] // 8, 8, value.shape[1]), axis=1)

    to_unit = gather((256, LANES), 8)
    mid = exact(fold_rows(same_row(mid)), to_unit)
    small = [fold_rows(same_row(win)), fold_rows(same_row(wout)), bin_, jnp.zeros((7, 256), f32)]
    small = exact(jnp.concatenate(small, axis=0), to_unit)
    b2 = lax.dot_general(
        jnp.ones((8, LANES), f32),
        fold_rows(b2_ref[...]),
        (((1,), (1,)), ((), ())),
        precision=lax.Precision.HIGHEST,
        preferred_element_type=f32,
    )
    units = jnp.concatenate([mid[8 * i : 8 * (i + 1), 0:32] for i in range(4)], axis=1)
    rows = [units[i : i + 1] for i in range(8)]
    rows.append(jnp.concatenate([small[i : i + 1, 0:32] for i in range(4)], axis=1))
    rows.append(
        jnp.concatenate([small[i : i + 1, 0:32] for i in range(4, 7)] + [b2[0:1]], axis=1)
    )
    rows.append(small[8:9])
    for peer in range(32):
        for i, row in enumerate(rows):
            total_ref[peer, :, LANES * i : LANES * (i + 1)] = row
    for copy in out_copies:
        copy.wait()


def sum_slab(got_ref, out_ref):
    total = jnp.sum(got_ref[...], axis=0)
    for peer in range(16):
        out_ref[peer] = total


def sum_column(scale, got_ref, win_ref, bin_ref, wmid_ref, bmid_ref, wout_ref):
    total = jnp.sum(got_ref[...], axis=0) * scale
    rows = [total[:, LANES * i : LANES * (i + 1)] for i in range(11)]
    units = jnp.concatenate(rows[:8], axis=0)
    wmid_ref[...] = jnp.concatenate([units[:, 32 * i : 32 * (i + 1)] for i in range(4)], axis=0)
    win_ref[...] = jnp.concatenate([rows[8][:, 32 * i : 32 * (i + 1)] for i in range(4)], axis=0)
    wout_ref[...] = jnp.concatenate([rows[9][:, 32 * i : 32 * (i + 1)] for i in range(3)], axis=0)
    bmid_ref[...] = rows[9][:, 96:128]
    bin_ref[...] = rows[10][:, 0:32]


def shards(velocity, buoyancy, cell_mask, spacing, cotangent, w_in, b_in, w_mid, b_mid, w_out):
    levels, rows, width = buoyancy.shape
    depth = spacing.shape[0]
    span_y = rows * 64
    table = dft_table(256, 1024)
    table_y = table[:, (np.arange(256) % 64) * 4 + np.arange(256) // 64]
    x_table, y_table, x_back, y_back = (
        jnp.asarray(two_parts(item)) for item in (table, table_y, table.T, table_y.T)
    )
    eigen = eigenvalue(width)
    lanes = np.arange(LANES)
    ey = eigen.reshape(4, 256)[lanes % 16 // 4].T.astype(np.float32)
    ex = eigen[np.arange(128)[:, None] + 128 * (lanes[None, :] // 16)].astype(np.float32)
    turns = twiddles(256, 1024)
    fixed = jnp.asarray(np.concatenate([turns, ey, ex], axis=0))
    turns = jnp.asarray(turns)
    cells = rows * width // 8
    dma = pltpu.SemaphoreType.DMA
    type_of = jax.ShapeDtypeStruct
    table = pltpu.VMEM((1024, 256), bf16)
    back_table = pltpu.VMEM((512, 512), bf16)
    turn_held = pltpu.VMEM((640, LANES), f32)
    first_held = pltpu.VMEM((608, cells), bf16)
    second_held = pltpu.VMEM((512, cells), bf16)
    wide = pltpu.VMEM((256, cells), bf16)
    wide_held = pltpu.VMEM((288, 640), bf16)
    mark_type = type_of((8, LANES), f32)
    table_flops = 4 * 512 * 256 * 512
    msg_type = type_of((128, 1, 3 * LANES), f32)
    msg, mark = call(
        forward_x,
        (msg_type, mark_type),
        (cotangent, x_table, turns),
        hbm=(0, 1, 2),
        scratch=(
            table,
            pltpu.VMEM((256, LANES), f32),
            pltpu.VMEM(cotangent.shape, f32),
            pltpu.VMEM((1024, LANES), f32),
            dma((3,)),
        ),
        flops=table_flops,
        name="forward_x",
    )
    msg = lax.all_to_all(msg, PLANE, 0, 0)

    first, second, weights, turns, mark = call(
        closure_forward,
        (
            pltpu.HBM((608, cells), bf16),
            pltpu.HBM((512, cells), bf16),
            pltpu.HBM((288, 640), bf16),
            pltpu.HBM((640, LANES), f32),
            mark_type,
        ),
        (velocity, buoyancy, w_in.T, b_in[None], w_mid, b_mid[None], w_out, fixed, mark, spacing),
        hbm=(0, 1, 7),
        smem=(9,),
        hbm_out=range(4),
        scratch=(
            first_held,
            second_held,
            wide_held,
            turn_held,
            pltpu.VMEM(velocity.shape, f32),
            pltpu.VMEM(buoyancy.shape, f32),
            dma((3,)),
            dma((6,)),
        ),
        flops=2 * 256 * 256 * cells * 4,
        name="closure_forward",
    )
    gathered, turns, second, x_back = call(
        forward_y,
        (type_of((4, 256, LANES), f32), turn_held, second_held, back_table),
        (msg, y_table, turns, second, x_back, mark),
        hbm=range(1, 5),
        scratch=(table, dma((4,))),
        flops=table_flops,
        name="forward_y",
    )
    gathered = lax.all_to_all(gathered, "x", 0, 0)
    msg, cotangent, cell_mask, first, weights = call(
        solve_back,
        (
            msg_type,
            pltpu.VMEM(cotangent.shape, f32),
            pltpu.VMEM(cell_mask.shape, jnp.int32),
            first_held,
            wide_held,
        ),
        (gathered, turns, y_back, cotangent, cell_mask, first, weights),
        hbm=range(2, 7),
        scratch=(back_table, dma((5,))),
        flops=table_flops,
        name="solve_back",
    )
    msg = lax.all_to_all(msg, PLANE, 0, 0)
    totals, grad_velocity, grad_buoyancy = call(
        closure_back,
        (
            type_of((32, 1, 11 * LANES), f32),
            pltpu.HBM(cotangent.shape, f32),
            pltpu.HBM(buoyancy.shape, f32),
        ),
        (msg, turns, second, x_back, cotangent, cell_mask, first, weights),
        hbm_out=(1, 2),
        scratch=(
            pltpu.VMEM((1024, LANES), f32),
            wide,
            wide,
            wide,
            wide,
            pltpu.VMEM((64, cells), bf16),
            pltpu.VMEM((256, LANES), f32),
            pltpu.VMEM(cotangent.shape, f32),
            pltpu.VMEM(buoyancy.shape, f32),
            dma((4,)),
        ),
        flops=table_flops + 2 * 256 * 256 * cells * 10,
        name="closure_back",
    )
    totals = lax.all_to_all(totals, SLAB, 0, 0)
    (totals,) = call(sum_slab, (type_of((16, 1, 11 * LANES), f32),), (totals,), name="sum_slab")
    totals = lax.all_to_all(totals, COLUMN, 0, 0)
    scale = 1.0 / math.sqrt(width * span_y * depth)
    grad_in, grad_b_in, grad_mid, grad_b_mid, grad_out = call(
        functools.partial(sum_column, scale),
        (
            type_of((4, 32), f32),
            type_of((1, 32), f32),
            type_of((32, 32), f32),
            type_of((1, 32), f32),
            type_of((3, 32), f32),
        ),
        (totals,),
        name="sum_column",
    )
    return (
        grad_velocity,
        grad_buoyancy,
        grad_in.T,
        grad_b_in[0],
        grad_mid,
        grad_b_mid[0],
        grad_out,
    )


def solution(mesh):
    fine = Mesh(
        mesh.devices.reshape([size for _, size in FINE]), tuple(name for name, _ in FINE)
    )
    field = P(None, NARROW, WIDE, None)
    cell = P(NARROW, WIDE, None)
    in_specs = (field, cell, cell, P(), field, P(), P(), P(), P(), P())
    out_specs = (field, cell, P(), P(), P(), P(), P())
    return jax.shard_map(shards, mesh=fine, in_specs=in_specs, out_specs=out_specs, check_vma=False)
```

```python
import functools
import math

import jax
import jax.numpy as jnp
import ml_dtypes
import numpy as np
from jax import lax
from jax.experimental import pallas as pl
from jax.experimental.pallas import tpu as pltpu
from jax.sharding import Mesh
from jax.sharding import PartitionSpec as P

free_surface = 0.05
f32 = jnp.float32
bf16 = jnp.bfloat16
LANES = 128
LEVELS = 8
VMEM_LIMIT = 24 * 1024 * 1024

FINE = (("y", 4), ("zl", 8), ("c", 2), ("zh", 2), ("x", 4))
WIDE = ("y", "zl", "c")
NARROW = ("zh", "x")
PLANE = ("zh", "y", "zl", "c")
SLAB = ("y", "x", "c")
COLUMN = ("zl", "zh")


def dft_table(count, length):
    indices = np.arange(count)
    angle = 2.0 * np.pi / count * (indices[:, None] * indices[None, :] % count)
    return np.concatenate([np.cos(angle), np.sin(angle)], axis=0) * np.sqrt(2.0 / length)


def twiddles(count, length):
    angle = 2.0 * np.pi / length * np.arange(count)[:, None] * np.arange(4)[None, :]
    held = np.zeros((count, LANES))
    held[:, 0:8:2] = np.cos(angle)
    held[:, 1:8:2] = np.sin(angle)
    return held.astype(np.float32)


def wavenumbers(length):
    half = np.arange(length // 2)
    return np.concatenate([half, np.where(half == 0, length // 2, half)])


def two_parts(table):
    high = table.astype(np.float32).astype(ml_dtypes.bfloat16)
    low = (table - high.astype(np.float64)).astype(np.float32).astype(ml_dtypes.bfloat16)
    return np.concatenate([high, low], axis=0)


def eigenvalue(length):
    return -4.0 * np.sin(np.pi / length * wavenumbers(length)) ** 2


def split(value):
    high = value.astype(bf16)
    low = (value - high.astype(f32)).astype(bf16)
    return high, low


def split_f32(value):
    high = value.astype(bf16).astype(f32)
    return high, value - high


def dot(a, b):
    return jnp.dot(a, b, preferred_element_type=f32)


def dot_table(table_ref, b):
    rows = table_ref.shape[0] // 2
    return dot(table_ref[0:rows], b) + dot(table_ref[rows : 2 * rows], b)


def dot_nt(a, b):
    return lax.dot_general(a, b, (((1,), (1,)), ((), ())), preferred_element_type=f32)


def roll(value, shift, axis):
    size = value.shape[axis]
    shift = shift % size
    return value if shift == 0 else pltpu.roll(value, shift, axis)


def lane_of(shape):
    return lax.broadcasted_iota(jnp.int32, shape, len(shape) - 1)


def start_copy(source, target, sems, index):
    copy = pltpu.make_async_copy(source, target, sems.at[index])
    copy.start()
    return copy


def call(kernel, out_shape, args, smem=(), hbm=(), hbm_out=(), scratch=(), flops=0, name=None):
    def space(index, held):
        return pl.BlockSpec(memory_space=held.get(index, pltpu.VMEM))

    held = {i: pltpu.SMEM for i in smem} | {i: pl.ANY for i in hbm}
    args = [
        pltpu.with_memory_space_constraint(a, pltpu.HBM) if i in hbm else a
        for i, a in enumerate(args)
    ]
    moved = sum(int(np.prod(a.shape)) * a.dtype.itemsize for a in args)
    return pl.pallas_call(
        kernel,
        out_shape=out_shape,
        in_specs=[space(i, held) for i in range(len(args))],
        out_specs=[space(i, {o: pl.ANY for o in hbm_out}) for i in range(len(out_shape))],
        scratch_shapes=list(scratch),
        compiler_params=pltpu.CompilerParams(vmem_limit_bytes=VMEM_LIMIT),
        cost_estimate=pl.CostEstimate(flops=flops, bytes_accessed=moved, transcendentals=0),
        name=name,
    )(*args)


def first_row(shape):
    return lax.broadcasted_iota(jnp.int32, shape, 0) == 0


def join(cos_r, sin_r):
    even_c, even_s = cos_r[0] + cos_r[2], sin_r[0] + sin_r[2]
    odd_c, odd_s = cos_r[1] + cos_r[3], sin_r[1] + sin_r[3]
    top = first_row(even_c.shape)
    ends = jnp.where(top, math.sqrt(0.5), 1.0)
    return (
        (even_c + odd_c) * ends,
        cos_r[0] - cos_r[2] - (sin_r[1] - sin_r[3]),
        jnp.where(top, even_c - odd_c, even_s + odd_s) * ends,
        sin_r[0] - sin_r[2] + (cos_r[1] - cos_r[3]),
    )


def part_back(blocks):
    top = first_row(blocks[0].shape)
    ends = jnp.where(top, math.sqrt(0.5), 1.0)
    low_c, high_c, low_s, high_s = blocks
    low_c, low_s = low_c * ends, low_s * ends
    last = jnp.where(top, low_s, 0.0)
    low_s = jnp.where(top, 0.0, low_s)
    even, odd = low_c + last, low_c - last
    return (
        (even + high_c, odd + high_s, even - high_c, odd - high_s),
        (low_s + high_s, low_s - high_c, low_s - high_s, low_s + high_c),
    )


def turn(cos_part, sin_part, cos_turn, sin_turn):
    return cos_part * cos_turn - sin_part * sin_turn, sin_part * cos_turn + cos_part * sin_turn


def turn_of(turn_ref, remainder):
    rows, shape = slice(0, 256), (256, LANES)
    return (
        jnp.broadcast_to(turn_ref[rows, 2 * remainder : 2 * remainder + 1], shape),
        jnp.broadcast_to(turn_ref[rows, 2 * remainder + 1 : 2 * remainder + 2], shape),
    )


def forward_x(cot_hbm, table_hbm, turn_hbm, out_ref, mark_ref,
              table_ref, turn_ref, cot_ref, line_ref, sems):
    first = start_copy(cot_hbm, cot_ref, sems, 0)
    copies = [
        start_copy(table_hbm, table_ref, sems, 1),
        start_copy(turn_hbm, turn_ref, sems, 2),
    ]
    first.wait()
    east, north, up = cot_ref[0, 0], cot_ref[1, 0], cot_ref[2, 0]
    rows, width = east.shape
    east = east - roll(east, -1, 1)
    high, low = split_f32(jnp.concatenate([east, north, up], axis=0))
    none = jnp.zeros((rows, width), f32)
    line_ref[...] = jnp.concatenate([high, none, low, none], axis=0).T
    lines = jnp.concatenate(
        [line_ref[pl.ds(r, 256, stride=4), :].astype(bf16) for r in range(4)], axis=1
    )
    for copy in copies:
        copy.wait()
    got = dot_table(table_ref, lines)
    cos_r, sin_r = [], []
    for r in range(4):
        cos_part = got[0:256, LANES * r : LANES * (r + 1)]
        sin_part = got[256:512, LANES * r : LANES * (r + 1)]
        if r > 0:
            cos_part, sin_part = turn(cos_part, sin_part, *turn_of(turn_ref, r))
        cos_r.append(cos_part)
        sin_r.append(sin_part)
    blocks = [block + roll(block, 64, 1) for block in join(cos_r, sin_r)]
    lane = lane_of((LANES, LANES))
    for field in range(3):
        packed = jnp.zeros((LANES, LANES), f32)
        for t in range(8):
            block = blocks[t // 2][LANES * (t % 2) : LANES * (t % 2 + 1)]
            packed = jnp.where(lane // 16 == t, roll(block, 16 * (t - field), 1), packed)
        out_ref[pl.ds(field, LANES, stride=3), :] = packed
    mark_ref[...] = jnp.zeros(mark_ref.shape, f32)


def pair_turns(turn_ref, pair, within):
    one, two = turn_of(turn_ref, 2 * pair), turn_of(turn_ref, 2 * pair + 1)
    return tuple(jnp.where(within < 8, a, b) for a, b in zip(one, two))


def forward_y(msg_ref, table_hbm, turn_hbm, second_hbm, back_hbm, mark_ref,
              out_ref, turn_ref, second_ref, back_ref, table_ref, sems):
    copies = [
        start_copy(table_hbm, table_ref, sems, 0),
        start_copy(turn_hbm, turn_ref, sems, 1),
    ]
    later_copies = [
        start_copy(back_hbm, back_ref, sems, 2),
        start_copy(second_hbm, second_ref, sems, 3),
    ]
    within = lane_of((64, LANES)) % 16
    highs = []
    lows = []
    for half in range(2):
        east, north, up = (
            msg_ref[pl.ds(192 * half + field, 64, stride=3), :] for field in range(3)
        )
        after = jnp.where(
            within < 15, roll(north, -1, 1), roll(roll(north, -1, 0), 15, 1)
        )
        for value in (east + north - after, up):
            high, low = split_f32(value)
            highs.append(high)
            lows.append(low)
    shifted = [roll(value, c, 1) for c, value in enumerate(highs + lows)]

    def line_of(j, to):
        line = shifted[0]
        for c in range(1, 8):
            line = jnp.where(within == (c + j) % 16, shifted[c], line)
        return roll(line, to - j, 1)

    lines = []
    for pair in range(2):
        rows = []
        for step in range(4):
            j = 4 * step + 2 * pair
            rows.append(jnp.where(within < 8, line_of(j, 0), line_of(j + 1, 8)).astype(bf16))
        lines.append(jnp.concatenate(rows, axis=0))
    lines = jnp.concatenate(lines, axis=1)
    for copy in copies:
        copy.wait()
    got = dot_table(table_ref, lines)
    within = lane_of((256, LANES)) % 16
    turned = [
        turn(
            got[0:256, LANES * pair : LANES * (pair + 1)],
            got[256:512, LANES * pair : LANES * (pair + 1)],
            *pair_turns(turn_ref, pair, within),
        )
        for pair in range(2)
    ]
    cos_r = [turned[0][0], roll(turned[0][0], -8, 1), turned[1][0], roll(turned[1][0], -8, 1)]
    sin_r = [turned[0][1], roll(turned[0][1], -8, 1), turned[1][1], roll(turned[1][1], -8, 1)]
    packed = jnp.zeros((256, LANES), f32)
    for g, block in enumerate(join(cos_r, sin_r)):
        block = block + roll(block, -4, 1)
        packed = jnp.where(within // 4 == g, roll(block, 4 * g, 1), packed)
    for peer in range(4):
        out_ref[peer] = packed
    for copy in later_copies:
        copy.wait()


def vertical(spacing):
    one = jnp.ones((1, LANES), f32)
    none = jnp.zeros((1, LANES), f32)
    spacing = [one * spacing[k] for k in range(LEVELS)]
    inv_dz = [1.0 / value for value in spacing]
    face = [2.0 / (spacing[k] + spacing[k + 1]) for k in range(LEVELS - 1)] + [none]
    lower = [none] + [inv_dz[k] * face[k - 1] for k in range(1, LEVELS)]
    upper = [inv_dz[k] * face[k] for k in range(LEVELS)]
    base = [-(lower[k] + upper[k]) for k in range(LEVELS)]
    base[-1] = base[-1] - free_surface * inv_dz[-1]
    sub = [none] + upper[:-1]
    sup = lower[1:] + [none]
    keep = [one] * (LEVELS - 1) + [none]
    return inv_dz, face, sub, base, sup, keep


def solve_back(got_ref, turn_ref, table_hbm, cot_hbm, mask_hbm, first_hbm, wide_hbm,
               out_ref, cot_ref, mask_ref, first_ref, wide_ref, table_ref, sems):
    copies = [start_copy(table_hbm, table_ref, sems, 0)]
    later_copies = [
        start_copy(cot_hbm, cot_ref, sems, 1),
        start_copy(mask_hbm, mask_ref, sems, 2),
        start_copy(wide_hbm, wide_ref, sems, 3),
        start_copy(first_hbm, first_ref, sems, 4),
    ]
    at = lax.axis_index("x")
    rows = got_ref.shape[1]
    lam = turn_ref[256 : 256 + rows]
    lane = lane_of((rows, LANES))
    inv_dz, face, sub, base, sup, keep = (
        [turn_ref[512 + 8 * i + k : 513 + 8 * i + k] for k in range(LEVELS)]
        for i in range(6)
    )
    ratios = []
    values = []
    below = None
    for k in range(LEVELS):
        packed = got_ref[k % 4]
        half = k // 4
        flux = roll(packed, -(2 * half + 1), 1) * face[k]
        right = roll(packed, -2 * half, 1) - flux
        if k > 0:
            right = right + below
        below = flux
        diagonal = lam + base[k]
        if k > 0:
            diagonal = diagonal - sub[k] * ratios[-1]
            right = right - sub[k] * values[-1]
        inverse = 1.0 / diagonal
        ratios.append(sup[k] * inverse)
        values.append(right * inverse)
    result = [None] * LEVELS
    result[-1] = values[-1]
    for k in range(LEVELS - 2, -1, -1):
        result[k] = values[k] - ratios[k] * result[k + 1]
    scaled = [result[k] * inv_dz[k] for k in range(LEVELS)] + [jnp.zeros_like(lam)]
    change = [(scaled[k] - scaled[k + 1]) * keep[k] for k in range(LEVELS)]

    def own(items, half):
        value = items[4 * half]
        for x in range(1, 4):
            value = jnp.where(at == x, items[4 * half + x], value)
        return value

    column = lane % 4
    both = own(result, 0)
    both = jnp.where(column == 1, roll(own(change, 0), 1, 1), both)
    both = jnp.where(column == 2, roll(own(result, 1), 2, 1), both)
    both = jnp.where(column == 3, roll(own(change, 1), 3, 1), both)
    for copy in copies:
        copy.wait()
    within = lane % 16
    blocks = []
    for g in range(4):
        block = roll(both, -4 * g, 1)
        blocks.append(jnp.where(within < 8, block, roll(block, 8, 1)))
    cos_r, sin_r = part_back(blocks)
    parts = ([], [])
    for pair in range(2):
        cos_part = jnp.where(within < 8, cos_r[2 * pair], cos_r[2 * pair + 1])
        sin_part = jnp.where(within < 8, sin_r[2 * pair], sin_r[2 * pair + 1])
        cos_turn, sin_turn = pair_turns(turn_ref, pair, within)
        for i, value in enumerate(turn(cos_part, sin_part, cos_turn, -sin_turn)):
            high, low = split_f32(jnp.where(within % 8 < 4, value, 0.0))
            parts[i].append((high + roll(low, 4, 1)).astype(bf16))
    columns = jnp.concatenate([jnp.concatenate(part, axis=1) for part in parts], axis=0)
    got = dot_table(table_ref, columns)
    within = lane_of((64, LANES)) % 16
    packed = [jnp.zeros((64, LANES), f32)] * 4
    for pair in range(2):
        found = got[:, LANES * pair : LANES * (pair + 1)]
        found = found + roll(found, -4, 1)
        for step in range(4):
            for one in range(2):
                j = 4 * step + 2 * pair + one
                moved = roll(found[64 * step : 64 * (step + 1)], j - 8 * one, 1)
                for c in range(4):
                    packed[c] = jnp.where(within == (j + c) % 16, moved, packed[c])
    for half in range(2):
        pressure = roll(packed[2 * half], -2 * half, 1)
        change_up = roll(packed[2 * half + 1], -(2 * half + 1), 1)
        before = jnp.where(
            within > 0, roll(pressure, 1, 1), roll(roll(pressure, 1, 0), -15, 1)
        )
        for field, value in enumerate((pressure, change_up, before - pressure)):
            out_ref[pl.ds(192 * half + field, 64, stride=3), :] = value
    for copy in later_copies:
        copy.wait()


CHUNK = 1024


def unit_rows(shape, axis):
    return lax.broadcasted_iota(jnp.int32, shape, axis) % 8


def same_row(value):
    shape = value.shape
    return jnp.where(unit_rows(shape, 0) == unit_rows(shape, 1), value, 0.0)


def gather(shape, step):
    to = lax.broadcasted_iota(jnp.int32, shape, 1)
    return (lax.broadcasted_iota(jnp.int32, shape, 0) // step == to).astype(f32)


def exact(a, b):
    return jnp.dot(a, b, precision=lax.Precision.HIGHEST, preferred_element_type=f32)


def spread(weight, columns):
    tall, wide = weight.shape
    step = (
        lax.broadcasted_iota(jnp.int32, (wide, columns), 1) // 8
        == lax.broadcasted_iota(jnp.int32, (wide, columns), 0)
    ).astype(f32)
    value = exact(weight, step)
    value = jnp.broadcast_to(value[:, None, :], (tall, 8, columns)).reshape(8 * tall, columns)
    return same_row(value)


def closure_forward(win_hbm, bin_hbm, wmid_hbm, bmid_hbm, wout_hbm, spacing_hbm,
                    vel_hbm, buoy_hbm, fixed_hbm, mark_ref,
                    first_hbm, second_hbm, wide_hbm, turn_hbm, done_ref,
                    win_ref, bin_ref, wmid_ref, bmid_ref, wout_ref, spacing_ref,
                    vel_ref, buoy_ref, turn_ref, first_ref, second_ref, wide_ref, sems, out_sems):
    sources = (win_hbm, bin_hbm, wmid_hbm, bmid_hbm, wout_hbm, spacing_hbm)
    sources += (vel_hbm, buoy_hbm, fixed_hbm)
    targets = (win_ref, bin_ref, wmid_ref, bmid_ref, wout_ref, spacing_ref)
    targets += (vel_ref, buoy_ref, turn_ref)
    copies = [start_copy(*pair, sems, i) for i, pair in enumerate(zip(sources, targets))]
    for copy in copies[:6]:
        copy.wait()
    win_t = win_ref[...]
    wmid = wmid_ref[...]
    wout_h, wout_l = split_f32(spread(wout_ref[...].T, 32))
    wide_ref[0:256, 0:96] = jnp.concatenate([wout_h, wout_h, wout_l], axis=1).astype(bf16)
    wide_ref[0:256, 96:128] = jnp.zeros((256, 32), bf16)
    wide_ref[0:256, 128:384], wide_ref[0:256, 384:640] = split(spread(wmid.T, 256))
    wide_ref[256:288, 0:128] = jnp.zeros((32, 128), bf16)
    wide_ref[256:288, 128:384], wide_ref[256:288, 384:640] = split(spread(win_t, 256))
    win_h, win_l = split_f32(spread(win_t.T, 32))
    win_cat = jnp.concatenate([win_h, win_h, win_l], axis=1).astype(bf16)
    wmh, wml = split(spread(wmid, 256))

    def tall(row):
        column = row.T
        return jnp.broadcast_to(column[:, None, :], (32, 8, 1)).reshape(256, 1)

    b_in, b_mid = tall(bin_ref[...]), tall(bmid_ref[...])
    for copy in copies[6:]:
        copy.wait()
    own = turn_ref[pl.ds(512 + lax.axis_index(PLANE), 1), :]
    turn_ref[256:512] = turn_ref[256:512] + own
    for i, rows in enumerate(vertical([spacing_ref[:, k : k + 1] for k in range(LEVELS)])):
        turn_ref[512 + 8 * i : 520 + 8 * i] = jnp.concatenate(rows, axis=0)
    copies = [
        start_copy(wide_ref, wide_hbm, out_sems, 0),
        start_copy(turn_ref, turn_hbm, out_sems, 1),
    ]
    width = buoy_ref.shape[-1]
    for half in range(2):
        part = slice(8 * half, 8 * (half + 1))
        for start in range(0, width, CHUNK):
            col = slice(start, start + CHUNK)
            to = slice(half * width + start, half * width + start + CHUNK)
            feats = jnp.concatenate(
                [vel_ref[c, 0, part, col] for c in range(3)] + [buoy_ref[0, part, col]], axis=0
            )
            high, low = split_f32(feats)
            stack = jnp.concatenate([high, low, high], axis=0).astype(bf16)
            first_ref[512:608, to] = jnp.concatenate(
                [high, low, jnp.ones((32, CHUNK), f32)], axis=0
            ).astype(bf16)
            first = jnp.tanh(dot(win_cat, stack) + b_in)
            fh, fl = split(first)
            first_ref[0:256, to] = fh
            first_ref[256:512, to] = fl
            second = dot(wmh, fh) + dot(wmh, fl) + dot(wml, fh)
            second = jnp.tanh(second + b_mid)
            sh, sl = split(second)
            second_ref[0:256, to] = sh
            second_ref[256:512, to] = sl
        whole = slice(half * width, (half + 1) * width)
        for i, (held, target) in enumerate(((first_ref, first_hbm), (second_ref, second_hbm))):
            copies.append(
                start_copy(held.at[:, whole], target.at[:, whole], out_sems, 2 + 2 * half + i)
            )
    done_ref[...] = jnp.zeros(done_ref.shape, f32)
    for copy in copies:
        copy.wait()


def closure_back(msg_ref, turn_ref, second_ref, table_ref, cot_ref, mask_ref, first_ref,
                 wide_ref, total_ref, gvel_hbm, gbuoy_hbm,
                 line_ref, e1h_ref, e1l_ref, e2h_ref, e2l_ref, dl_ref, b2_ref,
                 gvel_ref, gbuoy_ref, out_sems):
    width = mask_ref.shape[-1]
    lane = lane_of((LANES, LANES))
    halves = []
    items = [msg_ref[pl.ds(field, LANES, stride=3), :] for field in range(3)]
    for t in range(8):
        value = jnp.zeros((LANES, LANES), f32)
        for field, item in enumerate(items):
            value = jnp.where(lane // 16 == field, roll(item, 16 * (field - t), 1), value)
        halves.append(value)
    cos_r, sin_r = part_back(
        [jnp.concatenate(halves[2 * i : 2 * i + 2], axis=0) for i in range(4)]
    )
    parts = ([], [])
    for r in range(4):
        pair = (cos_r[r], sin_r[r])
        if r > 0:
            cos_turn, sin_turn = turn_of(turn_ref, r)
            pair = turn(*pair, cos_turn, -sin_turn)
        for i, value in enumerate(pair):
            high, low = split_f32(value)
            parts[i].append((high + roll(low, 64, 1)).astype(bf16))
    columns = jnp.concatenate([jnp.concatenate(part, axis=1) for part in parts], axis=0)
    found = dot_table(table_ref, columns)
    for r in range(4):
        block = found[:, LANES * r : LANES * (r + 1)]
        line_ref[pl.ds(r, 256, stride=4), :] = block + roll(block, 64, 1)
    field = line_ref[...].T
    pressure = field[0:16]
    east_back = roll(pressure, 1, 1) - pressure
    projected = (
        cot_ref[0, 0] - east_back,
        cot_ref[1, 0] - field[32:48],
        cot_ref[2, 0] - field[16:32],
    )
    wet = mask_ref[0].astype(f32)
    out_copies = []
    deltas = [value * wet for value in projected]
    blank = jnp.zeros((8, CHUNK), f32)
    bias2 = jnp.zeros((256, LANES), f32)
    for half in range(2):
        part = slice(8 * half, 8 * (half + 1))
        for start in range(0, width, CHUNK):
            col = slice(start, start + CHUNK)
            to = slice(half * width + start, half * width + start + CHUNK)
            delta = jnp.concatenate([value[part, col] for value in deltas] + [blank], axis=0)
            dh, dl = split_f32(delta)
            stack = jnp.concatenate([dh, dl, dh], axis=0).astype(bf16)
            dl_ref[:, to] = stack[0:64]
            second = second_ref[0:256, to].astype(f32) + second_ref[256:512, to].astype(f32)
            err2 = dot(wide_ref[0:256, 0:96], stack) * (1.0 - second * second)
            bias2 = bias2 + sum(err2[:, LANES * i : LANES * (i + 1)] for i in range(CHUNK // LANES))
            e2h, e2l = split(err2)
            e2h_ref[:, to] = e2h
            e2l_ref[:, to] = e2l
            first = first_ref[0:256, to].astype(f32) + first_ref[256:512, to].astype(f32)
            err1 = (
                dot(wide_ref[0:256, 128:384], e2h)
                + dot(wide_ref[0:256, 128:384], e2l)
                + dot(wide_ref[0:256, 384:640], e2h)
            )
            err1 = err1 * (1.0 - first * first)
            e1h, e1l = split(err1)
            e1h_ref[:, to] = e1h
            e1l_ref[:, to] = e1l
            out = (
                dot(wide_ref[256:288, 128:384], e1h)
                + dot(wide_ref[256:288, 128:384], e1l)
                + dot(wide_ref[256:288, 384:640], e1h)
            )
            for c in range(3):
                gvel_ref[c, 0, part, col] = projected[c][part, col] + out[8 * c : 8 * (c + 1)]
            gbuoy_ref[0, part, col] = out[24:32]
        out_copies += [
            start_copy(gvel_ref.at[:, :, part, :], gvel_hbm.at[:, :, part, :], out_sems, 2 * half),
            start_copy(gbuoy_ref.at[:, part, :], gbuoy_hbm.at[:, part, :], out_sems, 2 * half + 1),
        ]
    b2_ref[...] = bias2
    mid = (
        dot_nt(e2h_ref[...], first_ref[0:256])
        + dot_nt(e2h_ref[...], first_ref[256:512])
        + dot_nt(e2l_ref[...], first_ref[0:256])
    )
    both1 = dot_nt(first_ref[512:608], e1h_ref[...])
    rest1 = dot_nt(first_ref[512:608], e1l_ref[...])
    win = both1[0:32] + both1[32:64] + rest1[0:32]
    bin_ = both1[64:65] + rest1[64:65]
    both2 = dot_nt(dl_ref[...], second_ref[0:256])
    rest2 = dot_nt(dl_ref[...], second_ref[256:512])
    wout = both2[0:32] + both2[32:64] + rest2[0:32]

    def fold_rows(value):
        return jnp.sum(value.reshape(value.shape[0] // 8, 8, value.shape[1]), axis=1)

    to_unit = gather((256, LANES), 8)
    mid = exact(fold_rows(same_row(mid)), to_unit)
    small = [fold_rows(same_row(win)), fold_rows(same_row(wout)), bin_, jnp.zeros((7, 256), f32)]
    small = exact(jnp.concatenate(small, axis=0), to_unit)
    b2 = lax.dot_general(
        jnp.ones((8, LANES), f32),
        fold_rows(b2_ref[...]),
        (((1,), (1,)), ((), ())),
        precision=lax.Precision.HIGHEST,
        preferred_element_type=f32,
    )
    units = jnp.concatenate([mid[8 * i : 8 * (i + 1), 0:32] for i in range(4)], axis=1)
    rows = [units[i : i + 1] for i in range(8)]
    rows.append(jnp.concatenate([small[i : i + 1, 0:32] for i in range(4)], axis=1))
    rows.append(
        jnp.concatenate([small[i : i + 1, 0:32] for i in range(4, 7)] + [b2[0:1]], axis=1)
    )
    rows.append(small[8:9])
    rows = jnp.concatenate(rows, axis=0)
    for peer in range(32):
        total_ref[11 * peer : 11 * (peer + 1), :] = rows
    for copy in out_copies:
        copy.wait()


def sum_rows(got_ref):
    return [
        jnp.sum(got_ref[pl.ds(i, got_ref.shape[0] // 11, stride=11), :], axis=0, keepdims=True)
        for i in range(11)
    ]


def sum_slab(got_ref, out_ref):
    total = jnp.concatenate(sum_rows(got_ref), axis=0)
    for peer in range(16):
        out_ref[11 * peer : 11 * (peer + 1), :] = total


def sum_column(scale, got_ref, win_ref, bin_ref, wmid_ref, bmid_ref, wout_ref):
    rows = [row * scale for row in sum_rows(got_ref)]
    units = jnp.concatenate(rows[:8], axis=0)
    wmid_ref[...] = jnp.concatenate([units[:, 32 * i : 32 * (i + 1)] for i in range(4)], axis=0)
    win_ref[...] = jnp.concatenate([rows[8][:, 32 * i : 32 * (i + 1)] for i in range(4)], axis=0)
    wout_ref[...] = jnp.concatenate([rows[9][:, 32 * i : 32 * (i + 1)] for i in range(3)], axis=0)
    bmid_ref[...] = rows[9][:, 96:128]
    bin_ref[...] = rows[10][:, 0:32]


def trade(rows, peers, axes):
    size = rows.shape[0] // peers * LANES
    got = lax.all_to_all(rows.reshape(peers, 1, size), axes, 0, 0)
    return got.reshape(rows.shape)


def shards(velocity, buoyancy, cell_mask, spacing, cotangent, w_in, b_in, w_mid, b_mid, w_out):
    levels, rows, width = buoyancy.shape
    depth = spacing.shape[0]
    span_y = rows * 64
    table = dft_table(256, 1024)
    table_y = table[:, (np.arange(256) % 64) * 4 + np.arange(256) // 64]
    x_table, y_table, x_back, y_back = (
        jnp.asarray(two_parts(item)) for item in (table, table_y, table.T, table_y.T)
    )
    eigen = eigenvalue(width)
    lanes = np.arange(LANES)
    ey = eigen.reshape(4, 256)[lanes % 16 // 4].T.astype(np.float32)
    ex = eigen[np.arange(128)[:, None] + 128 * (lanes[None, :] // 16)].astype(np.float32)
    turns = twiddles(256, 1024)
    fixed = jnp.asarray(np.concatenate([turns, ey, ex], axis=0))
    turns = jnp.asarray(turns)
    cells = rows * width // 8
    dma = pltpu.SemaphoreType.DMA
    type_of = jax.ShapeDtypeStruct
    table = pltpu.VMEM((1024, 256), bf16)
    back_table = pltpu.VMEM((512, 512), bf16)
    turn_held = pltpu.VMEM((640, LANES), f32)
    first_held = pltpu.VMEM((608, cells), bf16)
    second_held = pltpu.VMEM((512, cells), bf16)
    wide = pltpu.VMEM((256, cells), bf16)
    wide_held = pltpu.VMEM((288, 640), bf16)
    mark_type = type_of((8, LANES), f32)
    table_flops = 4 * 512 * 256 * 512
    msg_type = type_of((128 * 3, LANES), f32)
    msg, mark = call(
        forward_x,
        (msg_type, mark_type),
        (cotangent, x_table, turns),
        hbm=(0, 1, 2),
        scratch=(
            table,
            pltpu.VMEM((256, LANES), f32),
            pltpu.VMEM(cotangent.shape, f32),
            pltpu.VMEM((1024, LANES), f32),
            dma((3,)),
        ),
        flops=table_flops,
        name="forward_x",
    )
    msg = trade(msg, 128, PLANE)

    first, second, weights, turns, mark = call(
        closure_forward,
        (
            pltpu.HBM((608, cells), bf16),
            pltpu.HBM((512, cells), bf16),
            pltpu.HBM((288, 640), bf16),
            pltpu.HBM((640, LANES), f32),
            mark_type,
        ),
        (w_in.T, b_in[None], w_mid, b_mid[None], w_out, spacing[None])
        + (velocity, buoyancy, fixed, mark),
        hbm=range(9),
        hbm_out=range(4),
        scratch=(
            pltpu.VMEM((4, 32), f32),
            pltpu.VMEM((1, 32), f32),
            pltpu.VMEM((32, 32), f32),
            pltpu.VMEM((1, 32), f32),
            pltpu.VMEM((3, 32), f32),
            pltpu.VMEM((1, LEVELS), f32),
            pltpu.VMEM(velocity.shape, f32),
            pltpu.VMEM(buoyancy.shape, f32),
            turn_held,
            first_held,
            second_held,
            wide_held,
            dma((9,)),
            dma((6,)),
        ),
        flops=2 * 256 * 256 * cells * 4,
        name="closure_forward",
    )
    gathered, turns, second, x_back = call(
        forward_y,
        (type_of((4, 256, LANES), f32), turn_held, second_held, back_table),
        (msg, y_table, turns, second, x_back, mark),
        hbm=range(1, 5),
        scratch=(table, dma((4,))),
        flops=table_flops,
        name="forward_y",
    )
    gathered = lax.all_to_all(gathered, "x", 0, 0)
    msg, cotangent, cell_mask, first, weights = call(
        solve_back,
        (
            msg_type,
            pltpu.VMEM(cotangent.shape, f32),
            pltpu.VMEM(cell_mask.shape, jnp.int32),
            first_held,
            wide_held,
        ),
        (gathered, turns, y_back, cotangent, cell_mask, first, weights),
        hbm=range(2, 7),
        scratch=(back_table, dma((5,))),
        flops=table_flops,
        name="solve_back",
    )
    msg = trade(msg, 128, PLANE)
    totals, grad_velocity, grad_buoyancy = call(
        closure_back,
        (
            type_of((32 * 11, LANES), f32),
            pltpu.HBM(cotangent.shape, f32),
            pltpu.HBM(buoyancy.shape, f32),
        ),
        (msg, turns, second, x_back, cotangent, cell_mask, first, weights),
        hbm_out=(1, 2),
        scratch=(
            pltpu.VMEM((1024, LANES), f32),
            wide,
            wide,
            wide,
            wide,
            pltpu.VMEM((64, cells), bf16),
            pltpu.VMEM((256, LANES), f32),
            pltpu.VMEM(cotangent.shape, f32),
            pltpu.VMEM(buoyancy.shape, f32),
            dma((4,)),
        ),
        flops=table_flops + 2 * 256 * 256 * cells * 10,
        name="closure_back",
    )
    totals = trade(totals, 32, SLAB)
    (totals,) = call(sum_slab, (type_of((16 * 11, LANES), f32),), (totals,), name="sum_slab")
    totals = trade(totals, 16, COLUMN)
    scale = 1.0 / math.sqrt(width * span_y * depth)
    grad_in, grad_b_in, grad_mid, grad_b_mid, grad_out = call(
        functools.partial(sum_column, scale),
        (
            type_of((4, 32), f32),
            type_of((1, 32), f32),
            type_of((32, 32), f32),
            type_of((1, 32), f32),
            type_of((3, 32), f32),
        ),
        (totals,),
        name="sum_column",
    )
    return (
        grad_velocity,
        grad_buoyancy,
        grad_in.T,
        grad_b_in[0],
        grad_mid,
        grad_b_mid[0],
        grad_out,
    )


def solution(mesh):
    fine = Mesh(
        mesh.devices.reshape([size for _, size in FINE]), tuple(name for name, _ in FINE)
    )
    field = P(None, NARROW, WIDE, None)
    cell = P(NARROW, WIDE, None)
    in_specs = (field, cell, cell, P(), field, P(), P(), P(), P(), P())
    out_specs = (field, cell, P(), P(), P(), P(), P())
    return jax.shard_map(shards, mesh=fine, in_specs=in_specs, out_specs=out_specs, check_vma=False)
```

```python
import functools
import math

import jax
import jax.numpy as jnp
import ml_dtypes
import numpy as np
from jax import lax
from jax.experimental import pallas as pl
from jax.experimental.pallas import tpu as pltpu
from jax.sharding import Mesh
from jax.sharding import PartitionSpec as P

free_surface = 0.05
f32 = jnp.float32
bf16 = jnp.bfloat16
LANES = 128
LEVELS = 8
VMEM_LIMIT = 24 * 1024 * 1024

FINE = (("y", 4), ("zl", 8), ("c", 2), ("zh", 2), ("x", 4))
WIDE = ("y", "zl", "c")
NARROW = ("zh", "x")
PLANE = ("zh", "y", "zl", "c")
SLAB = ("y", "x", "c")
COLUMN = ("zl", "zh")


def dft_table(count, length):
    indices = np.arange(count)
    angle = 2.0 * np.pi / count * (indices[:, None] * indices[None, :] % count)
    return np.concatenate([np.cos(angle), np.sin(angle)], axis=0) * np.sqrt(2.0 / length)


def twiddles(count, length):
    angle = 2.0 * np.pi / length * np.arange(count)[:, None] * np.arange(4)[None, :]
    held = np.zeros((count, LANES))
    held[:, 0:8:2] = np.cos(angle)
    held[:, 1:8:2] = np.sin(angle)
    return held.astype(np.float32)


def wavenumbers(length):
    half = np.arange(length // 2)
    return np.concatenate([half, np.where(half == 0, length // 2, half)])


def two_parts(table):
    high = table.astype(np.float32).astype(ml_dtypes.bfloat16)
    low = (table - high.astype(np.float64)).astype(np.float32).astype(ml_dtypes.bfloat16)
    return np.concatenate([high, low], axis=0)


def eigenvalue(length):
    return -4.0 * np.sin(np.pi / length * wavenumbers(length)) ** 2


def split(value):
    high = value.astype(bf16)
    low = (value - high.astype(f32)).astype(bf16)
    return high, low


def split_f32(value):
    high = value.astype(bf16).astype(f32)
    return high, value - high


def dot(a, b):
    return jnp.dot(a, b, preferred_element_type=f32)


def dot_table(table_ref, b, start, rows):
    middle = start + rows
    return dot(table_ref[start:middle], b) + dot(table_ref[middle : middle + rows], b)


def dot_nt(a, b):
    return lax.dot_general(a, b, (((1,), (1,)), ((), ())), preferred_element_type=f32)


def roll(value, shift, axis):
    size = value.shape[axis]
    shift = shift % size
    return value if shift == 0 else pltpu.roll(value, shift, axis)


def lane_of(shape):
    return lax.broadcasted_iota(jnp.int32, shape, len(shape) - 1)


def start_copy(source, target, sems, index):
    copy = pltpu.make_async_copy(source, target, sems.at[index])
    copy.start()
    return copy


def call(kernel, out_shape, args, smem=(), hbm=(), hbm_out=(), scratch=(), flops=0, name=None):
    def space(index, held):
        return pl.BlockSpec(memory_space=held.get(index, pltpu.VMEM))

    held = {i: pltpu.SMEM for i in smem} | {i: pl.ANY for i in hbm}
    args = [
        pltpu.with_memory_space_constraint(a, pltpu.HBM) if i in hbm else a
        for i, a in enumerate(args)
    ]
    moved = sum(int(np.prod(a.shape)) * a.dtype.itemsize for a in args)
    return pl.pallas_call(
        kernel,
        out_shape=out_shape,
        in_specs=[space(i, held) for i in range(len(args))],
        out_specs=[space(i, {o: pl.ANY for o in hbm_out}) for i in range(len(out_shape))],
        scratch_shapes=list(scratch),
        compiler_params=pltpu.CompilerParams(vmem_limit_bytes=VMEM_LIMIT),
        cost_estimate=pl.CostEstimate(flops=flops, bytes_accessed=moved, transcendentals=0),
        name=name,
    )(*args)


def first_row(shape):
    return lax.broadcasted_iota(jnp.int32, shape, 0) == 0


def join(cos_r, sin_r):
    even_c, even_s = cos_r[0] + cos_r[2], sin_r[0] + sin_r[2]
    odd_c, odd_s = cos_r[1] + cos_r[3], sin_r[1] + sin_r[3]
    top = first_row(even_c.shape)
    ends = jnp.where(top, math.sqrt(0.5), 1.0)
    return (
        (even_c + odd_c) * ends,
        cos_r[0] - cos_r[2] - (sin_r[1] - sin_r[3]),
        jnp.where(top, even_c - odd_c, even_s + odd_s) * ends,
        sin_r[0] - sin_r[2] + (cos_r[1] - cos_r[3]),
    )


def part_back(blocks):
    top = first_row(blocks[0].shape)
    ends = jnp.where(top, math.sqrt(0.5), 1.0)
    low_c, high_c, low_s, high_s = blocks
    low_c, low_s = low_c * ends, low_s * ends
    last = jnp.where(top, low_s, 0.0)
    low_s = jnp.where(top, 0.0, low_s)
    even, odd = low_c + last, low_c - last
    return (
        (even + high_c, odd + high_s, even - high_c, odd - high_s),
        (low_s + high_s, low_s - high_c, low_s - high_s, low_s + high_c),
    )


def turn(cos_part, sin_part, cos_turn, sin_turn):
    return cos_part * cos_turn - sin_part * sin_turn, sin_part * cos_turn + cos_part * sin_turn


def turn_of(turn_ref, remainder):
    rows, shape = slice(0, 256), (256, LANES)
    return (
        jnp.broadcast_to(turn_ref[rows, 2 * remainder : 2 * remainder + 1], shape),
        jnp.broadcast_to(turn_ref[rows, 2 * remainder + 1 : 2 * remainder + 2], shape),
    )


def forward_x(cot_hbm, table_hbm, turn_hbm, out_ref, mark_ref,
              table_ref, turn_ref, cot_ref, line_ref, sems):
    first = start_copy(cot_hbm, cot_ref, sems, 0)
    copies = [
        start_copy(table_hbm, table_ref, sems, 1),
        start_copy(turn_hbm, turn_ref, sems, 2),
    ]
    first.wait()
    east, north, up = cot_ref[0, 0], cot_ref[1, 0], cot_ref[2, 0]
    rows, width = east.shape
    east = east - roll(east, -1, 1)
    high, low = split_f32(jnp.concatenate([east, north, up], axis=0))
    none = jnp.zeros((rows, width), f32)
    line_ref[...] = jnp.concatenate([high, none, low, none], axis=0).T
    lines = jnp.concatenate(
        [line_ref[pl.ds(r, 256, stride=4), :].astype(bf16) for r in range(4)], axis=1
    )
    for copy in copies:
        copy.wait()
    got = dot_table(table_ref, lines, 0, 512)
    cos_r, sin_r = [], []
    for r in range(4):
        cos_part = got[0:256, LANES * r : LANES * (r + 1)]
        sin_part = got[256:512, LANES * r : LANES * (r + 1)]
        if r > 0:
            cos_part, sin_part = turn(cos_part, sin_part, *turn_of(turn_ref, r))
        cos_r.append(cos_part)
        sin_r.append(sin_part)
    blocks = [block + roll(block, 64, 1) for block in join(cos_r, sin_r)]
    lane = lane_of((LANES, LANES))
    for field in range(3):
        packed = jnp.zeros((LANES, LANES), f32)
        for t in range(8):
            block = blocks[t // 2][LANES * (t % 2) : LANES * (t % 2 + 1)]
            packed = jnp.where(lane // 16 == t, roll(block, 16 * (t - field), 1), packed)
        out_ref[pl.ds(field, LANES, stride=3), :] = packed
    mark_ref[...] = jnp.zeros(mark_ref.shape, f32)


def pair_turns(turn_ref, pair, within):
    one, two = turn_of(turn_ref, 2 * pair), turn_of(turn_ref, 2 * pair + 1)
    return tuple(jnp.where(within < 8, a, b) for a, b in zip(one, two))


def forward_y(msg_ref, table_hbm, turn_hbm, back_hbm, wide_hbm, mark_ref,
              out_ref, turn_ref, back_ref, wide_ref, table_ref, sems):
    copies = [
        start_copy(table_hbm, table_ref, sems, 0),
        start_copy(turn_hbm, turn_ref, sems, 1),
    ]
    later_copies = [
        start_copy(back_hbm, back_ref, sems, 2),
        start_copy(wide_hbm, wide_ref, sems, 3),
    ]
    within = lane_of((64, LANES)) % 16
    highs = []
    lows = []
    for half in range(2):
        east, north, up = (
            msg_ref[pl.ds(192 * half + field, 64, stride=3), :] for field in range(3)
        )
        after = jnp.where(
            within < 15, roll(north, -1, 1), roll(roll(north, -1, 0), 15, 1)
        )
        for value in (east + north - after, up):
            high, low = split_f32(value)
            highs.append(high)
            lows.append(low)
    shifted = [roll(value, c, 1) for c, value in enumerate(highs + lows)]

    def line_of(j, to):
        line = shifted[0]
        for c in range(1, 8):
            line = jnp.where(within == (c + j) % 16, shifted[c], line)
        return roll(line, to - j, 1)

    lines = []
    for pair in range(2):
        rows = []
        for step in range(4):
            j = 4 * step + 2 * pair
            rows.append(jnp.where(within < 8, line_of(j, 0), line_of(j + 1, 8)).astype(bf16))
        lines.append(jnp.concatenate(rows, axis=0))
    lines = jnp.concatenate(lines, axis=1)
    for copy in copies:
        copy.wait()
    got = dot_table(table_ref, lines, 0, 512)
    within = lane_of((256, LANES)) % 16
    turned = [
        turn(
            got[0:256, LANES * pair : LANES * (pair + 1)],
            got[256:512, LANES * pair : LANES * (pair + 1)],
            *pair_turns(turn_ref, pair, within),
        )
        for pair in range(2)
    ]
    cos_r = [turned[0][0], roll(turned[0][0], -8, 1), turned[1][0], roll(turned[1][0], -8, 1)]
    sin_r = [turned[0][1], roll(turned[0][1], -8, 1), turned[1][1], roll(turned[1][1], -8, 1)]
    packed = jnp.zeros((256, LANES), f32)
    for g, block in enumerate(join(cos_r, sin_r)):
        block = block + roll(block, -4, 1)
        packed = jnp.where(within // 4 == g, roll(block, 4 * g, 1), packed)
    for peer in range(4):
        out_ref[peer] = packed
    for copy in later_copies:
        copy.wait()


def vertical(spacing):
    one = jnp.ones((1, LANES), f32)
    none = jnp.zeros((1, LANES), f32)
    spacing = [one * spacing[k] for k in range(LEVELS)]
    inv_dz = [1.0 / value for value in spacing]
    face = [2.0 / (spacing[k] + spacing[k + 1]) for k in range(LEVELS - 1)] + [none]
    lower = [none] + [inv_dz[k] * face[k - 1] for k in range(1, LEVELS)]
    upper = [inv_dz[k] * face[k] for k in range(LEVELS)]
    base = [-(lower[k] + upper[k]) for k in range(LEVELS)]
    base[-1] = base[-1] - free_surface * inv_dz[-1]
    sub = [none] + upper[:-1]
    sup = lower[1:] + [none]
    keep = [one] * (LEVELS - 1) + [none]
    return inv_dz, face, sub, base, sup, keep


def solve_back(got_ref, turn_ref, table_ref, out_ref):
    at = lax.axis_index("x")
    rows = got_ref.shape[1]
    lam = turn_ref[256 : 256 + rows // 4]
    lane = lane_of((rows, LANES))
    column = lane_of(lam.shape) % 4
    inv_dz, face, sub, base, sup, keep = (
        [turn_ref[512 + 8 * i + k : 513 + 8 * i + k] for k in range(LEVELS)]
        for i in range(6)
    )
    quarters = [slice(rows // 4 * r, rows // 4 * (r + 1)) for r in range(4)]

    def gathered(k, field):
        at_lane = 2 * (k // 4) + field
        value = roll(got_ref[k % 4, quarters[0], :], -at_lane, 1)
        for r in range(1, 4):
            moved = roll(got_ref[k % 4, quarters[r], :], r - at_lane, 1)
            value = jnp.where(column == r, moved, value)
        return value

    ratios = []
    values = []
    below = None
    for k in range(LEVELS):
        flux = gathered(k, 1) * face[k]
        right = gathered(k, 0) - flux
        if k > 0:
            right = right + below
        below = flux
        diagonal = lam + base[k]
        if k > 0:
            diagonal = diagonal - sub[k] * ratios[-1]
            right = right - sub[k] * values[-1]
        inverse = 1.0 / diagonal
        ratios.append(sup[k] * inverse)
        values.append(right * inverse)
    result = [None] * LEVELS
    result[-1] = values[-1]
    for k in range(LEVELS - 2, -1, -1):
        result[k] = values[k] - ratios[k] * result[k + 1]
    scaled = [result[k] * inv_dz[k] for k in range(LEVELS)] + [jnp.zeros_like(lam)]
    change = [(scaled[k] - scaled[k + 1]) * keep[k] for k in range(LEVELS)]

    def own(items, half):
        value = items[4 * half]
        for x in range(1, 4):
            value = jnp.where(at == x, items[4 * half + x], value)
        return value

    fields = [own(result, 0), own(change, 0), own(result, 1), own(change, 1)]
    both = []
    for r in range(4):
        value = roll(fields[0], -r, 1)
        for c in range(1, 4):
            value = jnp.where(column == c, roll(fields[c], c - r, 1), value)
        both.append(value)
    both = jnp.concatenate(both, axis=0)
    within = lane % 16
    blocks = []
    for g in range(4):
        block = roll(both, -4 * g, 1)
        blocks.append(jnp.where(within < 8, block, roll(block, 8, 1)))
    cos_r, sin_r = part_back(blocks)
    parts = ([], [])
    for pair in range(2):
        cos_part = jnp.where(within < 8, cos_r[2 * pair], cos_r[2 * pair + 1])
        sin_part = jnp.where(within < 8, sin_r[2 * pair], sin_r[2 * pair + 1])
        cos_turn, sin_turn = pair_turns(turn_ref, pair, within)
        for i, value in enumerate(turn(cos_part, sin_part, cos_turn, -sin_turn)):
            high, low = split_f32(jnp.where(within % 8 < 4, value, 0.0))
            parts[i].append((high + roll(low, 4, 1)).astype(bf16))
    columns = jnp.concatenate([jnp.concatenate(part, axis=1) for part in parts], axis=0)
    got = dot_table(table_ref, columns, 512, 256)
    within = lane_of((64, LANES)) % 16
    packed = [jnp.zeros((64, LANES), f32)] * 4
    for pair in range(2):
        found = got[:, LANES * pair : LANES * (pair + 1)]
        found = found + roll(found, -4, 1)
        for step in range(4):
            for one in range(2):
                j = 4 * step + 2 * pair + one
                moved = roll(found[64 * step : 64 * (step + 1)], j - 8 * one, 1)
                for c in range(4):
                    packed[c] = jnp.where(within == (j + c) % 16, moved, packed[c])
    for half in range(2):
        pressure = roll(packed[2 * half], -2 * half, 1)
        change_up = roll(packed[2 * half + 1], -(2 * half + 1), 1)
        before = jnp.where(
            within > 0, roll(pressure, 1, 1), roll(roll(pressure, 1, 0), -15, 1)
        )
        for field, value in enumerate((pressure, change_up, before - pressure)):
            out_ref[pl.ds(192 * half + field, 64, stride=3), :] = value


CHUNK = 1024


def unit_rows(shape, axis):
    return lax.broadcasted_iota(jnp.int32, shape, axis) % 8


def same_row(value):
    shape = value.shape
    return jnp.where(unit_rows(shape, 0) == unit_rows(shape, 1), value, 0.0)


def gather(shape, step):
    to = lax.broadcasted_iota(jnp.int32, shape, 1)
    return (lax.broadcasted_iota(jnp.int32, shape, 0) // step == to).astype(f32)


def exact(a, b):
    return jnp.dot(a, b, precision=lax.Precision.HIGHEST, preferred_element_type=f32)


def spread(weight, columns):
    tall, wide = weight.shape
    step = (
        lax.broadcasted_iota(jnp.int32, (wide, columns), 1) // 8
        == lax.broadcasted_iota(jnp.int32, (wide, columns), 0)
    ).astype(f32)
    value = exact(weight, step)
    value = jnp.broadcast_to(value[:, None, :], (tall, 8, columns)).reshape(8 * tall, columns)
    return same_row(value)


def closure_forward(win_hbm, bin_hbm, wmid_hbm, bmid_hbm, wout_hbm, spacing_hbm,
                    vel_hbm, buoy_hbm, fixed_hbm, mark_ref,
                    first_hbm, second_hbm, wide_hbm, turn_hbm, done_ref,
                    win_ref, bin_ref, wmid_ref, bmid_ref, wout_ref, spacing_ref,
                    vel_ref, buoy_ref, turn_ref, first_ref, second_ref, wide_ref, sems, out_sems):
    sources = (win_hbm, bin_hbm, wmid_hbm, bmid_hbm, wout_hbm, spacing_hbm)
    sources += (vel_hbm, buoy_hbm, fixed_hbm)
    targets = (win_ref, bin_ref, wmid_ref, bmid_ref, wout_ref, spacing_ref)
    targets += (vel_ref, buoy_ref, turn_ref)
    copies = [start_copy(*pair, sems, i) for i, pair in enumerate(zip(sources, targets))]
    for copy in copies[:6]:
        copy.wait()
    win_t = win_ref[...]
    wmid = wmid_ref[...]
    wout_h, wout_l = split_f32(spread(wout_ref[...].T, 32))
    wide_ref[0:256, 0:96] = jnp.concatenate([wout_h, wout_h, wout_l], axis=1).astype(bf16)
    wide_ref[0:256, 96:128] = jnp.zeros((256, 32), bf16)
    wide_ref[0:256, 128:384], wide_ref[0:256, 384:640] = split(spread(wmid.T, 256))
    wide_ref[256:288, 0:128] = jnp.zeros((32, 128), bf16)
    wide_ref[256:288, 128:384], wide_ref[256:288, 384:640] = split(spread(win_t, 256))
    win_h, win_l = split_f32(spread(win_t.T, 32))
    win_cat = jnp.concatenate([win_h, win_h, win_l], axis=1).astype(bf16)
    wmh, wml = split(spread(wmid, 256))

    def tall(row):
        column = row.T
        return jnp.broadcast_to(column[:, None, :], (32, 8, 1)).reshape(256, 1)

    b_in, b_mid = tall(bin_ref[...]), tall(bmid_ref[...])
    for copy in copies[6:]:
        copy.wait()
    own = turn_ref[pl.ds(512 + lax.axis_index(PLANE), 1), :]
    turn_ref[256:512] = turn_ref[256:512] + own
    for i, rows in enumerate(vertical([spacing_ref[:, k : k + 1] for k in range(LEVELS)])):
        turn_ref[512 + 8 * i : 520 + 8 * i] = jnp.concatenate(rows, axis=0)
    copies = [
        start_copy(wide_ref, wide_hbm, out_sems, 0),
        start_copy(turn_ref, turn_hbm, out_sems, 1),
    ]
    width = buoy_ref.shape[-1]
    for half in range(2):
        part = slice(8 * half, 8 * (half + 1))
        for start in range(0, width, CHUNK):
            col = slice(start, start + CHUNK)
            to = slice(half * width + start, half * width + start + CHUNK)
            feats = jnp.concatenate(
                [vel_ref[c, 0, part, col] for c in range(3)] + [buoy_ref[0, part, col]], axis=0
            )
            high, low = split_f32(feats)
            stack = jnp.concatenate([high, low, high], axis=0).astype(bf16)
            first_ref[512:608, to] = jnp.concatenate(
                [high, low, jnp.ones((32, CHUNK), f32)], axis=0
            ).astype(bf16)
            first = jnp.tanh(dot(win_cat, stack) + b_in)
            fh, fl = split(first)
            first_ref[0:256, to] = fh
            first_ref[256:512, to] = fl
            second = dot(wmh, fh) + dot(wmh, fl) + dot(wml, fh)
            second = jnp.tanh(second + b_mid)
            sh, sl = split(second)
            second_ref[0:256, to] = sh
            second_ref[256:512, to] = sl
        whole = slice(half * width, (half + 1) * width)
        for i, (held, target) in enumerate(((first_ref, first_hbm), (second_ref, second_hbm))):
            copies.append(
                start_copy(held.at[:, whole], target.at[:, whole], out_sems, 2 + 2 * half + i)
            )
    done_ref[...] = jnp.zeros(done_ref.shape, f32)
    for copy in copies:
        copy.wait()


def closure_back(msg_ref, turn_ref, second_ref, table_ref, cot_ref, mask_ref, first_ref,
                 wide_ref, total_ref, gvel_hbm, gbuoy_hbm,
                 line_ref, e1h_ref, e1l_ref, e2h_ref, e2l_ref, dl_ref, b2_ref,
                 gvel_ref, gbuoy_ref, out_sems):
    width = mask_ref.shape[-1]
    lane = lane_of((LANES, LANES))
    halves = []
    items = [msg_ref[pl.ds(field, LANES, stride=3), :] for field in range(3)]
    for t in range(8):
        value = jnp.zeros((LANES, LANES), f32)
        for field, item in enumerate(items):
            value = jnp.where(lane // 16 == field, roll(item, 16 * (field - t), 1), value)
        halves.append(value)
    cos_r, sin_r = part_back(
        [jnp.concatenate(halves[2 * i : 2 * i + 2], axis=0) for i in range(4)]
    )
    parts = ([], [])
    for r in range(4):
        pair = (cos_r[r], sin_r[r])
        if r > 0:
            cos_turn, sin_turn = turn_of(turn_ref, r)
            pair = turn(*pair, cos_turn, -sin_turn)
        for i, value in enumerate(pair):
            high, low = split_f32(value)
            parts[i].append((high + roll(low, 64, 1)).astype(bf16))
    columns = jnp.concatenate([jnp.concatenate(part, axis=1) for part in parts], axis=0)
    found = dot_table(table_ref, columns, 0, 256)
    for r in range(4):
        block = found[:, LANES * r : LANES * (r + 1)]
        line_ref[pl.ds(r, 256, stride=4), :] = block + roll(block, 64, 1)
    field = line_ref[...].T
    pressure = field[0:16]
    east_back = roll(pressure, 1, 1) - pressure
    projected = (
        cot_ref[0, 0] - east_back,
        cot_ref[1, 0] - field[32:48],
        cot_ref[2, 0] - field[16:32],
    )
    wet = mask_ref[0].astype(f32)
    out_copies = []
    deltas = [value * wet for value in projected]
    blank = jnp.zeros((8, CHUNK), f32)
    bias2 = jnp.zeros((256, LANES), f32)
    for half in range(2):
        part = slice(8 * half, 8 * (half + 1))
        for start in range(0, width, CHUNK):
            col = slice(start, start + CHUNK)
            to = slice(half * width + start, half * width + start + CHUNK)
            delta = jnp.concatenate([value[part, col] for value in deltas] + [blank], axis=0)
            dh, dl = split_f32(delta)
            stack = jnp.concatenate([dh, dl, dh], axis=0).astype(bf16)
            dl_ref[:, to] = stack[0:64]
            second = second_ref[0:256, to].astype(f32) + second_ref[256:512, to].astype(f32)
            err2 = dot(wide_ref[0:256, 0:96], stack) * (1.0 - second * second)
            bias2 = bias2 + sum(err2[:, LANES * i : LANES * (i + 1)] for i in range(CHUNK // LANES))
            e2h, e2l = split(err2)
            e2h_ref[:, to] = e2h
            e2l_ref[:, to] = e2l
            first = first_ref[0:256, to].astype(f32) + first_ref[256:512, to].astype(f32)
            err1 = (
                dot(wide_ref[0:256, 128:384], e2h)
                + dot(wide_ref[0:256, 128:384], e2l)
                + dot(wide_ref[0:256, 384:640], e2h)
            )
            err1 = err1 * (1.0 - first * first)
            e1h, e1l = split(err1)
            e1h_ref[:, to] = e1h
            e1l_ref[:, to] = e1l
            out = (
                dot(wide_ref[256:288, 128:384], e1h)
                + dot(wide_ref[256:288, 128:384], e1l)
                + dot(wide_ref[256:288, 384:640], e1h)
            )
            for c in range(3):
                gvel_ref[c, 0, part, col] = projected[c][part, col] + out[8 * c : 8 * (c + 1)]
            gbuoy_ref[0, part, col] = out[24:32]
        out_copies += [
            start_copy(gvel_ref.at[:, :, part, :], gvel_hbm.at[:, :, part, :], out_sems, 2 * half),
            start_copy(gbuoy_ref.at[:, part, :], gbuoy_hbm.at[:, part, :], out_sems, 2 * half + 1),
        ]
    b2_ref[...] = bias2
    mid = (
        dot_nt(e2h_ref[...], first_ref[0:256])
        + dot_nt(e2h_ref[...], first_ref[256:512])
        + dot_nt(e2l_ref[...], first_ref[0:256])
    )
    both1 = dot_nt(first_ref[512:608], e1h_ref[...])
    rest1 = dot_nt(first_ref[512:608], e1l_ref[...])
    win = both1[0:32] + both1[32:64] + rest1[0:32]
    bin_ = both1[64:65] + rest1[64:65]
    both2 = dot_nt(dl_ref[...], second_ref[0:256])
    rest2 = dot_nt(dl_ref[...], second_ref[256:512])
    wout = both2[0:32] + both2[32:64] + rest2[0:32]

    def fold_rows(value):
        return jnp.sum(value.reshape(value.shape[0] // 8, 8, value.shape[1]), axis=1)

    to_unit = gather((256, LANES), 8)
    mid = exact(fold_rows(same_row(mid)), to_unit)
    small = [fold_rows(same_row(win)), fold_rows(same_row(wout)), bin_, jnp.zeros((7, 256), f32)]
    small = exact(jnp.concatenate(small, axis=0), to_unit)
    b2 = lax.dot_general(
        jnp.ones((8, LANES), f32),
        fold_rows(b2_ref[...]),
        (((1,), (1,)), ((), ())),
        precision=lax.Precision.HIGHEST,
        preferred_element_type=f32,
    )
    units = jnp.concatenate([mid[8 * i : 8 * (i + 1), 0:32] for i in range(4)], axis=1)
    rows = [units[i : i + 1] for i in range(8)]
    rows.append(jnp.concatenate([small[i : i + 1, 0:32] for i in range(4)], axis=1))
    rows.append(
        jnp.concatenate([small[i : i + 1, 0:32] for i in range(4, 7)] + [b2[0:1]], axis=1)
    )
    rows.append(small[8:9])
    rows = jnp.concatenate(rows, axis=0)
    for peer in range(32):
        total_ref[11 * peer : 11 * (peer + 1), :] = rows
    for copy in out_copies:
        copy.wait()


def sum_rows(got_ref):
    return [
        jnp.sum(got_ref[pl.ds(i, got_ref.shape[0] // 11, stride=11), :], axis=0, keepdims=True)
        for i in range(11)
    ]


def sum_slab(got_ref, out_ref):
    total = jnp.concatenate(sum_rows(got_ref), axis=0)
    for peer in range(16):
        out_ref[11 * peer : 11 * (peer + 1), :] = total


def sum_column(scale, got_ref, win_ref, bin_ref, wmid_ref, bmid_ref, wout_ref):
    rows = [row * scale for row in sum_rows(got_ref)]
    units = jnp.concatenate(rows[:8], axis=0)
    wmid_ref[...] = jnp.concatenate([units[:, 32 * i : 32 * (i + 1)] for i in range(4)], axis=0)
    win_ref[...] = jnp.concatenate([rows[8][:, 32 * i : 32 * (i + 1)] for i in range(4)], axis=0)
    wout_ref[...] = jnp.concatenate([rows[9][:, 32 * i : 32 * (i + 1)] for i in range(3)], axis=0)
    bmid_ref[...] = rows[9][:, 96:128]
    bin_ref[...] = rows[10][:, 0:32]


def trade(rows, peers, axes):
    size = rows.shape[0] // peers * LANES
    got = lax.all_to_all(rows.reshape(peers, 1, size), axes, 0, 0)
    return got.reshape(rows.shape)


def shards(velocity, buoyancy, cell_mask, spacing, cotangent, w_in, b_in, w_mid, b_mid, w_out):
    levels, rows, width = buoyancy.shape
    depth = spacing.shape[0]
    span_y = rows * 64
    table = dft_table(256, 1024)
    table_y = table[:, (np.arange(256) % 64) * 4 + np.arange(256) // 64]
    x_table, y_table = jnp.asarray(two_parts(table)), jnp.asarray(two_parts(table_y))
    backs = jnp.asarray(np.concatenate([two_parts(table.T), two_parts(table_y.T)], axis=0))
    eigen = eigenvalue(width)
    lanes = np.arange(LANES)
    ey = eigen.reshape(4, 4, 64)[lanes % 16 // 4, lanes % 4].T.astype(np.float32)
    ey = np.concatenate([ey, np.zeros((192, LANES), np.float32)], axis=0)
    ex = eigen[np.arange(128)[:, None] + 128 * (lanes[None, :] // 16)].astype(np.float32)
    turns = twiddles(256, 1024)
    fixed = jnp.asarray(np.concatenate([turns, ey, ex], axis=0))
    turns = jnp.asarray(turns)
    cells = rows * width // 8
    dma = pltpu.SemaphoreType.DMA
    type_of = jax.ShapeDtypeStruct
    table = pltpu.VMEM((1024, 256), bf16)
    back_tables = pltpu.VMEM((1024, 512), bf16)
    turn_held = pltpu.VMEM((640, LANES), f32)
    first_held = pltpu.VMEM((608, cells), bf16)
    second_held = pltpu.VMEM((512, cells), bf16)
    wide = pltpu.VMEM((256, cells), bf16)
    wide_held = pltpu.VMEM((288, 640), bf16)
    mark_type = type_of((8, LANES), f32)
    table_flops = 4 * 512 * 256 * 512
    msg_type = type_of((128 * 3, LANES), f32)
    msg, mark = call(
        forward_x,
        (msg_type, mark_type),
        (cotangent, x_table, turns),
        hbm=(0, 1, 2),
        scratch=(
            table,
            pltpu.VMEM((256, LANES), f32),
            pltpu.VMEM(cotangent.shape, f32),
            pltpu.VMEM((1024, LANES), f32),
            dma((3,)),
        ),
        flops=table_flops,
        name="forward_x",
    )
    msg = trade(msg, 128, PLANE)

    first, second, weights, turns, mark = call(
        closure_forward,
        (
            pltpu.HBM((608, cells), bf16),
            pltpu.HBM((512, cells), bf16),
            pltpu.HBM((288, 640), bf16),
            pltpu.HBM((640, LANES), f32),
            mark_type,
        ),
        (w_in.T, b_in[None], w_mid, b_mid[None], w_out, spacing[None])
        + (velocity, buoyancy, fixed, mark),
        hbm=range(9),
        hbm_out=range(4),
        scratch=(
            pltpu.VMEM((4, 32), f32),
            pltpu.VMEM((1, 32), f32),
            pltpu.VMEM((32, 32), f32),
            pltpu.VMEM((1, 32), f32),
            pltpu.VMEM((3, 32), f32),
            pltpu.VMEM((1, LEVELS), f32),
            pltpu.VMEM(velocity.shape, f32),
            pltpu.VMEM(buoyancy.shape, f32),
            turn_held,
            first_held,
            second_held,
            wide_held,
            dma((9,)),
            dma((6,)),
        ),
        flops=2 * 256 * 256 * cells * 4,
        name="closure_forward",
    )
    gathered, turns, backs, weights = call(
        forward_y,
        (type_of((4, 256, LANES), f32), turn_held, back_tables, wide_held),
        (msg, y_table, turns, backs, weights, mark),
        hbm=(1, 2, 3, 4),
        scratch=(table, dma((4,))),
        flops=table_flops,
        name="forward_y",
    )
    gathered = lax.all_to_all(gathered, "x", 0, 0)
    (msg,) = call(
        solve_back,
        (msg_type,),
        (gathered, turns, backs),
        flops=table_flops,
        name="solve_back",
    )
    msg = trade(msg, 128, PLANE)
    totals, grad_velocity, grad_buoyancy = call(
        closure_back,
        (
            type_of((32 * 11, LANES), f32),
            pltpu.HBM(cotangent.shape, f32),
            pltpu.HBM(buoyancy.shape, f32),
        ),
        (msg, turns, second, backs, cotangent, cell_mask, first, weights),
        hbm_out=(1, 2),
        scratch=(
            pltpu.VMEM((1024, LANES), f32),
            wide,
            wide,
            wide,
            wide,
            pltpu.VMEM((64, cells), bf16),
            pltpu.VMEM((256, LANES), f32),
            pltpu.VMEM(cotangent.shape, f32),
            pltpu.VMEM(buoyancy.shape, f32),
            dma((4,)),
        ),
        flops=table_flops + 2 * 256 * 256 * cells * 10,
        name="closure_back",
    )
    totals = trade(totals, 32, SLAB)
    (totals,) = call(sum_slab, (type_of((16 * 11, LANES), f32),), (totals,), name="sum_slab")
    totals = trade(totals, 16, COLUMN)
    scale = 1.0 / math.sqrt(width * span_y * depth)
    grad_in, grad_b_in, grad_mid, grad_b_mid, grad_out = call(
        functools.partial(sum_column, scale),
        (
            type_of((4, 32), f32),
            type_of((1, 32), f32),
            type_of((32, 32), f32),
            type_of((1, 32), f32),
            type_of((3, 32), f32),
        ),
        (totals,),
        name="sum_column",
    )
    return (
        grad_velocity,
        grad_buoyancy,
        grad_in.T,
        grad_b_in[0],
        grad_mid,
        grad_b_mid[0],
        grad_out,
    )


def solution(mesh):
    fine = Mesh(
        mesh.devices.reshape([size for _, size in FINE]), tuple(name for name, _ in FINE)
    )
    field = P(None, NARROW, WIDE, None)
    cell = P(NARROW, WIDE, None)
    in_specs = (field, cell, cell, P(), field, P(), P(), P(), P(), P())
    out_specs = (field, cell, P(), P(), P(), P(), P())
    return jax.shard_map(shards, mesh=fine, in_specs=in_specs, out_specs=out_specs, check_vma=False)
```

```python
import functools
import math

import jax
import jax.numpy as jnp
import ml_dtypes
import numpy as np
from jax import lax
from jax.experimental import pallas as pl
from jax.experimental.pallas import tpu as pltpu
from jax.sharding import Mesh
from jax.sharding import PartitionSpec as P

free_surface = 0.05
f32 = jnp.float32
bf16 = jnp.bfloat16
LANES = 128
LEVELS = 8
VMEM_LIMIT = 24 * 1024 * 1024

FINE = (("y", 4), ("zl", 8), ("c", 2), ("zh", 2), ("x", 4))
WIDE = ("y", "zl", "c")
NARROW = ("zh", "x")
PLANE = ("y", "zl", "c", "zh")
SLAB = ("y", "x", "c")
COLUMN = ("zh", "zl")


def dft_table(count, length):
    indices = np.arange(count)
    angle = 2.0 * np.pi / count * (indices[:, None] * indices[None, :] % count)
    return np.concatenate([np.cos(angle), np.sin(angle)], axis=0) * np.sqrt(2.0 / length)


def twiddles(count, length):
    angle = 2.0 * np.pi / length * np.arange(count)[:, None] * np.arange(4)[None, :]
    held = np.zeros((count, LANES))
    held[:, 0:8:2] = np.cos(angle)
    held[:, 1:8:2] = np.sin(angle)
    return held.astype(np.float32)


def wavenumbers(length):
    half = np.arange(length // 2)
    return np.concatenate([half, np.where(half == 0, length // 2, half)])


def two_parts(table):
    high = table.astype(np.float32).astype(ml_dtypes.bfloat16)
    low = (table - high.astype(np.float64)).astype(np.float32).astype(ml_dtypes.bfloat16)
    return np.concatenate([high, low], axis=0)


def eigenvalue(length):
    return -4.0 * np.sin(np.pi / length * wavenumbers(length)) ** 2


def split(value):
    high = value.astype(bf16)
    low = (value - high.astype(f32)).astype(bf16)
    return high, low


def split_f32(value):
    high = value.astype(bf16).astype(f32)
    return high, value - high


def dot(a, b):
    return jnp.dot(a, b, preferred_element_type=f32)


def dot_table(table_ref, b, start, rows):
    middle = start + rows
    return dot(table_ref[start:middle], b) + dot(table_ref[middle : middle + rows], b)


def dot_nt(a, b):
    return lax.dot_general(a, b, (((1,), (1,)), ((), ())), preferred_element_type=f32)


def roll(value, shift, axis):
    size = value.shape[axis]
    shift = shift % size
    return value if shift == 0 else pltpu.roll(value, shift, axis)


def lane_of(shape):
    return lax.broadcasted_iota(jnp.int32, shape, len(shape) - 1)


def start_copy(source, target, sems, index):
    copy = pltpu.make_async_copy(source, target, sems.at[index])
    copy.start()
    return copy


def call(kernel, out_shape, args, smem=(), hbm=(), hbm_out=(), scratch=(), flops=0, name=None):
    def space(index, held):
        return pl.BlockSpec(memory_space=held.get(index, pltpu.VMEM))

    held = {i: pltpu.SMEM for i in smem} | {i: pl.ANY for i in hbm}
    args = [
        pltpu.with_memory_space_constraint(a, pltpu.HBM) if i in hbm else a
        for i, a in enumerate(args)
    ]
    moved = sum(int(np.prod(a.shape)) * a.dtype.itemsize for a in args)
    return pl.pallas_call(
        kernel,
        out_shape=out_shape,
        in_specs=[space(i, held) for i in range(len(args))],
        out_specs=[space(i, {o: pl.ANY for o in hbm_out}) for i in range(len(out_shape))],
        scratch_shapes=list(scratch),
        compiler_params=pltpu.CompilerParams(vmem_limit_bytes=VMEM_LIMIT),
        cost_estimate=pl.CostEstimate(flops=flops, bytes_accessed=moved, transcendentals=0),
        name=name,
    )(*args)


def first_row(shape):
    return lax.broadcasted_iota(jnp.int32, shape, 0) == 0


def join(cos_r, sin_r):
    even_c, even_s = cos_r[0] + cos_r[2], sin_r[0] + sin_r[2]
    odd_c, odd_s = cos_r[1] + cos_r[3], sin_r[1] + sin_r[3]
    top = first_row(even_c.shape)
    ends = jnp.where(top, math.sqrt(0.5), 1.0)
    return (
        (even_c + odd_c) * ends,
        cos_r[0] - cos_r[2] - (sin_r[1] - sin_r[3]),
        jnp.where(top, even_c - odd_c, even_s + odd_s) * ends,
        sin_r[0] - sin_r[2] + (cos_r[1] - cos_r[3]),
    )


def part_back(blocks):
    top = first_row(blocks[0].shape)
    ends = jnp.where(top, math.sqrt(0.5), 1.0)
    low_c, high_c, low_s, high_s = blocks
    low_c, low_s = low_c * ends, low_s * ends
    last = jnp.where(top, low_s, 0.0)
    low_s = jnp.where(top, 0.0, low_s)
    even, odd = low_c + last, low_c - last
    return (
        (even + high_c, odd + high_s, even - high_c, odd - high_s),
        (low_s + high_s, low_s - high_c, low_s - high_s, low_s + high_c),
    )


def turn(cos_part, sin_part, cos_turn, sin_turn):
    return cos_part * cos_turn - sin_part * sin_turn, sin_part * cos_turn + cos_part * sin_turn


def turn_of(turn_ref, remainder):
    rows, shape = slice(0, 256), (256, LANES)
    return (
        jnp.broadcast_to(turn_ref[rows, 2 * remainder : 2 * remainder + 1], shape),
        jnp.broadcast_to(turn_ref[rows, 2 * remainder + 1 : 2 * remainder + 2], shape),
    )


def forward_x(cot_hbm, table_hbm, turn_hbm, out_ref, mark_ref,
              table_ref, turn_ref, cot_ref, line_ref, sems):
    first = start_copy(cot_hbm, cot_ref, sems, 0)
    copies = [
        start_copy(table_hbm, table_ref, sems, 1),
        start_copy(turn_hbm, turn_ref, sems, 2),
    ]
    first.wait()
    east, north, up = cot_ref[0, 0], cot_ref[1, 0], cot_ref[2, 0]
    rows, width = east.shape
    east = east - roll(east, -1, 1)
    high, low = split_f32(jnp.concatenate([east, north, up], axis=0))
    none = jnp.zeros((rows, width), f32)
    line_ref[...] = jnp.concatenate([high, none, low, none], axis=0).T
    lines = jnp.concatenate(
        [line_ref[pl.ds(r, 256, stride=4), :].astype(bf16) for r in range(4)], axis=1
    )
    for copy in copies:
        copy.wait()
    got = dot_table(table_ref, lines, 0, 512)
    cos_r, sin_r = [], []
    for r in range(4):
        cos_part = got[0:256, LANES * r : LANES * (r + 1)]
        sin_part = got[256:512, LANES * r : LANES * (r + 1)]
        if r > 0:
            cos_part, sin_part = turn(cos_part, sin_part, *turn_of(turn_ref, r))
        cos_r.append(cos_part)
        sin_r.append(sin_part)
    blocks = [block + roll(block, 64, 1) for block in join(cos_r, sin_r)]
    lane = lane_of((LANES, LANES))
    for field in range(3):
        packed = jnp.zeros((LANES, LANES), f32)
        for t in range(8):
            block = blocks[t // 2][LANES * (t % 2) : LANES * (t % 2 + 1)]
            packed = jnp.where(lane // 16 == t, roll(block, 16 * (t - field), 1), packed)
        out_ref[pl.ds(field, LANES, stride=3), :] = packed
    mark_ref[...] = jnp.zeros(mark_ref.shape, f32)


def pair_turns(turn_ref, pair, within):
    one, two = turn_of(turn_ref, 2 * pair), turn_of(turn_ref, 2 * pair + 1)
    return tuple(jnp.where(within < 8, a, b) for a, b in zip(one, two))


def forward_y(msg_ref, table_hbm, turn_hbm, back_hbm, wide_hbm, mark_ref,
              out_ref, turn_ref, back_ref, wide_ref, table_ref, sems):
    copies = [
        start_copy(table_hbm, table_ref, sems, 0),
        start_copy(turn_hbm, turn_ref, sems, 1),
    ]
    later_copies = [
        start_copy(back_hbm, back_ref, sems, 2),
        start_copy(wide_hbm, wide_ref, sems, 3),
    ]
    within = lane_of((64, LANES)) % 16
    highs = []
    lows = []
    for half in range(2):
        east, north, up = (
            msg_ref[pl.ds(3 * half + field, 64, stride=6), :] for field in range(3)
        )
        after = jnp.where(
            within < 15, roll(north, -1, 1), roll(roll(north, -1, 0), 15, 1)
        )
        for value in (east + north - after, up):
            high, low = split_f32(value)
            highs.append(high)
            lows.append(low)
    shifted = [roll(value, c, 1) for c, value in enumerate(highs + lows)]

    def line_of(j, to):
        line = shifted[0]
        for c in range(1, 8):
            line = jnp.where(within == (c + j) % 16, shifted[c], line)
        return roll(line, to - j, 1)

    lines = []
    for pair in range(2):
        rows = []
        for step in range(4):
            j = 4 * step + 2 * pair
            rows.append(jnp.where(within < 8, line_of(j, 0), line_of(j + 1, 8)).astype(bf16))
        lines.append(jnp.concatenate(rows, axis=0))
    lines = jnp.concatenate(lines, axis=1)
    for copy in copies:
        copy.wait()
    got = dot_table(table_ref, lines, 0, 512)
    within = lane_of((256, LANES)) % 16
    turned = [
        turn(
            got[0:256, LANES * pair : LANES * (pair + 1)],
            got[256:512, LANES * pair : LANES * (pair + 1)],
            *pair_turns(turn_ref, pair, within),
        )
        for pair in range(2)
    ]
    cos_r = [turned[0][0], roll(turned[0][0], -8, 1), turned[1][0], roll(turned[1][0], -8, 1)]
    sin_r = [turned[0][1], roll(turned[0][1], -8, 1), turned[1][1], roll(turned[1][1], -8, 1)]
    packed = jnp.zeros((256, LANES), f32)
    for g, block in enumerate(join(cos_r, sin_r)):
        block = block + roll(block, -4, 1)
        packed = jnp.where(within // 4 == g, roll(block, 4 * g, 1), packed)
    for peer in range(4):
        out_ref[peer] = packed
    for copy in later_copies:
        copy.wait()


def vertical(spacing):
    one = jnp.ones((1, LANES), f32)
    none = jnp.zeros((1, LANES), f32)
    spacing = [one * spacing[k] for k in range(LEVELS)]
    inv_dz = [1.0 / value for value in spacing]
    face = [2.0 / (spacing[k] + spacing[k + 1]) for k in range(LEVELS - 1)] + [none]
    lower = [none] + [inv_dz[k] * face[k - 1] for k in range(1, LEVELS)]
    upper = [inv_dz[k] * face[k] for k in range(LEVELS)]
    base = [-(lower[k] + upper[k]) for k in range(LEVELS)]
    base[-1] = base[-1] - free_surface * inv_dz[-1]
    sub = [none] + upper[:-1]
    sup = lower[1:] + [none]
    keep = [one] * (LEVELS - 1) + [none]
    return inv_dz, face, sub, base, sup, keep


def solve_back(got_ref, turn_ref, table_ref, out_ref):
    at = lax.axis_index("x")
    rows = got_ref.shape[1]
    lam = turn_ref[256 : 256 + rows // 4]
    lane = lane_of((rows, LANES))
    column = lane_of(lam.shape) % 4
    inv_dz, face, sub, base, sup, keep = (
        [turn_ref[512 + 8 * i + k : 513 + 8 * i + k] for k in range(LEVELS)]
        for i in range(6)
    )
    quarters = [slice(rows // 4 * r, rows // 4 * (r + 1)) for r in range(4)]

    def gathered(k, field):
        at_lane = 2 * (k // 4) + field
        value = roll(got_ref[k % 4, quarters[0], :], -at_lane, 1)
        for r in range(1, 4):
            moved = roll(got_ref[k % 4, quarters[r], :], r - at_lane, 1)
            value = jnp.where(column == r, moved, value)
        return value

    ratios = []
    values = []
    below = None
    for k in range(LEVELS):
        flux = gathered(k, 1) * face[k]
        right = gathered(k, 0) - flux
        if k > 0:
            right = right + below
        below = flux
        diagonal = lam + base[k]
        if k > 0:
            diagonal = diagonal - sub[k] * ratios[-1]
            right = right - sub[k] * values[-1]
        inverse = 1.0 / diagonal
        ratios.append(sup[k] * inverse)
        values.append(right * inverse)
    result = [None] * LEVELS
    result[-1] = values[-1]
    for k in range(LEVELS - 2, -1, -1):
        result[k] = values[k] - ratios[k] * result[k + 1]
    scaled = [result[k] * inv_dz[k] for k in range(LEVELS)] + [jnp.zeros_like(lam)]
    change = [(scaled[k] - scaled[k + 1]) * keep[k] for k in range(LEVELS)]

    def own(items, half):
        value = items[4 * half]
        for x in range(1, 4):
            value = jnp.where(at == x, items[4 * half + x], value)
        return value

    fields = [own(result, 0), own(change, 0), own(result, 1), own(change, 1)]
    both = []
    for r in range(4):
        value = roll(fields[0], -r, 1)
        for c in range(1, 4):
            value = jnp.where(column == c, roll(fields[c], c - r, 1), value)
        both.append(value)
    both = jnp.concatenate(both, axis=0)
    within = lane % 16
    blocks = []
    for g in range(4):
        block = roll(both, -4 * g, 1)
        blocks.append(jnp.where(within < 8, block, roll(block, 8, 1)))
    cos_r, sin_r = part_back(blocks)
    parts = ([], [])
    for pair in range(2):
        cos_part = jnp.where(within < 8, cos_r[2 * pair], cos_r[2 * pair + 1])
        sin_part = jnp.where(within < 8, sin_r[2 * pair], sin_r[2 * pair + 1])
        cos_turn, sin_turn = pair_turns(turn_ref, pair, within)
        for i, value in enumerate(turn(cos_part, sin_part, cos_turn, -sin_turn)):
            high, low = split_f32(jnp.where(within % 8 < 4, value, 0.0))
            parts[i].append((high + roll(low, 4, 1)).astype(bf16))
    columns = jnp.concatenate([jnp.concatenate(part, axis=1) for part in parts], axis=0)
    got = dot_table(table_ref, columns, 512, 256)
    within = lane_of((64, LANES)) % 16
    packed = [jnp.zeros((64, LANES), f32)] * 4
    for pair in range(2):
        found = got[:, LANES * pair : LANES * (pair + 1)]
        found = found + roll(found, -4, 1)
        for step in range(4):
            for one in range(2):
                j = 4 * step + 2 * pair + one
                moved = roll(found[64 * step : 64 * (step + 1)], j - 8 * one, 1)
                for c in range(4):
                    packed[c] = jnp.where(within == (j + c) % 16, moved, packed[c])
    for half in range(2):
        pressure = roll(packed[2 * half], -2 * half, 1)
        change_up = roll(packed[2 * half + 1], -(2 * half + 1), 1)
        before = jnp.where(
            within > 0, roll(pressure, 1, 1), roll(roll(pressure, 1, 0), -15, 1)
        )
        for field, value in enumerate((pressure, change_up, before - pressure)):
            out_ref[pl.ds(3 * half + field, 64, stride=6), :] = value


CHUNK = 1024


def unit_rows(shape, axis):
    return lax.broadcasted_iota(jnp.int32, shape, axis) % 8


def same_row(value):
    shape = value.shape
    return jnp.where(unit_rows(shape, 0) == unit_rows(shape, 1), value, 0.0)


def gather(shape, step):
    to = lax.broadcasted_iota(jnp.int32, shape, 1)
    return (lax.broadcasted_iota(jnp.int32, shape, 0) // step == to).astype(f32)


def exact(a, b):
    return jnp.dot(a, b, precision=lax.Precision.HIGHEST, preferred_element_type=f32)


def spread(weight, columns):
    tall, wide = weight.shape
    step = (
        lax.broadcasted_iota(jnp.int32, (wide, columns), 1) // 8
        == lax.broadcasted_iota(jnp.int32, (wide, columns), 0)
    ).astype(f32)
    value = exact(weight, step)
    value = jnp.broadcast_to(value[:, None, :], (tall, 8, columns)).reshape(8 * tall, columns)
    return same_row(value)


def closure_forward(win_hbm, bin_hbm, wmid_hbm, bmid_hbm, wout_hbm, spacing_hbm,
                    vel_hbm, buoy_hbm, fixed_hbm, mark_ref,
                    first_hbm, second_hbm, wide_hbm, turn_hbm, done_ref,
                    win_ref, bin_ref, wmid_ref, bmid_ref, wout_ref, spacing_ref,
                    vel_ref, buoy_ref, turn_ref, first_ref, second_ref, wide_ref, sems, out_sems):
    sources = (win_hbm, bin_hbm, wmid_hbm, bmid_hbm, wout_hbm, spacing_hbm)
    sources += (vel_hbm, buoy_hbm, fixed_hbm)
    targets = (win_ref, bin_ref, wmid_ref, bmid_ref, wout_ref, spacing_ref)
    targets += (vel_ref, buoy_ref, turn_ref)
    copies = [start_copy(*pair, sems, i) for i, pair in enumerate(zip(sources, targets))]
    for copy in copies[:6]:
        copy.wait()
    win_t = win_ref[...]
    wmid = wmid_ref[...]
    wout_h, wout_l = split_f32(spread(wout_ref[...].T, 32))
    wide_ref[0:256, 0:96] = jnp.concatenate([wout_h, wout_h, wout_l], axis=1).astype(bf16)
    wide_ref[0:256, 96:128] = jnp.zeros((256, 32), bf16)
    wide_ref[0:256, 128:384], wide_ref[0:256, 384:640] = split(spread(wmid.T, 256))
    wide_ref[256:288, 0:128] = jnp.zeros((32, 128), bf16)
    wide_ref[256:288, 128:384], wide_ref[256:288, 384:640] = split(spread(win_t, 256))
    win_h, win_l = split_f32(spread(win_t.T, 32))
    win_cat = jnp.concatenate([win_h, win_h, win_l], axis=1).astype(bf16)
    wmh, wml = split(spread(wmid, 256))

    def tall(row):
        column = row.T
        return jnp.broadcast_to(column[:, None, :], (32, 8, 1)).reshape(256, 1)

    b_in, b_mid = tall(bin_ref[...]), tall(bmid_ref[...])
    for copy in copies[6:]:
        copy.wait()
    own = turn_ref[pl.ds(512 + lax.axis_index(PLANE), 1), :]
    turn_ref[256:512] = turn_ref[256:512] + own
    for i, rows in enumerate(vertical([spacing_ref[:, k : k + 1] for k in range(LEVELS)])):
        turn_ref[512 + 8 * i : 520 + 8 * i] = jnp.concatenate(rows, axis=0)
    copies = [
        start_copy(wide_ref, wide_hbm, out_sems, 0),
        start_copy(turn_ref, turn_hbm, out_sems, 1),
    ]
    width = buoy_ref.shape[-1]
    for half in range(2):
        part = slice(8 * half, 8 * (half + 1))
        for start in range(0, width, CHUNK):
            col = slice(start, start + CHUNK)
            to = slice(half * width + start, half * width + start + CHUNK)
            feats = jnp.concatenate(
                [vel_ref[c, 0, part, col] for c in range(3)] + [buoy_ref[0, part, col]], axis=0
            )
            high, low = split_f32(feats)
            stack = jnp.concatenate([high, low, high], axis=0).astype(bf16)
            first_ref[512:608, to] = jnp.concatenate(
                [high, low, jnp.ones((32, CHUNK), f32)], axis=0
            ).astype(bf16)
            first = jnp.tanh(dot(win_cat, stack) + b_in)
            fh, fl = split(first)
            first_ref[0:256, to] = fh
            first_ref[256:512, to] = fl
            second = dot(wmh, fh) + dot(wmh, fl) + dot(wml, fh)
            second = jnp.tanh(second + b_mid)
            sh, sl = split(second)
            second_ref[0:256, to] = sh
            second_ref[256:512, to] = sl
        whole = slice(half * width, (half + 1) * width)
        for i, (held, target) in enumerate(((first_ref, first_hbm), (second_ref, second_hbm))):
            copies.append(
                start_copy(held.at[:, whole], target.at[:, whole], out_sems, 2 + 2 * half + i)
            )
    done_ref[...] = jnp.zeros(done_ref.shape, f32)
    for copy in copies:
        copy.wait()


def closure_back(msg_ref, turn_ref, second_ref, table_ref, cot_ref, mask_ref, first_ref,
                 wide_ref, total_ref, gvel_hbm, gbuoy_hbm,
                 line_ref, e1h_ref, e1l_ref, e2h_ref, e2l_ref, dl_ref, b2_ref,
                 gvel_ref, gbuoy_ref, out_sems):
    width = mask_ref.shape[-1]
    lane = lane_of((LANES, LANES))
    halves = []
    items = [msg_ref[pl.ds(field, LANES, stride=3), :] for field in range(3)]
    for t in range(8):
        value = jnp.zeros((LANES, LANES), f32)
        for field, item in enumerate(items):
            value = jnp.where(lane // 16 == field, roll(item, 16 * (field - t), 1), value)
        halves.append(value)
    cos_r, sin_r = part_back(
        [jnp.concatenate(halves[2 * i : 2 * i + 2], axis=0) for i in range(4)]
    )
    parts = ([], [])
    for r in range(4):
        pair = (cos_r[r], sin_r[r])
        if r > 0:
            cos_turn, sin_turn = turn_of(turn_ref, r)
            pair = turn(*pair, cos_turn, -sin_turn)
        for i, value in enumerate(pair):
            high, low = split_f32(value)
            parts[i].append((high + roll(low, 64, 1)).astype(bf16))
    columns = jnp.concatenate([jnp.concatenate(part, axis=1) for part in parts], axis=0)
    found = dot_table(table_ref, columns, 0, 256)
    for r in range(4):
        block = found[:, LANES * r : LANES * (r + 1)]
        line_ref[pl.ds(r, 256, stride=4), :] = block + roll(block, 64, 1)
    field = line_ref[...].T
    pressure = field[0:16]
    east_back = roll(pressure, 1, 1) - pressure
    projected = (
        cot_ref[0, 0] - east_back,
        cot_ref[1, 0] - field[32:48],
        cot_ref[2, 0] - field[16:32],
    )
    wet = mask_ref[0].astype(f32)
    out_copies = []
    deltas = [value * wet for value in projected]
    blank = jnp.zeros((8, CHUNK), f32)
    bias2 = jnp.zeros((256, LANES), f32)
    for half in range(2):
        part = slice(8 * half, 8 * (half + 1))
        for start in range(0, width, CHUNK):
            col = slice(start, start + CHUNK)
            to = slice(half * width + start, half * width + start + CHUNK)
            delta = jnp.concatenate([value[part, col] for value in deltas] + [blank], axis=0)
            dh, dl = split_f32(delta)
            stack = jnp.concatenate([dh, dl, dh], axis=0).astype(bf16)
            dl_ref[:, to] = stack[0:64]
            second = second_ref[0:256, to].astype(f32) + second_ref[256:512, to].astype(f32)
            err2 = dot(wide_ref[0:256, 0:96], stack) * (1.0 - second * second)
            bias2 = bias2 + sum(err2[:, LANES * i : LANES * (i + 1)] for i in range(CHUNK // LANES))
            e2h, e2l = split(err2)
            e2h_ref[:, to] = e2h
            e2l_ref[:, to] = e2l
            first = first_ref[0:256, to].astype(f32) + first_ref[256:512, to].astype(f32)
            err1 = (
                dot(wide_ref[0:256, 128:384], e2h)
                + dot(wide_ref[0:256, 128:384], e2l)
                + dot(wide_ref[0:256, 384:640], e2h)
            )
            err1 = err1 * (1.0 - first * first)
            e1h, e1l = split(err1)
            e1h_ref[:, to] = e1h
            e1l_ref[:, to] = e1l
            out = (
                dot(wide_ref[256:288, 128:384], e1h)
                + dot(wide_ref[256:288, 128:384], e1l)
                + dot(wide_ref[256:288, 384:640], e1h)
            )
            for c in range(3):
                gvel_ref[c, 0, part, col] = projected[c][part, col] + out[8 * c : 8 * (c + 1)]
            gbuoy_ref[0, part, col] = out[24:32]
        out_copies += [
            start_copy(gvel_ref.at[:, :, part, :], gvel_hbm.at[:, :, part, :], out_sems, 2 * half),
            start_copy(gbuoy_ref.at[:, part, :], gbuoy_hbm.at[:, part, :], out_sems, 2 * half + 1),
        ]
    b2_ref[...] = bias2
    mid = (
        dot_nt(e2h_ref[...], first_ref[0:256])
        + dot_nt(e2h_ref[...], first_ref[256:512])
        + dot_nt(e2l_ref[...], first_ref[0:256])
    )
    both1 = dot_nt(first_ref[512:608], e1h_ref[...])
    rest1 = dot_nt(first_ref[512:608], e1l_ref[...])
    win = both1[0:32] + both1[32:64] + rest1[0:32]
    bin_ = both1[64:65] + rest1[64:65]
    both2 = dot_nt(dl_ref[...], second_ref[0:256])
    rest2 = dot_nt(dl_ref[...], second_ref[256:512])
    wout = both2[0:32] + both2[32:64] + rest2[0:32]

    def fold_rows(value):
        return jnp.sum(value.reshape(value.shape[0] // 8, 8, value.shape[1]), axis=1)

    to_unit = gather((256, LANES), 8)
    mid = exact(fold_rows(same_row(mid)), to_unit)
    small = [fold_rows(same_row(win)), fold_rows(same_row(wout)), bin_, jnp.zeros((7, 256), f32)]
    small = exact(jnp.concatenate(small, axis=0), to_unit)
    b2 = lax.dot_general(
        jnp.ones((8, LANES), f32),
        fold_rows(b2_ref[...]),
        (((1,), (1,)), ((), ())),
        precision=lax.Precision.HIGHEST,
        preferred_element_type=f32,
    )
    units = jnp.concatenate([mid[8 * i : 8 * (i + 1), 0:32] for i in range(4)], axis=1)
    rows = [units[i : i + 1] for i in range(8)]
    rows.append(jnp.concatenate([small[i : i + 1, 0:32] for i in range(4)], axis=1))
    rows.append(
        jnp.concatenate([small[i : i + 1, 0:32] for i in range(4, 7)] + [b2[0:1]], axis=1)
    )
    rows.append(small[8:9])
    rows = jnp.concatenate(rows, axis=0)
    for peer in range(32):
        total_ref[11 * peer : 11 * (peer + 1), :] = rows
    for copy in out_copies:
        copy.wait()


def sum_rows(got_ref):
    return [
        jnp.sum(got_ref[pl.ds(i, got_ref.shape[0] // 11, stride=11), :], axis=0, keepdims=True)
        for i in range(11)
    ]


def sum_slab(got_ref, out_ref):
    total = jnp.concatenate(sum_rows(got_ref), axis=0)
    for peer in range(16):
        out_ref[11 * peer : 11 * (peer + 1), :] = total


def sum_column(scale, got_ref, win_ref, bin_ref, wmid_ref, bmid_ref, wout_ref):
    rows = [row * scale for row in sum_rows(got_ref)]
    units = jnp.concatenate(rows[:8], axis=0)
    wmid_ref[...] = jnp.concatenate([units[:, 32 * i : 32 * (i + 1)] for i in range(4)], axis=0)
    win_ref[...] = jnp.concatenate([rows[8][:, 32 * i : 32 * (i + 1)] for i in range(4)], axis=0)
    wout_ref[...] = jnp.concatenate([rows[9][:, 32 * i : 32 * (i + 1)] for i in range(3)], axis=0)
    bmid_ref[...] = rows[9][:, 96:128]
    bin_ref[...] = rows[10][:, 0:32]


def trade(rows, peers, axes):
    size = rows.shape[0] // peers * LANES
    got = lax.all_to_all(rows.reshape(peers, 1, size), axes, 0, 0)
    return got.reshape(rows.shape)


def shards(velocity, buoyancy, cell_mask, spacing, cotangent, w_in, b_in, w_mid, b_mid, w_out):
    levels, rows, width = buoyancy.shape
    depth = spacing.shape[0]
    span_y = rows * 64
    table = dft_table(256, 1024)
    table_y = table[:, (np.arange(256) % 64) * 4 + np.arange(256) // 64]
    x_table, y_table = jnp.asarray(two_parts(table)), jnp.asarray(two_parts(table_y))
    backs = jnp.asarray(np.concatenate([two_parts(table.T), two_parts(table_y.T)], axis=0))
    eigen = eigenvalue(width)
    lanes = np.arange(LANES)
    ey = eigen.reshape(4, 4, 64)[lanes % 16 // 4, lanes % 4].T.astype(np.float32)
    ey = np.concatenate([ey, np.zeros((192, LANES), np.float32)], axis=0)
    ex = eigen[np.arange(128)[:, None] + 128 * (lanes[None, :] // 16)].astype(np.float32)
    turns = twiddles(256, 1024)
    fixed = jnp.asarray(np.concatenate([turns, ey, ex], axis=0))
    turns = jnp.asarray(turns)
    cells = rows * width // 8
    dma = pltpu.SemaphoreType.DMA
    type_of = jax.ShapeDtypeStruct
    table = pltpu.VMEM((1024, 256), bf16)
    back_tables = pltpu.VMEM((1024, 512), bf16)
    turn_held = pltpu.VMEM((640, LANES), f32)
    first_held = pltpu.VMEM((608, cells), bf16)
    second_held = pltpu.VMEM((512, cells), bf16)
    wide = pltpu.VMEM((256, cells), bf16)
    wide_held = pltpu.VMEM((288, 640), bf16)
    mark_type = type_of((8, LANES), f32)
    table_flops = 4 * 512 * 256 * 512
    msg_type = type_of((128 * 3, LANES), f32)
    msg, mark = call(
        forward_x,
        (msg_type, mark_type),
        (cotangent, x_table, turns),
        hbm=(0, 1, 2),
        scratch=(
            table,
            pltpu.VMEM((256, LANES), f32),
            pltpu.VMEM(cotangent.shape, f32),
            pltpu.VMEM((1024, LANES), f32),
            dma((3,)),
        ),
        flops=table_flops,
        name="forward_x",
    )
    msg = trade(msg, 128, PLANE)

    first, second, weights, turns, mark = call(
        closure_forward,
        (
            pltpu.HBM((608, cells), bf16),
            pltpu.HBM((512, cells), bf16),
            pltpu.HBM((288, 640), bf16),
            pltpu.HBM((640, LANES), f32),
            mark_type,
        ),
        (w_in.T, b_in[None], w_mid, b_mid[None], w_out, spacing[None])
        + (velocity, buoyancy, fixed, mark),
        hbm=range(9),
        hbm_out=range(4),
        scratch=(
            pltpu.VMEM((4, 32), f32),
            pltpu.VMEM((1, 32), f32),
            pltpu.VMEM((32, 32), f32),
            pltpu.VMEM((1, 32), f32),
            pltpu.VMEM((3, 32), f32),
            pltpu.VMEM((1, LEVELS), f32),
            pltpu.VMEM(velocity.shape, f32),
            pltpu.VMEM(buoyancy.shape, f32),
            turn_held,
            first_held,
            second_held,
            wide_held,
            dma((9,)),
            dma((6,)),
        ),
        flops=2 * 256 * 256 * cells * 4,
        name="closure_forward",
    )
    gathered, turns, backs, weights = call(
        forward_y,
        (type_of((4, 256, LANES), f32), turn_held, back_tables, wide_held),
        (msg, y_table, turns, backs, weights, mark),
        hbm=(1, 2, 3, 4),
        scratch=(table, dma((4,))),
        flops=table_flops,
        name="forward_y",
    )
    gathered = lax.all_to_all(gathered, "x", 0, 0)
    (msg,) = call(
        solve_back,
        (msg_type,),
        (gathered, turns, backs),
        flops=table_flops,
        name="solve_back",
    )
    msg = trade(msg, 128, PLANE)
    totals, grad_velocity, grad_buoyancy = call(
        closure_back,
        (
            type_of((32 * 11, LANES), f32),
            pltpu.HBM(cotangent.shape, f32),
            pltpu.HBM(buoyancy.shape, f32),
        ),
        (msg, turns, second, backs, cotangent, cell_mask, first, weights),
        hbm_out=(1, 2),
        scratch=(
            pltpu.VMEM((1024, LANES), f32),
            wide,
            wide,
            wide,
            wide,
            pltpu.VMEM((64, cells), bf16),
            pltpu.VMEM((256, LANES), f32),
            pltpu.VMEM(cotangent.shape, f32),
            pltpu.VMEM(buoyancy.shape, f32),
            dma((4,)),
        ),
        flops=table_flops + 2 * 256 * 256 * cells * 10,
        name="closure_back",
    )
    totals = trade(totals, 32, SLAB)
    (totals,) = call(sum_slab, (type_of((16 * 11, LANES), f32),), (totals,), name="sum_slab")
    totals = trade(totals, 16, COLUMN)
    scale = 1.0 / math.sqrt(width * span_y * depth)
    grad_in, grad_b_in, grad_mid, grad_b_mid, grad_out = call(
        functools.partial(sum_column, scale),
        (
            type_of((4, 32), f32),
            type_of((1, 32), f32),
            type_of((32, 32), f32),
            type_of((1, 32), f32),
            type_of((3, 32), f32),
        ),
        (totals,),
        name="sum_column",
    )
    return (
        grad_velocity,
        grad_buoyancy,
        grad_in.T,
        grad_b_in[0],
        grad_mid,
        grad_b_mid[0],
        grad_out,
    )


def solution(mesh):
    fine = Mesh(
        mesh.devices.reshape([size for _, size in FINE]), tuple(name for name, _ in FINE)
    )
    field = P(None, NARROW, WIDE, None)
    cell = P(NARROW, WIDE, None)
    in_specs = (field, cell, cell, P(), field, P(), P(), P(), P(), P())
    out_specs = (field, cell, P(), P(), P(), P(), P())
    return jax.shard_map(shards, mesh=fine, in_specs=in_specs, out_specs=out_specs, check_vma=False)
```

```python
import functools
import math

import jax
import jax.numpy as jnp
import ml_dtypes
import numpy as np
from jax import lax
from jax.experimental import pallas as pl
from jax.experimental.pallas import tpu as pltpu
from jax.sharding import Mesh
from jax.sharding import PartitionSpec as P

free_surface = 0.05
f32 = jnp.float32
bf16 = jnp.bfloat16
LANES = 128
LEVELS = 8
VMEM_LIMIT = 24 * 1024 * 1024

FINE = (("y", 4), ("zl", 8), ("c", 2), ("zh", 2), ("x", 4))
WIDE = ("y", "zl", "c")
NARROW = ("zh", "x")
PLANE = ("y", "zl", "c", "zh")
SLAB = ("y", "x", "c")
COLUMN = ("zh", "zl")


def dft_table(count, length):
    indices = np.arange(count)
    angle = 2.0 * np.pi / count * (indices[:, None] * indices[None, :] % count)
    return np.concatenate([np.cos(angle), np.sin(angle)], axis=0) * np.sqrt(2.0 / length)


def twiddles(count, length):
    angle = 2.0 * np.pi / length * np.arange(count)[:, None] * np.arange(4)[None, :]
    held = np.zeros((count, LANES))
    held[:, 0:8:2] = np.cos(angle)
    held[:, 1:8:2] = np.sin(angle)
    return held.astype(np.float32)


def wavenumbers(length):
    half = np.arange(length // 2)
    return np.concatenate([half, np.where(half == 0, length // 2, half)])


def two_parts(table):
    high = table.astype(np.float32).astype(ml_dtypes.bfloat16)
    low = (table - high.astype(np.float64)).astype(np.float32).astype(ml_dtypes.bfloat16)
    return np.concatenate([high, low], axis=0)


def eigenvalue(length):
    return -4.0 * np.sin(np.pi / length * wavenumbers(length)) ** 2


def split(value):
    high = value.astype(bf16)
    low = (value - high.astype(f32)).astype(bf16)
    return high, low


def split_f32(value):
    high = value.astype(bf16).astype(f32)
    return high, value - high


def dot(a, b):
    return jnp.dot(a, b, preferred_element_type=f32)


def dot_table(table_ref, b, start, rows):
    middle = start + rows
    return dot(table_ref[start:middle], b) + dot(table_ref[middle : middle + rows], b)


def dot_nt(a, b):
    return lax.dot_general(a, b, (((1,), (1,)), ((), ())), preferred_element_type=f32)


def roll(value, shift, axis):
    size = value.shape[axis]
    shift = shift % size
    return value if shift == 0 else pltpu.roll(value, shift, axis)


def lane_of(shape):
    return lax.broadcasted_iota(jnp.int32, shape, len(shape) - 1)


def start_copy(source, target, sems, index):
    copy = pltpu.make_async_copy(source, target, sems.at[index])
    copy.start()
    return copy


def call(kernel, out_shape, args, smem=(), hbm=(), hbm_out=(), scratch=(), flops=0, name=None):
    def space(index, held):
        return pl.BlockSpec(memory_space=held.get(index, pltpu.VMEM))

    held = {i: pltpu.SMEM for i in smem} | {i: pl.ANY for i in hbm}
    args = [
        pltpu.with_memory_space_constraint(a, pltpu.HBM) if i in hbm else a
        for i, a in enumerate(args)
    ]
    moved = sum(int(np.prod(a.shape)) * a.dtype.itemsize for a in args)
    return pl.pallas_call(
        kernel,
        out_shape=out_shape,
        in_specs=[space(i, held) for i in range(len(args))],
        out_specs=[space(i, {o: pl.ANY for o in hbm_out}) for i in range(len(out_shape))],
        scratch_shapes=list(scratch),
        compiler_params=pltpu.CompilerParams(vmem_limit_bytes=VMEM_LIMIT),
        cost_estimate=pl.CostEstimate(flops=flops, bytes_accessed=moved, transcendentals=0),
        name=name,
    )(*args)


def first_row(shape):
    return lax.broadcasted_iota(jnp.int32, shape, 0) == 0


def join(cos_r, sin_r):
    even_c, even_s = cos_r[0] + cos_r[2], sin_r[0] + sin_r[2]
    odd_c, odd_s = cos_r[1] + cos_r[3], sin_r[1] + sin_r[3]
    top = first_row(even_c.shape)
    ends = jnp.where(top, math.sqrt(0.5), 1.0)
    return (
        (even_c + odd_c) * ends,
        cos_r[0] - cos_r[2] - (sin_r[1] - sin_r[3]),
        jnp.where(top, even_c - odd_c, even_s + odd_s) * ends,
        sin_r[0] - sin_r[2] + (cos_r[1] - cos_r[3]),
    )


def part_back(blocks):
    top = first_row(blocks[0].shape)
    ends = jnp.where(top, math.sqrt(0.5), 1.0)
    low_c, high_c, low_s, high_s = blocks
    low_c, low_s = low_c * ends, low_s * ends
    last = jnp.where(top, low_s, 0.0)
    low_s = jnp.where(top, 0.0, low_s)
    even, odd = low_c + last, low_c - last
    return (
        (even + high_c, odd + high_s, even - high_c, odd - high_s),
        (low_s + high_s, low_s - high_c, low_s - high_s, low_s + high_c),
    )


def turn(cos_part, sin_part, cos_turn, sin_turn):
    return cos_part * cos_turn - sin_part * sin_turn, sin_part * cos_turn + cos_part * sin_turn


def turn_of(turn_ref, remainder):
    rows, shape = slice(0, 256), (256, LANES)
    return (
        jnp.broadcast_to(turn_ref[rows, 2 * remainder : 2 * remainder + 1], shape),
        jnp.broadcast_to(turn_ref[rows, 2 * remainder + 1 : 2 * remainder + 2], shape),
    )


def forward_x(cot_hbm, table_hbm, turn_hbm, out_ref, mark_ref,
              table_ref, turn_ref, cot_ref, line_ref, sems):
    first = start_copy(cot_hbm, cot_ref, sems, 0)
    copies = [
        start_copy(table_hbm, table_ref, sems, 1),
        start_copy(turn_hbm, turn_ref, sems, 2),
    ]
    first.wait()
    east, north, up = cot_ref[0, 0], cot_ref[1, 0], cot_ref[2, 0]
    rows, width = east.shape
    east = east - roll(east, -1, 1)
    high, low = split_f32(jnp.concatenate([east, north, up], axis=0))
    none = jnp.zeros((rows, width), f32)
    line_ref[...] = jnp.concatenate([high, none, low, none], axis=0).T
    lines = jnp.concatenate(
        [line_ref[pl.ds(r, 256, stride=4), :].astype(bf16) for r in range(4)], axis=1
    )
    for copy in copies:
        copy.wait()
    got = dot_table(table_ref, lines, 0, 512)
    cos_r, sin_r = [], []
    for r in range(4):
        cos_part = got[0:256, LANES * r : LANES * (r + 1)]
        sin_part = got[256:512, LANES * r : LANES * (r + 1)]
        if r > 0:
            cos_part, sin_part = turn(cos_part, sin_part, *turn_of(turn_ref, r))
        cos_r.append(cos_part)
        sin_r.append(sin_part)
    blocks = [block + roll(block, 64, 1) for block in join(cos_r, sin_r)]
    lane = lane_of((LANES, LANES))
    for field in range(3):
        packed = jnp.zeros((LANES, LANES), f32)
        for t in range(8):
            block = blocks[t // 2][LANES * (t % 2) : LANES * (t % 2 + 1)]
            packed = jnp.where(lane // 16 == t, roll(block, 16 * (t - field), 1), packed)
        out_ref[pl.ds(field, LANES, stride=3), :] = packed
    mark_ref[...] = jnp.zeros(mark_ref.shape, f32)


def pair_turns(turn_ref, pair, within):
    one, two = turn_of(turn_ref, 2 * pair), turn_of(turn_ref, 2 * pair + 1)
    return tuple(jnp.where(within < 8, a, b) for a, b in zip(one, two))


def forward_y(msg_ref, table_hbm, turn_hbm, back_hbm, wide_hbm, mark_ref,
              out_ref, turn_ref, back_ref, wide_ref, table_ref, sems):
    copies = [
        start_copy(table_hbm, table_ref, sems, 0),
        start_copy(turn_hbm, turn_ref, sems, 1),
    ]
    later_copies = [
        start_copy(back_hbm, back_ref, sems, 2),
        start_copy(wide_hbm, wide_ref, sems, 3),
    ]
    within = lane_of((64, LANES)) % 16
    highs = []
    lows = []
    for half in range(2):
        east, north, up = (
            msg_ref[pl.ds(3 * half + field, 64, stride=6), :] for field in range(3)
        )
        after = jnp.where(
            within < 15, roll(north, -1, 1), roll(roll(north, -1, 0), 15, 1)
        )
        for value in (east + north - after, up):
            high, low = split_f32(value)
            highs.append(high)
            lows.append(low)
    shifted = [roll(value, c, 1) for c, value in enumerate(highs + lows)]

    def line_of(j, to):
        line = shifted[0]
        for c in range(1, 8):
            line = jnp.where(within == (c + j) % 16, shifted[c], line)
        return roll(line, to - j, 1)

    lines = []
    for pair in range(2):
        rows = []
        for step in range(4):
            j = 4 * step + 2 * pair
            rows.append(jnp.where(within < 8, line_of(j, 0), line_of(j + 1, 8)).astype(bf16))
        lines.append(jnp.concatenate(rows, axis=0))
    lines = jnp.concatenate(lines, axis=1)
    for copy in copies:
        copy.wait()
    got = dot_table(table_ref, lines, 0, 512)
    within = lane_of((256, LANES)) % 16
    turned = [
        turn(
            got[0:256, LANES * pair : LANES * (pair + 1)],
            got[256:512, LANES * pair : LANES * (pair + 1)],
            *pair_turns(turn_ref, pair, within),
        )
        for pair in range(2)
    ]
    cos_r = [turned[0][0], roll(turned[0][0], -8, 1), turned[1][0], roll(turned[1][0], -8, 1)]
    sin_r = [turned[0][1], roll(turned[0][1], -8, 1), turned[1][1], roll(turned[1][1], -8, 1)]
    packed = jnp.zeros((256, LANES), f32)
    for g, block in enumerate(join(cos_r, sin_r)):
        block = block + roll(block, -4, 1)
        packed = jnp.where(within // 4 == g, roll(block, 4 * g, 1), packed)
    for peer in range(4):
        out_ref[peer] = packed
    for copy in later_copies:
        copy.wait()


def vertical(spacing):
    one = jnp.ones((1, LANES), f32)
    none = jnp.zeros((1, LANES), f32)
    spacing = [one * spacing[k] for k in range(LEVELS)]
    inv_dz = [1.0 / value for value in spacing]
    face = [2.0 / (spacing[k] + spacing[k + 1]) for k in range(LEVELS - 1)] + [none]
    lower = [none] + [inv_dz[k] * face[k - 1] for k in range(1, LEVELS)]
    upper = [inv_dz[k] * face[k] for k in range(LEVELS)]
    base = [-(lower[k] + upper[k]) for k in range(LEVELS)]
    base[-1] = base[-1] - free_surface * inv_dz[-1]
    sub = [none] + upper[:-1]
    sup = lower[1:] + [none]
    keep = [one] * (LEVELS - 1) + [none]
    return inv_dz, face, sub, base, sup, keep


def solve_back(got_ref, turn_ref, table_ref, out_ref):
    at = lax.axis_index("x")
    rows = got_ref.shape[1]
    lam = turn_ref[256 : 256 + rows // 4]
    lane = lane_of((rows, LANES))
    column = lane_of(lam.shape) % 4
    inv_dz, face, sub, base, sup, keep = (
        [turn_ref[512 + 8 * i + k : 513 + 8 * i + k] for k in range(LEVELS)]
        for i in range(6)
    )
    quarters = [slice(rows // 4 * r, rows // 4 * (r + 1)) for r in range(4)]

    def gathered(k, field):
        at_lane = 2 * (k // 4) + field
        value = roll(got_ref[k % 4, quarters[0], :], -at_lane, 1)
        for r in range(1, 4):
            moved = roll(got_ref[k % 4, quarters[r], :], r - at_lane, 1)
            value = jnp.where(column == r, moved, value)
        return value

    ratios = []
    values = []
    below = None
    for k in range(LEVELS):
        flux = gathered(k, 1) * face[k]
        right = gathered(k, 0) - flux
        if k > 0:
            right = right + below
        below = flux
        diagonal = lam + base[k]
        if k > 0:
            diagonal = diagonal - sub[k] * ratios[-1]
            right = right - sub[k] * values[-1]
        inverse = 1.0 / diagonal
        ratios.append(sup[k] * inverse)
        values.append(right * inverse)
    result = [None] * LEVELS
    result[-1] = values[-1]
    for k in range(LEVELS - 2, -1, -1):
        result[k] = values[k] - ratios[k] * result[k + 1]
    scaled = [result[k] * inv_dz[k] for k in range(LEVELS)] + [jnp.zeros_like(lam)]
    change = [(scaled[k] - scaled[k + 1]) * keep[k] for k in range(LEVELS)]

    def own(items, half):
        value = items[4 * half]
        for x in range(1, 4):
            value = jnp.where(at == x, items[4 * half + x], value)
        return value

    fields = [own(result, 0), own(change, 0), own(result, 1), own(change, 1)]
    both = []
    for r in range(4):
        value = roll(fields[0], -r, 1)
        for c in range(1, 4):
            value = jnp.where(column == c, roll(fields[c], c - r, 1), value)
        both.append(value)
    both = jnp.concatenate(both, axis=0)
    within = lane % 16
    blocks = []
    for g in range(4):
        block = roll(both, -4 * g, 1)
        blocks.append(jnp.where(within < 8, block, roll(block, 8, 1)))
    cos_r, sin_r = part_back(blocks)
    parts = ([], [])
    for pair in range(2):
        cos_part = jnp.where(within < 8, cos_r[2 * pair], cos_r[2 * pair + 1])
        sin_part = jnp.where(within < 8, sin_r[2 * pair], sin_r[2 * pair + 1])
        cos_turn, sin_turn = pair_turns(turn_ref, pair, within)
        for i, value in enumerate(turn(cos_part, sin_part, cos_turn, -sin_turn)):
            high, low = split_f32(jnp.where(within % 8 < 4, value, 0.0))
            parts[i].append((high + roll(low, 4, 1)).astype(bf16))
    columns = jnp.concatenate([jnp.concatenate(part, axis=1) for part in parts], axis=0)
    got = dot_table(table_ref, columns, 512, 256)
    within = lane_of((64, LANES)) % 16
    packed = [jnp.zeros((64, LANES), f32)] * 4
    for pair in range(2):
        found = got[:, LANES * pair : LANES * (pair + 1)]
        found = found + roll(found, -4, 1)
        for step in range(4):
            for one in range(2):
                j = 4 * step + 2 * pair + one
                moved = roll(found[64 * step : 64 * (step + 1)], j - 8 * one, 1)
                for c in range(4):
                    packed[c] = jnp.where(within == (j + c) % 16, moved, packed[c])
    for half in range(2):
        pressure = roll(packed[2 * half], -2 * half, 1)
        change_up = roll(packed[2 * half + 1], -(2 * half + 1), 1)
        before = jnp.where(
            within > 0, roll(pressure, 1, 1), roll(roll(pressure, 1, 0), -15, 1)
        )
        for field, value in enumerate((pressure, change_up, before - pressure)):
            out_ref[pl.ds(3 * half + field, 64, stride=6), :] = value


CHUNK = 1024


def unit_rows(shape, axis):
    return lax.broadcasted_iota(jnp.int32, shape, axis) % 8


def same_row(value):
    shape = value.shape
    return jnp.where(unit_rows(shape, 0) == unit_rows(shape, 1), value, 0.0)


def gather(shape, step):
    to = lax.broadcasted_iota(jnp.int32, shape, 1)
    return (lax.broadcasted_iota(jnp.int32, shape, 0) // step == to).astype(f32)


def exact(a, b):
    return jnp.dot(a, b, precision=lax.Precision.HIGHEST, preferred_element_type=f32)


def spread(weight, columns):
    tall, wide = weight.shape
    step = (
        lax.broadcasted_iota(jnp.int32, (wide, columns), 1) // 8
        == lax.broadcasted_iota(jnp.int32, (wide, columns), 0)
    ).astype(f32)
    value = exact(weight, step)
    value = jnp.broadcast_to(value[:, None, :], (tall, 8, columns)).reshape(8 * tall, columns)
    return same_row(value)


def closure_forward(win_hbm, bin_hbm, wmid_hbm, bmid_hbm, wout_hbm, spacing_hbm,
                    vel_hbm, buoy_hbm, fixed_hbm, mark_ref,
                    first_hbm, second_hbm, wide_hbm, turn_hbm, done_ref,
                    win_ref, bin_ref, wmid_ref, bmid_ref, wout_ref, spacing_ref,
                    vel_ref, buoy_ref, turn_ref, first_ref, second_ref, wide_ref, sems, out_sems):
    sources = (win_hbm, bin_hbm, wmid_hbm, bmid_hbm, wout_hbm, spacing_hbm)
    sources += (vel_hbm, buoy_hbm, fixed_hbm)
    targets = (win_ref, bin_ref, wmid_ref, bmid_ref, wout_ref, spacing_ref)
    targets += (vel_ref, buoy_ref, turn_ref)
    copies = [start_copy(*pair, sems, i) for i, pair in enumerate(zip(sources, targets))]
    for copy in copies[:6]:
        copy.wait()
    win_t = win_ref[...]
    wmid = wmid_ref[...]
    wout_h, wout_l = split_f32(spread(wout_ref[...].T, 32))
    wide_ref[0:256, 0:96] = jnp.concatenate([wout_h, wout_h, wout_l], axis=1).astype(bf16)
    wide_ref[0:256, 96:128] = jnp.zeros((256, 32), bf16)
    wide_ref[0:256, 128:384], wide_ref[0:256, 384:640] = split(spread(wmid.T, 256))
    wide_ref[256:288, 0:128] = jnp.zeros((32, 128), bf16)
    wide_ref[256:288, 128:384], wide_ref[256:288, 384:640] = split(spread(win_t, 256))
    win_h, win_l = split_f32(spread(win_t.T, 32))
    win_cat = jnp.concatenate([win_h, win_h, win_l], axis=1).astype(bf16)
    wmh, wml = split(spread(wmid, 256))

    def tall(row):
        column = row.T
        return jnp.broadcast_to(column[:, None, :], (32, 8, 1)).reshape(256, 1)

    b_in, b_mid = tall(bin_ref[...]), tall(bmid_ref[...])
    for copy in copies[6:]:
        copy.wait()
    own = turn_ref[pl.ds(512 + lax.axis_index(PLANE), 1), :]
    turn_ref[256:512] = turn_ref[256:512] + own
    for i, rows in enumerate(vertical([spacing_ref[:, k : k + 1] for k in range(LEVELS)])):
        turn_ref[512 + 8 * i : 520 + 8 * i] = jnp.concatenate(rows, axis=0)
    copies = [
        start_copy(wide_ref, wide_hbm, out_sems, 0),
        start_copy(turn_ref, turn_hbm, out_sems, 1),
    ]
    width = buoy_ref.shape[-1]
    for half in range(2):
        part = slice(8 * half, 8 * (half + 1))
        for start in range(0, width, CHUNK):
            col = slice(start, start + CHUNK)
            to = slice(half * width + start, half * width + start + CHUNK)
            feats = jnp.concatenate(
                [vel_ref[c, 0, part, col] for c in range(3)] + [buoy_ref[0, part, col]], axis=0
            )
            high, low = split_f32(feats)
            stack = jnp.concatenate([high, low, high], axis=0).astype(bf16)
            first_ref[512:608, to] = jnp.concatenate(
                [high, low, jnp.ones((32, CHUNK), f32)], axis=0
            ).astype(bf16)
            first = jnp.tanh(dot(win_cat, stack) + b_in)
            fh, fl = split(first)
            first_ref[0:256, to] = fh
            first_ref[256:512, to] = fl
            second = dot(wmh, fh) + dot(wmh, fl) + dot(wml, fh)
            second = jnp.tanh(second + b_mid)
            sh, sl = split(second)
            second_ref[0:256, to] = sh
            second_ref[256:512, to] = sl
        whole = slice(half * width, (half + 1) * width)
        for i, (held, target) in enumerate(((first_ref, first_hbm), (second_ref, second_hbm))):
            copies.append(
                start_copy(held.at[:, whole], target.at[:, whole], out_sems, 2 + 2 * half + i)
            )
    done_ref[...] = jnp.zeros(done_ref.shape, f32)
    for copy in copies:
        copy.wait()


def closure_back(msg_ref, turn_ref, second_ref, table_ref, cot_ref, mask_ref, first_ref,
                 wide_ref, total_ref, gvel_hbm, gbuoy_hbm,
                 line_ref, e1h_ref, e1l_ref, e2h_ref, e2l_ref, dl_ref, b2_ref,
                 gvel_ref, gbuoy_ref, out_sems):
    width = mask_ref.shape[-1]
    lane = lane_of((LANES, LANES))
    halves = []
    items = [msg_ref[pl.ds(field, LANES, stride=3), :] for field in range(3)]
    for t in range(8):
        value = jnp.zeros((LANES, LANES), f32)
        for field, item in enumerate(items):
            value = jnp.where(lane // 16 == field, roll(item, 16 * (field - t), 1), value)
        halves.append(value)
    cos_r, sin_r = part_back(
        [jnp.concatenate(halves[2 * i : 2 * i + 2], axis=0) for i in range(4)]
    )
    parts = ([], [])
    for r in range(4):
        pair = (cos_r[r], sin_r[r])
        if r > 0:
            at = 512 * (r - 1)
            cos_turn, sin_turn = turn_ref[at : at + 256], turn_ref[at + 256 : at + 512]
            pair = turn(*pair, cos_turn, -sin_turn)
        for i, value in enumerate(pair):
            high, low = split_f32(value)
            parts[i].append((high + roll(low, 64, 1)).astype(bf16))
    columns = jnp.concatenate([jnp.concatenate(part, axis=1) for part in parts], axis=0)
    found = dot_table(table_ref, columns, 0, 256)
    for r in range(4):
        block = found[:, LANES * r : LANES * (r + 1)]
        line_ref[pl.ds(r, 256, stride=4), :] = block + roll(block, 64, 1)
    field = line_ref[...].T
    pressure = field[0:16]
    east_back = roll(pressure, 1, 1) - pressure
    projected = (
        cot_ref[0, 0] - east_back,
        cot_ref[1, 0] - field[32:48],
        cot_ref[2, 0] - field[16:32],
    )
    wet = mask_ref[0].astype(f32)
    out_copies = []
    deltas = [value * wet for value in projected]
    blank = jnp.zeros((8, CHUNK), f32)
    bias2 = jnp.zeros((256, LANES), f32)
    for half in range(2):
        part = slice(8 * half, 8 * (half + 1))
        for start in range(0, width, CHUNK):
            col = slice(start, start + CHUNK)
            to = slice(half * width + start, half * width + start + CHUNK)
            delta = jnp.concatenate([value[part, col] for value in deltas] + [blank], axis=0)
            dh, dl = split_f32(delta)
            stack = jnp.concatenate([dh, dl, dh], axis=0).astype(bf16)
            dl_ref[:, to] = stack[0:64]
            second = second_ref[0:256, to].astype(f32) + second_ref[256:512, to].astype(f32)
            err2 = dot(wide_ref[0:256, 0:96], stack) * (1.0 - second * second)
            bias2 = bias2 + sum(err2[:, LANES * i : LANES * (i + 1)] for i in range(CHUNK // LANES))
            e2h, e2l = split(err2)
            e2h_ref[:, to] = e2h
            e2l_ref[:, to] = e2l
            first = first_ref[0:256, to].astype(f32) + first_ref[256:512, to].astype(f32)
            err1 = (
                dot(wide_ref[0:256, 128:384], e2h)
                + dot(wide_ref[0:256, 128:384], e2l)
                + dot(wide_ref[0:256, 384:640], e2h)
            )
            err1 = err1 * (1.0 - first * first)
            e1h, e1l = split(err1)
            e1h_ref[:, to] = e1h
            e1l_ref[:, to] = e1l
            out = (
                dot(wide_ref[256:288, 128:384], e1h)
                + dot(wide_ref[256:288, 128:384], e1l)
                + dot(wide_ref[256:288, 384:640], e1h)
            )
            for c in range(3):
                gvel_ref[c, 0, part, col] = projected[c][part, col] + out[8 * c : 8 * (c + 1)]
            gbuoy_ref[0, part, col] = out[24:32]
        out_copies += [
            start_copy(gvel_ref.at[:, :, part, :], gvel_hbm.at[:, :, part, :], out_sems, 2 * half),
            start_copy(gbuoy_ref.at[:, part, :], gbuoy_hbm.at[:, part, :], out_sems, 2 * half + 1),
        ]
    b2_ref[...] = bias2
    mid = (
        dot_nt(e2h_ref[...], first_ref[0:256])
        + dot_nt(e2h_ref[...], first_ref[256:512])
        + dot_nt(e2l_ref[...], first_ref[0:256])
    )
    both1 = dot_nt(first_ref[512:608], e1h_ref[...])
    rest1 = dot_nt(first_ref[512:608], e1l_ref[...])
    win = both1[0:32] + both1[32:64] + rest1[0:32]
    bin_ = both1[64:65] + rest1[64:65]
    both2 = dot_nt(dl_ref[...], second_ref[0:256])
    rest2 = dot_nt(dl_ref[...], second_ref[256:512])
    wout = both2[0:32] + both2[32:64] + rest2[0:32]

    def fold_rows(value):
        return jnp.sum(value.reshape(value.shape[0] // 8, 8, value.shape[1]), axis=1)

    to_unit = gather((256, LANES), 8)
    mid = exact(fold_rows(same_row(mid)), to_unit)
    small = [fold_rows(same_row(win)), fold_rows(same_row(wout)), bin_, jnp.zeros((7, 256), f32)]
    small = exact(jnp.concatenate(small, axis=0), to_unit)
    b2 = lax.dot_general(
        jnp.ones((8, LANES), f32),
        fold_rows(b2_ref[...]),
        (((1,), (1,)), ((), ())),
        precision=lax.Precision.HIGHEST,
        preferred_element_type=f32,
    )
    units = jnp.concatenate([mid[8 * i : 8 * (i + 1), 0:32] for i in range(4)], axis=1)
    rows = [units[i : i + 1] for i in range(8)]
    rows.append(jnp.concatenate([small[i : i + 1, 0:32] for i in range(4)], axis=1))
    rows.append(
        jnp.concatenate([small[i : i + 1, 0:32] for i in range(4, 7)] + [b2[0:1]], axis=1)
    )
    rows.append(small[8:9])
    rows = jnp.concatenate(rows, axis=0)
    for peer in range(32):
        total_ref[11 * peer : 11 * (peer + 1), :] = rows
    for copy in out_copies:
        copy.wait()


def sum_rows(got_ref):
    return [
        jnp.sum(got_ref[pl.ds(i, got_ref.shape[0] // 11, stride=11), :], axis=0, keepdims=True)
        for i in range(11)
    ]


def sum_slab(got_ref, out_ref):
    total = jnp.concatenate(sum_rows(got_ref), axis=0)
    for peer in range(16):
        out_ref[11 * peer : 11 * (peer + 1), :] = total


def sum_column(scale, got_ref, win_ref, bin_ref, wmid_ref, bmid_ref, wout_ref):
    rows = [row * scale for row in sum_rows(got_ref)]
    units = jnp.concatenate(rows[:8], axis=0)
    wmid_ref[...] = jnp.concatenate([units[:, 32 * i : 32 * (i + 1)] for i in range(4)], axis=0)
    win_ref[...] = jnp.concatenate([rows[8][:, 32 * i : 32 * (i + 1)] for i in range(4)], axis=0)
    wout_ref[...] = jnp.concatenate([rows[9][:, 32 * i : 32 * (i + 1)] for i in range(3)], axis=0)
    bmid_ref[...] = rows[9][:, 96:128]
    bin_ref[...] = rows[10][:, 0:32]


def trade(rows, peers, axes):
    size = rows.shape[0] // peers * LANES
    got = lax.all_to_all(rows.reshape(peers, 1, size), axes, 0, 0)
    return got.reshape(rows.shape)


def shards(velocity, buoyancy, cell_mask, spacing, cotangent, w_in, b_in, w_mid, b_mid, w_out):
    levels, rows, width = buoyancy.shape
    depth = spacing.shape[0]
    span_y = rows * 64
    table = dft_table(256, 1024)
    table_y = table[:, (np.arange(256) % 64) * 4 + np.arange(256) // 64]
    x_table, y_table = jnp.asarray(two_parts(table)), jnp.asarray(two_parts(table_y))
    backs = jnp.asarray(np.concatenate([two_parts(table.T), two_parts(table_y.T)], axis=0))
    eigen = eigenvalue(width)
    lanes = np.arange(LANES)
    ey = eigen.reshape(4, 4, 64)[lanes % 16 // 4, lanes % 4].T.astype(np.float32)
    ey = np.concatenate([ey, np.zeros((192, LANES), np.float32)], axis=0)
    ex = eigen[np.arange(128)[:, None] + 128 * (lanes[None, :] // 16)].astype(np.float32)
    turns = twiddles(256, 1024)
    fixed = jnp.asarray(np.concatenate([turns, ey, ex], axis=0))
    spread_turns = jnp.asarray(
        np.concatenate([np.repeat(turns[:, i : i + 1], LANES, axis=1) for i in range(2, 8)], axis=0)
    )
    turns = jnp.asarray(turns)
    cells = rows * width // 8
    dma = pltpu.SemaphoreType.DMA
    type_of = jax.ShapeDtypeStruct
    table = pltpu.VMEM((1024, 256), bf16)
    back_tables = pltpu.VMEM((1024, 512), bf16)
    turn_held = pltpu.VMEM((640, LANES), f32)
    first_held = pltpu.VMEM((608, cells), bf16)
    second_held = pltpu.VMEM((512, cells), bf16)
    wide = pltpu.VMEM((256, cells), bf16)
    wide_held = pltpu.VMEM((288, 640), bf16)
    mark_type = type_of((8, LANES), f32)
    table_flops = 4 * 512 * 256 * 512
    msg_type = type_of((128 * 3, LANES), f32)
    msg, mark = call(
        forward_x,
        (msg_type, mark_type),
        (cotangent, x_table, turns),
        hbm=(0, 1, 2),
        scratch=(
            table,
            pltpu.VMEM((256, LANES), f32),
            pltpu.VMEM(cotangent.shape, f32),
            pltpu.VMEM((1024, LANES), f32),
            dma((3,)),
        ),
        flops=table_flops,
        name="forward_x",
    )
    msg = trade(msg, 128, PLANE)

    first, second, weights, turns, mark = call(
        closure_forward,
        (
            pltpu.HBM((608, cells), bf16),
            pltpu.HBM((512, cells), bf16),
            pltpu.HBM((288, 640), bf16),
            pltpu.HBM((640, LANES), f32),
            mark_type,
        ),
        (w_in.T, b_in[None], w_mid, b_mid[None], w_out, spacing[None])
        + (velocity, buoyancy, fixed, mark),
        hbm=range(9),
        hbm_out=range(4),
        scratch=(
            pltpu.VMEM((4, 32), f32),
            pltpu.VMEM((1, 32), f32),
            pltpu.VMEM((32, 32), f32),
            pltpu.VMEM((1, 32), f32),
            pltpu.VMEM((3, 32), f32),
            pltpu.VMEM((1, LEVELS), f32),
            pltpu.VMEM(velocity.shape, f32),
            pltpu.VMEM(buoyancy.shape, f32),
            turn_held,
            first_held,
            second_held,
            wide_held,
            dma((9,)),
            dma((6,)),
        ),
        flops=2 * 256 * 256 * cells * 4,
        name="closure_forward",
    )
    gathered, turns, backs, weights = call(
        forward_y,
        (type_of((4, 256, LANES), f32), turn_held, back_tables, wide_held),
        (msg, y_table, turns, backs, weights, mark),
        hbm=(1, 2, 3, 4),
        scratch=(table, dma((4,))),
        flops=table_flops,
        name="forward_y",
    )
    gathered = lax.all_to_all(gathered, "x", 0, 0)
    (msg,) = call(
        solve_back,
        (msg_type,),
        (gathered, turns, backs),
        flops=table_flops,
        name="solve_back",
    )
    msg = trade(msg, 128, PLANE)
    totals, grad_velocity, grad_buoyancy = call(
        closure_back,
        (
            type_of((32 * 11, LANES), f32),
            pltpu.HBM(cotangent.shape, f32),
            pltpu.HBM(buoyancy.shape, f32),
        ),
        (msg, spread_turns, second, backs, cotangent, cell_mask, first, weights),
        hbm_out=(1, 2),
        scratch=(
            pltpu.VMEM((1024, LANES), f32),
            wide,
            wide,
            wide,
            wide,
            pltpu.VMEM((64, cells), bf16),
            pltpu.VMEM((256, LANES), f32),
            pltpu.VMEM(cotangent.shape, f32),
            pltpu.VMEM(buoyancy.shape, f32),
            dma((4,)),
        ),
        flops=table_flops + 2 * 256 * 256 * cells * 10,
        name="closure_back",
    )
    totals = trade(totals, 32, SLAB)
    (totals,) = call(sum_slab, (type_of((16 * 11, LANES), f32),), (totals,), name="sum_slab")
    totals = trade(totals, 16, COLUMN)
    scale = 1.0 / math.sqrt(width * span_y * depth)
    grad_in, grad_b_in, grad_mid, grad_b_mid, grad_out = call(
        functools.partial(sum_column, scale),
        (
            type_of((4, 32), f32),
            type_of((1, 32), f32),
            type_of((32, 32), f32),
            type_of((1, 32), f32),
            type_of((3, 32), f32),
        ),
        (totals,),
        name="sum_column",
    )
    return (
        grad_velocity,
        grad_buoyancy,
        grad_in.T,
        grad_b_in[0],
        grad_mid,
        grad_b_mid[0],
        grad_out,
    )


def solution(mesh):
    fine = Mesh(
        mesh.devices.reshape([size for _, size in FINE]), tuple(name for name, _ in FINE)
    )
    field = P(None, NARROW, WIDE, None)
    cell = P(NARROW, WIDE, None)
    in_specs = (field, cell, cell, P(), field, P(), P(), P(), P(), P())
    out_specs = (field, cell, P(), P(), P(), P(), P())
    return jax.shard_map(shards, mesh=fine, in_specs=in_specs, out_specs=out_specs, check_vma=False)
```

```python
import functools
import math

import jax
import jax.numpy as jnp
import ml_dtypes
import numpy as np
from jax import lax
from jax.experimental import pallas as pl
from jax.experimental.pallas import tpu as pltpu
from jax.sharding import Mesh
from jax.sharding import PartitionSpec as P

free_surface = 0.05
f32 = jnp.float32
bf16 = jnp.bfloat16
LANES = 128
LEVELS = 8
VMEM_LIMIT = 24 * 1024 * 1024

FINE = (("y", 4), ("zl", 8), ("c", 2), ("zh", 2), ("x", 4))
WIDE = ("y", "zl", "c")
NARROW = ("zh", "x")
PLANE = ("y", "zl", "c", "zh")
SLAB = ("y", "x", "c")
COLUMN = ("zh", "zl")


def dft_table(count, length):
    indices = np.arange(count)
    angle = 2.0 * np.pi / count * (indices[:, None] * indices[None, :] % count)
    return np.concatenate([np.cos(angle), np.sin(angle)], axis=0) * np.sqrt(2.0 / length)


def twiddles(count, length):
    angle = 2.0 * np.pi / length * np.arange(count)[:, None] * np.arange(4)[None, :]
    held = np.zeros((count, LANES))
    held[:, 0:8:2] = np.cos(angle)
    held[:, 1:8:2] = np.sin(angle)
    return held.astype(np.float32)


def wavenumbers(length):
    half = np.arange(length // 2)
    return np.concatenate([half, np.where(half == 0, length // 2, half)])


def two_parts(table):
    high = table.astype(np.float32).astype(ml_dtypes.bfloat16)
    low = (table - high.astype(np.float64)).astype(np.float32).astype(ml_dtypes.bfloat16)
    return np.concatenate([high, low], axis=0)


def eigenvalue(length):
    return -4.0 * np.sin(np.pi / length * wavenumbers(length)) ** 2


def split(value):
    high = value.astype(bf16)
    low = (value - high.astype(f32)).astype(bf16)
    return high, low


def split_f32(value):
    high = value.astype(bf16).astype(f32)
    return high, value - high


def dot(a, b):
    return jnp.dot(a, b, preferred_element_type=f32)


def dot_table(table_ref, b, start, rows):
    middle = start + rows
    return dot(table_ref[start:middle], b) + dot(table_ref[middle : middle + rows], b)


def dot_nt(a, b):
    return lax.dot_general(a, b, (((1,), (1,)), ((), ())), preferred_element_type=f32)


def roll(value, shift, axis):
    size = value.shape[axis]
    shift = shift % size
    return value if shift == 0 else pltpu.roll(value, shift, axis)


def lane_of(shape):
    return lax.broadcasted_iota(jnp.int32, shape, len(shape) - 1)


def start_copy(source, target, sems, index):
    copy = pltpu.make_async_copy(source, target, sems.at[index])
    copy.start()
    return copy


def call(kernel, out_shape, args, smem=(), hbm=(), hbm_out=(), scratch=(), flops=0, name=None):
    def space(index, held):
        return pl.BlockSpec(memory_space=held.get(index, pltpu.VMEM))

    held = {i: pltpu.SMEM for i in smem} | {i: pl.ANY for i in hbm}
    args = [
        pltpu.with_memory_space_constraint(a, pltpu.HBM) if i in hbm else a
        for i, a in enumerate(args)
    ]
    moved = sum(int(np.prod(a.shape)) * a.dtype.itemsize for a in args)
    return pl.pallas_call(
        kernel,
        out_shape=out_shape,
        in_specs=[space(i, held) for i in range(len(args))],
        out_specs=[space(i, {o: pl.ANY for o in hbm_out}) for i in range(len(out_shape))],
        scratch_shapes=list(scratch),
        compiler_params=pltpu.CompilerParams(vmem_limit_bytes=VMEM_LIMIT),
        cost_estimate=pl.CostEstimate(flops=flops, bytes_accessed=moved, transcendentals=0),
        name=name,
    )(*args)


def first_row(shape):
    return lax.broadcasted_iota(jnp.int32, shape, 0) == 0


def join(cos_r, sin_r):
    even_c, even_s = cos_r[0] + cos_r[2], sin_r[0] + sin_r[2]
    odd_c, odd_s = cos_r[1] + cos_r[3], sin_r[1] + sin_r[3]
    top = first_row(even_c.shape)
    ends = jnp.where(top, math.sqrt(0.5), 1.0)
    return (
        (even_c + odd_c) * ends,
        cos_r[0] - cos_r[2] - (sin_r[1] - sin_r[3]),
        jnp.where(top, even_c - odd_c, even_s + odd_s) * ends,
        sin_r[0] - sin_r[2] + (cos_r[1] - cos_r[3]),
    )


def part_back(blocks):
    top = first_row(blocks[0].shape)
    ends = jnp.where(top, math.sqrt(0.5), 1.0)
    low_c, high_c, low_s, high_s = blocks
    low_c, low_s = low_c * ends, low_s * ends
    last = jnp.where(top, low_s, 0.0)
    low_s = jnp.where(top, 0.0, low_s)
    even, odd = low_c + last, low_c - last
    return (
        (even + high_c, odd + high_s, even - high_c, odd - high_s),
        (low_s + high_s, low_s - high_c, low_s - high_s, low_s + high_c),
    )


def turn(cos_part, sin_part, cos_turn, sin_turn):
    return cos_part * cos_turn - sin_part * sin_turn, sin_part * cos_turn + cos_part * sin_turn


def turn_of(turn_ref, remainder):
    rows, shape = slice(0, 256), (256, LANES)
    return (
        jnp.broadcast_to(turn_ref[rows, 2 * remainder : 2 * remainder + 1], shape),
        jnp.broadcast_to(turn_ref[rows, 2 * remainder + 1 : 2 * remainder + 2], shape),
    )


def forward_x(cot_hbm, table_hbm, turn_hbm, out_ref, mark_ref,
              table_ref, turn_ref, cot_ref, line_ref, sems):
    first = start_copy(cot_hbm, cot_ref, sems, 0)
    copies = [
        start_copy(table_hbm, table_ref, sems, 1),
        start_copy(turn_hbm, turn_ref, sems, 2),
    ]
    first.wait()
    east, north, up = cot_ref[0, 0], cot_ref[1, 0], cot_ref[2, 0]
    rows, width = east.shape
    east = east - roll(east, -1, 1)
    high, low = split_f32(jnp.concatenate([east, north, up], axis=0))
    none = jnp.zeros((rows, width), f32)
    line_ref[...] = jnp.concatenate([high, none, low, none], axis=0).T
    lines = jnp.concatenate(
        [line_ref[pl.ds(r, 256, stride=4), :].astype(bf16) for r in range(4)], axis=1
    )
    for copy in copies:
        copy.wait()
    got = dot_table(table_ref, lines, 0, 512)
    cos_r, sin_r = [], []
    for r in range(4):
        cos_part = got[0:256, LANES * r : LANES * (r + 1)]
        sin_part = got[256:512, LANES * r : LANES * (r + 1)]
        if r > 0:
            cos_part, sin_part = turn(cos_part, sin_part, *turn_of(turn_ref, r))
        cos_r.append(cos_part)
        sin_r.append(sin_part)
    blocks = [block + roll(block, 64, 1) for block in join(cos_r, sin_r)]
    lane = lane_of((LANES, LANES))
    for field in range(3):
        packed = jnp.zeros((LANES, LANES), f32)
        for t in range(8):
            block = blocks[t // 2][LANES * (t % 2) : LANES * (t % 2 + 1)]
            packed = jnp.where(lane // 16 == t, roll(block, 16 * (t - field), 1), packed)
        out_ref[pl.ds(field, LANES, stride=3), :] = packed
    mark_ref[...] = jnp.zeros(mark_ref.shape, f32)


def pair_turns(turn_ref, pair, within):
    one, two = turn_of(turn_ref, 2 * pair), turn_of(turn_ref, 2 * pair + 1)
    return tuple(jnp.where(within < 8, a, b) for a, b in zip(one, two))


def forward_y(msg_ref, table_hbm, turn_hbm, back_hbm, wide_hbm, mark_ref,
              out_ref, turn_ref, back_ref, wide_ref, table_ref, sems):
    copies = [
        start_copy(table_hbm, table_ref, sems, 0),
        start_copy(turn_hbm, turn_ref, sems, 1),
    ]
    later_copies = [
        start_copy(back_hbm, back_ref, sems, 2),
        start_copy(wide_hbm, wide_ref, sems, 3),
    ]
    within = lane_of((64, LANES)) % 16
    highs = []
    lows = []
    for half in range(2):
        east, north, up = (
            msg_ref[pl.ds(3 * half + field, 64, stride=6), :] for field in range(3)
        )
        after = jnp.where(
            within < 15, roll(north, -1, 1), roll(roll(north, -1, 0), 15, 1)
        )
        for value in (east + north - after, up):
            high, low = split_f32(value)
            highs.append(high)
            lows.append(low)
    shifted = [roll(value, c, 1) for c, value in enumerate(highs + lows)]

    def line_of(j, to):
        line = shifted[0]
        for c in range(1, 8):
            line = jnp.where(within == (c + j) % 16, shifted[c], line)
        return roll(line, to - j, 1)

    lines = []
    for pair in range(2):
        rows = []
        for step in range(4):
            j = 4 * step + 2 * pair
            rows.append(jnp.where(within < 8, line_of(j, 0), line_of(j + 1, 8)).astype(bf16))
        lines.append(jnp.concatenate(rows, axis=0))
    lines = jnp.concatenate(lines, axis=1)
    for copy in copies:
        copy.wait()
    got = dot_table(table_ref, lines, 0, 512)
    within = lane_of((256, LANES)) % 16
    turned = [
        turn(
            got[0:256, LANES * pair : LANES * (pair + 1)],
            got[256:512, LANES * pair : LANES * (pair + 1)],
            *pair_turns(turn_ref, pair, within),
        )
        for pair in range(2)
    ]
    cos_r = [turned[0][0], roll(turned[0][0], -8, 1), turned[1][0], roll(turned[1][0], -8, 1)]
    sin_r = [turned[0][1], roll(turned[0][1], -8, 1), turned[1][1], roll(turned[1][1], -8, 1)]
    packed = jnp.zeros((256, LANES), f32)
    for g, block in enumerate(join(cos_r, sin_r)):
        block = block + roll(block, -4, 1)
        packed = jnp.where(within // 4 == g, roll(block, 4 * g, 1), packed)
    for peer in range(4):
        out_ref[peer] = packed
    for copy in later_copies:
        copy.wait()


def vertical(spacing):
    one = jnp.ones((1, LANES), f32)
    none = jnp.zeros((1, LANES), f32)
    spacing = [one * spacing[k] for k in range(LEVELS)]
    inv_dz = [1.0 / value for value in spacing]
    face = [2.0 / (spacing[k] + spacing[k + 1]) for k in range(LEVELS - 1)] + [none]
    lower = [none] + [inv_dz[k] * face[k - 1] for k in range(1, LEVELS)]
    upper = [inv_dz[k] * face[k] for k in range(LEVELS)]
    base = [-(lower[k] + upper[k]) for k in range(LEVELS)]
    base[-1] = base[-1] - free_surface * inv_dz[-1]
    sub = [none] + upper[:-1]
    sup = lower[1:] + [none]
    keep = [one] * (LEVELS - 1) + [none]
    return inv_dz, face, sub, base, sup, keep


def solve_back(got_ref, turn_ref, table_ref, pair_ref, out_ref):
    at = lax.axis_index("x")
    rows = got_ref.shape[1]
    lam = turn_ref[256 : 256 + rows // 4]
    lane = lane_of((rows, LANES))
    column = lane_of(lam.shape) % 4
    inv_dz, face, sub, base, sup, keep = (
        [turn_ref[512 + 8 * i + k : 513 + 8 * i + k] for k in range(LEVELS)]
        for i in range(6)
    )
    quarters = [slice(rows // 4 * r, rows // 4 * (r + 1)) for r in range(4)]

    def gathered(k, field):
        at_lane = 2 * (k // 4) + field
        value = roll(got_ref[k % 4, quarters[0], :], -at_lane, 1)
        for r in range(1, 4):
            moved = roll(got_ref[k % 4, quarters[r], :], r - at_lane, 1)
            value = jnp.where(column == r, moved, value)
        return value

    ratios = []
    values = []
    below = None
    for k in range(LEVELS):
        flux = gathered(k, 1) * face[k]
        right = gathered(k, 0) - flux
        if k > 0:
            right = right + below
        below = flux
        diagonal = lam + base[k]
        if k > 0:
            diagonal = diagonal - sub[k] * ratios[-1]
            right = right - sub[k] * values[-1]
        inverse = 1.0 / diagonal
        ratios.append(sup[k] * inverse)
        values.append(right * inverse)
    result = [None] * LEVELS
    result[-1] = values[-1]
    for k in range(LEVELS - 2, -1, -1):
        result[k] = values[k] - ratios[k] * result[k + 1]
    scaled = [result[k] * inv_dz[k] for k in range(LEVELS)] + [jnp.zeros_like(lam)]
    change = [(scaled[k] - scaled[k + 1]) * keep[k] for k in range(LEVELS)]

    def own(items, half):
        value = items[4 * half]
        for x in range(1, 4):
            value = jnp.where(at == x, items[4 * half + x], value)
        return value

    fields = [own(result, 0), own(change, 0), own(result, 1), own(change, 1)]
    both = []
    for r in range(4):
        value = roll(fields[0], -r, 1)
        for c in range(1, 4):
            value = jnp.where(column == c, roll(fields[c], c - r, 1), value)
        both.append(value)
    both = jnp.concatenate(both, axis=0)
    within = lane % 16
    blocks = []
    for g in range(4):
        block = roll(both, -4 * g, 1)
        blocks.append(jnp.where(within < 8, block, roll(block, 8, 1)))
    cos_r, sin_r = part_back(blocks)
    parts = ([], [])
    for pair in range(2):
        cos_part = jnp.where(within < 8, cos_r[2 * pair], cos_r[2 * pair + 1])
        sin_part = jnp.where(within < 8, sin_r[2 * pair], sin_r[2 * pair + 1])
        at = 512 * pair
        cos_turn, sin_turn = pair_ref[at : at + 256], pair_ref[at + 256 : at + 512]
        for i, value in enumerate(turn(cos_part, sin_part, cos_turn, -sin_turn)):
            high, low = split_f32(jnp.where(within % 8 < 4, value, 0.0))
            parts[i].append((high + roll(low, 4, 1)).astype(bf16))
    columns = jnp.concatenate([jnp.concatenate(part, axis=1) for part in parts], axis=0)
    got = dot_table(table_ref, columns, 512, 256)
    within = lane_of((64, LANES)) % 16
    packed = [jnp.zeros((64, LANES), f32)] * 4
    for pair in range(2):
        found = got[:, LANES * pair : LANES * (pair + 1)]
        found = found + roll(found, -4, 1)
        for step in range(4):
            for one in range(2):
                j = 4 * step + 2 * pair + one
                moved = roll(found[64 * step : 64 * (step + 1)], j - 8 * one, 1)
                for c in range(4):
                    packed[c] = jnp.where(within == (j + c) % 16, moved, packed[c])
    for half in range(2):
        pressure = roll(packed[2 * half], -2 * half, 1)
        change_up = roll(packed[2 * half + 1], -(2 * half + 1), 1)
        before = jnp.where(
            within > 0, roll(pressure, 1, 1), roll(roll(pressure, 1, 0), -15, 1)
        )
        for field, value in enumerate((pressure, change_up, before - pressure)):
            out_ref[pl.ds(3 * half + field, 64, stride=6), :] = value


CHUNK = 1024


def unit_rows(shape, axis):
    return lax.broadcasted_iota(jnp.int32, shape, axis) % 8


def same_row(value):
    shape = value.shape
    return jnp.where(unit_rows(shape, 0) == unit_rows(shape, 1), value, 0.0)


def gather(shape, step):
    to = lax.broadcasted_iota(jnp.int32, shape, 1)
    return (lax.broadcasted_iota(jnp.int32, shape, 0) // step == to).astype(f32)


def exact(a, b):
    return jnp.dot(a, b, precision=lax.Precision.HIGHEST, preferred_element_type=f32)


def spread(weight, columns):
    tall, wide = weight.shape
    step = (
        lax.broadcasted_iota(jnp.int32, (wide, columns), 1) // 8
        == lax.broadcasted_iota(jnp.int32, (wide, columns), 0)
    ).astype(f32)
    value = exact(weight, step)
    value = jnp.broadcast_to(value[:, None, :], (tall, 8, columns)).reshape(8 * tall, columns)
    return same_row(value)


def closure_forward(win_hbm, bin_hbm, wmid_hbm, bmid_hbm, wout_hbm, spacing_hbm,
                    vel_hbm, buoy_hbm, fixed_hbm, mark_ref,
                    first_hbm, second_hbm, wide_hbm, turn_hbm, done_ref,
                    win_ref, bin_ref, wmid_ref, bmid_ref, wout_ref, spacing_ref,
                    vel_ref, buoy_ref, turn_ref, first_ref, second_ref, wide_ref, sems, out_sems):
    sources = (win_hbm, bin_hbm, wmid_hbm, bmid_hbm, wout_hbm, spacing_hbm)
    sources += (vel_hbm, buoy_hbm, fixed_hbm)
    targets = (win_ref, bin_ref, wmid_ref, bmid_ref, wout_ref, spacing_ref)
    targets += (vel_ref, buoy_ref, turn_ref)
    copies = [start_copy(*pair, sems, i) for i, pair in enumerate(zip(sources, targets))]
    for copy in copies[:6]:
        copy.wait()
    win_t = win_ref[...]
    wmid = wmid_ref[...]
    wout_h, wout_l = split_f32(spread(wout_ref[...].T, 32))
    wide_ref[0:256, 0:96] = jnp.concatenate([wout_h, wout_h, wout_l], axis=1).astype(bf16)
    wide_ref[0:256, 96:128] = jnp.zeros((256, 32), bf16)
    wide_ref[0:256, 128:384], wide_ref[0:256, 384:640] = split(spread(wmid.T, 256))
    wide_ref[256:288, 0:128] = jnp.zeros((32, 128), bf16)
    wide_ref[256:288, 128:384], wide_ref[256:288, 384:640] = split(spread(win_t, 256))
    win_h, win_l = split_f32(spread(win_t.T, 32))
    win_cat = jnp.concatenate([win_h, win_h, win_l], axis=1).astype(bf16)
    wmh, wml = split(spread(wmid, 256))

    def tall(row):
        column = row.T
        return jnp.broadcast_to(column[:, None, :], (32, 8, 1)).reshape(256, 1)

    b_in, b_mid = tall(bin_ref[...]), tall(bmid_ref[...])
    for copy in copies[6:]:
        copy.wait()
    own = turn_ref[pl.ds(512 + lax.axis_index(PLANE), 1), :]
    turn_ref[256:512] = turn_ref[256:512] + own
    for i, rows in enumerate(vertical([spacing_ref[:, k : k + 1] for k in range(LEVELS)])):
        turn_ref[512 + 8 * i : 520 + 8 * i] = jnp.concatenate(rows, axis=0)
    copies = [
        start_copy(wide_ref, wide_hbm, out_sems, 0),
        start_copy(turn_ref, turn_hbm, out_sems, 1),
    ]
    width = buoy_ref.shape[-1]
    for half in range(2):
        part = slice(8 * half, 8 * (half + 1))
        for start in range(0, width, CHUNK):
            col = slice(start, start + CHUNK)
            to = slice(half * width + start, half * width + start + CHUNK)
            feats = jnp.concatenate(
                [vel_ref[c, 0, part, col] for c in range(3)] + [buoy_ref[0, part, col]], axis=0
            )
            high, low = split_f32(feats)
            stack = jnp.concatenate([high, low, high], axis=0).astype(bf16)
            first_ref[512:608, to] = jnp.concatenate(
                [high, low, jnp.ones((32, CHUNK), f32)], axis=0
            ).astype(bf16)
            first = jnp.tanh(dot(win_cat, stack) + b_in)
            fh, fl = split(first)
            first_ref[0:256, to] = fh
            first_ref[256:512, to] = fl
            second = dot(wmh, fh) + dot(wmh, fl) + dot(wml, fh)
            second = jnp.tanh(second + b_mid)
            sh, sl = split(second)
            second_ref[0:256, to] = sh
            second_ref[256:512, to] = sl
        whole = slice(half * width, (half + 1) * width)
        for i, (held, target) in enumerate(((first_ref, first_hbm), (second_ref, second_hbm))):
            copies.append(
                start_copy(held.at[:, whole], target.at[:, whole], out_sems, 2 + 2 * half + i)
            )
    done_ref[...] = jnp.zeros(done_ref.shape, f32)
    for copy in copies:
        copy.wait()


def closure_back(msg_ref, turn_ref, second_ref, table_ref, cot_ref, mask_ref, first_ref,
                 wide_ref, total_ref, gvel_hbm, gbuoy_hbm,
                 line_ref, e1h_ref, e1l_ref, e2h_ref, e2l_ref, dl_ref, b2_ref,
                 gvel_ref, gbuoy_ref, out_sems):
    width = mask_ref.shape[-1]
    lane = lane_of((LANES, LANES))
    halves = []
    items = [msg_ref[pl.ds(field, LANES, stride=3), :] for field in range(3)]
    for t in range(8):
        value = jnp.zeros((LANES, LANES), f32)
        for field, item in enumerate(items):
            value = jnp.where(lane // 16 == field, roll(item, 16 * (field - t), 1), value)
        halves.append(value)
    cos_r, sin_r = part_back(
        [jnp.concatenate(halves[2 * i : 2 * i + 2], axis=0) for i in range(4)]
    )
    parts = ([], [])
    for r in range(4):
        pair = (cos_r[r], sin_r[r])
        if r > 0:
            at = 512 * (r - 1)
            cos_turn, sin_turn = turn_ref[at : at + 256], turn_ref[at + 256 : at + 512]
            pair = turn(*pair, cos_turn, -sin_turn)
        for i, value in enumerate(pair):
            high, low = split_f32(value)
            parts[i].append((high + roll(low, 64, 1)).astype(bf16))
    columns = jnp.concatenate([jnp.concatenate(part, axis=1) for part in parts], axis=0)
    found = dot_table(table_ref, columns, 0, 256)
    for r in range(4):
        block = found[:, LANES * r : LANES * (r + 1)]
        line_ref[pl.ds(r, 256, stride=4), :] = block + roll(block, 64, 1)
    field = line_ref[...].T
    pressure = field[0:16]
    east_back = roll(pressure, 1, 1) - pressure
    projected = (
        cot_ref[0, 0] - east_back,
        cot_ref[1, 0] - field[32:48],
        cot_ref[2, 0] - field[16:32],
    )
    wet = mask_ref[0].astype(f32)
    out_copies = []
    deltas = [value * wet for value in projected]
    blank = jnp.zeros((8, CHUNK), f32)
    bias2 = jnp.zeros((256, LANES), f32)
    for half in range(2):
        part = slice(8 * half, 8 * (half + 1))
        for start in range(0, width, CHUNK):
            col = slice(start, start + CHUNK)
            to = slice(half * width + start, half * width + start + CHUNK)
            delta = jnp.concatenate([value[part, col] for value in deltas] + [blank], axis=0)
            dh, dl = split_f32(delta)
            stack = jnp.concatenate([dh, dl, dh], axis=0).astype(bf16)
            dl_ref[:, to] = stack[0:64]
            second = second_ref[0:256, to].astype(f32) + second_ref[256:512, to].astype(f32)
            err2 = dot(wide_ref[0:256, 0:96], stack) * (1.0 - second * second)
            bias2 = bias2 + sum(err2[:, LANES * i : LANES * (i + 1)] for i in range(CHUNK // LANES))
            e2h, e2l = split(err2)
            e2h_ref[:, to] = e2h
            e2l_ref[:, to] = e2l
            first = first_ref[0:256, to].astype(f32) + first_ref[256:512, to].astype(f32)
            err1 = (
                dot(wide_ref[0:256, 128:384], e2h)
                + dot(wide_ref[0:256, 128:384], e2l)
                + dot(wide_ref[0:256, 384:640], e2h)
            )
            err1 = err1 * (1.0 - first * first)
            e1h, e1l = split(err1)
            e1h_ref[:, to] = e1h
            e1l_ref[:, to] = e1l
            out = (
                dot(wide_ref[256:288, 128:384], e1h)
                + dot(wide_ref[256:288, 128:384], e1l)
                + dot(wide_ref[256:288, 384:640], e1h)
            )
            for c in range(3):
                gvel_ref[c, 0, part, col] = projected[c][part, col] + out[8 * c : 8 * (c + 1)]
            gbuoy_ref[0, part, col] = out[24:32]
        out_copies += [
            start_copy(gvel_ref.at[:, :, part, :], gvel_hbm.at[:, :, part, :], out_sems, 2 * half),
            start_copy(gbuoy_ref.at[:, part, :], gbuoy_hbm.at[:, part, :], out_sems, 2 * half + 1),
        ]
    b2_ref[...] = bias2
    mid = (
        dot_nt(e2h_ref[...], first_ref[0:256])
        + dot_nt(e2h_ref[...], first_ref[256:512])
        + dot_nt(e2l_ref[...], first_ref[0:256])
    )
    both1 = dot_nt(first_ref[512:608], e1h_ref[...])
    rest1 = dot_nt(first_ref[512:608], e1l_ref[...])
    win = both1[0:32] + both1[32:64] + rest1[0:32]
    bin_ = both1[64:65] + rest1[64:65]
    both2 = dot_nt(dl_ref[...], second_ref[0:256])
    rest2 = dot_nt(dl_ref[...], second_ref[256:512])
    wout = both2[0:32] + both2[32:64] + rest2[0:32]

    def fold_rows(value):
        return jnp.sum(value.reshape(value.shape[0] // 8, 8, value.shape[1]), axis=1)

    to_unit = gather((256, LANES), 8)
    mid = exact(fold_rows(same_row(mid)), to_unit)
    small = [fold_rows(same_row(win)), fold_rows(same_row(wout)), bin_, jnp.zeros((7, 256), f32)]
    small = exact(jnp.concatenate(small, axis=0), to_unit)
    b2 = lax.dot_general(
        jnp.ones((8, LANES), f32),
        fold_rows(b2_ref[...]),
        (((1,), (1,)), ((), ())),
        precision=lax.Precision.HIGHEST,
        preferred_element_type=f32,
    )
    units = jnp.concatenate([mid[8 * i : 8 * (i + 1), 0:32] for i in range(4)], axis=1)
    rows = [units[i : i + 1] for i in range(8)]
    rows.append(jnp.concatenate([small[i : i + 1, 0:32] for i in range(4)], axis=1))
    rows.append(
        jnp.concatenate([small[i : i + 1, 0:32] for i in range(4, 7)] + [b2[0:1]], axis=1)
    )
    rows.append(small[8:9])
    rows = jnp.concatenate(rows, axis=0)
    for peer in range(32):
        total_ref[11 * peer : 11 * (peer + 1), :] = rows
    for copy in out_copies:
        copy.wait()


def sum_rows(got_ref):
    return [
        jnp.sum(got_ref[pl.ds(i, got_ref.shape[0] // 11, stride=11), :], axis=0, keepdims=True)
        for i in range(11)
    ]


def sum_slab(got_ref, out_ref):
    total = jnp.concatenate(sum_rows(got_ref), axis=0)
    for peer in range(16):
        out_ref[11 * peer : 11 * (peer + 1), :] = total


def sum_column(scale, got_ref, win_ref, bin_ref, wmid_ref, bmid_ref, wout_ref):
    rows = [row * scale for row in sum_rows(got_ref)]
    units = jnp.concatenate(rows[:8], axis=0)
    wmid_ref[...] = jnp.concatenate([units[:, 32 * i : 32 * (i + 1)] for i in range(4)], axis=0)
    win_ref[...] = jnp.concatenate([rows[8][:, 32 * i : 32 * (i + 1)] for i in range(4)], axis=0)
    wout_ref[...] = jnp.concatenate([rows[9][:, 32 * i : 32 * (i + 1)] for i in range(3)], axis=0)
    bmid_ref[...] = rows[9][:, 96:128]
    bin_ref[...] = rows[10][:, 0:32]


def trade(rows, peers, axes):
    size = rows.shape[0] // peers * LANES
    got = lax.all_to_all(rows.reshape(peers, 1, size), axes, 0, 0)
    return got.reshape(rows.shape)


def shards(velocity, buoyancy, cell_mask, spacing, cotangent, w_in, b_in, w_mid, b_mid, w_out):
    levels, rows, width = buoyancy.shape
    depth = spacing.shape[0]
    span_y = rows * 64
    table = dft_table(256, 1024)
    table_y = table[:, (np.arange(256) % 64) * 4 + np.arange(256) // 64]
    x_table, y_table = jnp.asarray(two_parts(table)), jnp.asarray(two_parts(table_y))
    backs = jnp.asarray(np.concatenate([two_parts(table.T), two_parts(table_y.T)], axis=0))
    eigen = eigenvalue(width)
    lanes = np.arange(LANES)
    ey = eigen.reshape(4, 4, 64)[lanes % 16 // 4, lanes % 4].T.astype(np.float32)
    ey = np.concatenate([ey, np.zeros((192, LANES), np.float32)], axis=0)
    ex = eigen[np.arange(128)[:, None] + 128 * (lanes[None, :] // 16)].astype(np.float32)
    turns = twiddles(256, 1024)
    fixed = jnp.asarray(np.concatenate([turns, ey, ex], axis=0))
    spread_turns = jnp.asarray(
        np.concatenate([np.repeat(turns[:, i : i + 1], LANES, axis=1) for i in range(2, 8)], axis=0)
    )
    pair_turns_held = jnp.asarray(
        np.concatenate(
            [turns[:, 4 * pair + i + 2 * (lanes % 16 // 8)] for pair in range(2) for i in range(2)],
            axis=0,
        )
    )
    turns = jnp.asarray(turns)
    cells = rows * width // 8
    dma = pltpu.SemaphoreType.DMA
    type_of = jax.ShapeDtypeStruct
    table = pltpu.VMEM((1024, 256), bf16)
    back_tables = pltpu.VMEM((1024, 512), bf16)
    turn_held = pltpu.VMEM((640, LANES), f32)
    first_held = pltpu.VMEM((608, cells), bf16)
    second_held = pltpu.VMEM((512, cells), bf16)
    wide = pltpu.VMEM((256, cells), bf16)
    wide_held = pltpu.VMEM((288, 640), bf16)
    mark_type = type_of((8, LANES), f32)
    table_flops = 4 * 512 * 256 * 512
    msg_type = type_of((128 * 3, LANES), f32)
    msg, mark = call(
        forward_x,
        (msg_type, mark_type),
        (cotangent, x_table, turns),
        hbm=(0, 1, 2),
        scratch=(
            table,
            pltpu.VMEM((256, LANES), f32),
            pltpu.VMEM(cotangent.shape, f32),
            pltpu.VMEM((1024, LANES), f32),
            dma((3,)),
        ),
        flops=table_flops,
        name="forward_x",
    )
    msg = trade(msg, 128, PLANE)

    first, second, weights, turns, mark = call(
        closure_forward,
        (
            pltpu.HBM((608, cells), bf16),
            pltpu.HBM((512, cells), bf16),
            pltpu.HBM((288, 640), bf16),
            pltpu.HBM((640, LANES), f32),
            mark_type,
        ),
        (w_in.T, b_in[None], w_mid, b_mid[None], w_out, spacing[None])
        + (velocity, buoyancy, fixed, mark),
        hbm=range(9),
        hbm_out=range(4),
        scratch=(
            pltpu.VMEM((4, 32), f32),
            pltpu.VMEM((1, 32), f32),
            pltpu.VMEM((32, 32), f32),
            pltpu.VMEM((1, 32), f32),
            pltpu.VMEM((3, 32), f32),
            pltpu.VMEM((1, LEVELS), f32),
            pltpu.VMEM(velocity.shape, f32),
            pltpu.VMEM(buoyancy.shape, f32),
            turn_held,
            first_held,
            second_held,
            wide_held,
            dma((9,)),
            dma((6,)),
        ),
        flops=2 * 256 * 256 * cells * 4,
        name="closure_forward",
    )
    gathered, turns, backs, weights = call(
        forward_y,
        (type_of((4, 256, LANES), f32), turn_held, back_tables, wide_held),
        (msg, y_table, turns, backs, weights, mark),
        hbm=(1, 2, 3, 4),
        scratch=(table, dma((4,))),
        flops=table_flops,
        name="forward_y",
    )
    gathered = lax.all_to_all(gathered, "x", 0, 0)
    (msg,) = call(
        solve_back,
        (msg_type,),
        (gathered, turns, backs, pair_turns_held),
        flops=table_flops,
        name="solve_back",
    )
    msg = trade(msg, 128, PLANE)
    totals, grad_velocity, grad_buoyancy = call(
        closure_back,
        (
            type_of((32 * 11, LANES), f32),
            pltpu.HBM(cotangent.shape, f32),
            pltpu.HBM(buoyancy.shape, f32),
        ),
        (msg, spread_turns, second, backs, cotangent, cell_mask, first, weights),
        hbm_out=(1, 2),
        scratch=(
            pltpu.VMEM((1024, LANES), f32),
            wide,
            wide,
            wide,
            wide,
            pltpu.VMEM((64, cells), bf16),
            pltpu.VMEM((256, LANES), f32),
            pltpu.VMEM(cotangent.shape, f32),
            pltpu.VMEM(buoyancy.shape, f32),
            dma((4,)),
        ),
        flops=table_flops + 2 * 256 * 256 * cells * 10,
        name="closure_back",
    )
    totals = trade(totals, 32, SLAB)
    (totals,) = call(sum_slab, (type_of((16 * 11, LANES), f32),), (totals,), name="sum_slab")
    totals = trade(totals, 16, COLUMN)
    scale = 1.0 / math.sqrt(width * span_y * depth)
    grad_in, grad_b_in, grad_mid, grad_b_mid, grad_out = call(
        functools.partial(sum_column, scale),
        (
            type_of((4, 32), f32),
            type_of((1, 32), f32),
            type_of((32, 32), f32),
            type_of((1, 32), f32),
            type_of((3, 32), f32),
        ),
        (totals,),
        name="sum_column",
    )
    return (
        grad_velocity,
        grad_buoyancy,
        grad_in.T,
        grad_b_in[0],
        grad_mid,
        grad_b_mid[0],
        grad_out,
    )


def solution(mesh):
    fine = Mesh(
        mesh.devices.reshape([size for _, size in FINE]), tuple(name for name, _ in FINE)
    )
    field = P(None, NARROW, WIDE, None)
    cell = P(NARROW, WIDE, None)
    in_specs = (field, cell, cell, P(), field, P(), P(), P(), P(), P())
    out_specs = (field, cell, P(), P(), P(), P(), P())
    return jax.shard_map(shards, mesh=fine, in_specs=in_specs, out_specs=out_specs, check_vma=False)
```
